128 devices in a mesh: visit: 8 (over y, core), region: 16 (over x, z).
Axes of the slice: x: 4, y: 4, z: 4, core: 2. Of those that a mesh axis runs over, the one named last changes fastest.
Arguments:
- image: bfloat16 [32, 4096, 2048], P('visit', 'region'), may hold values from -8 to 8
- variance: bfloat16 [32, 4096, 2048], P('visit', 'region'), may hold values from 0.25 to 24
- psf_coef: float32 [32, 3], P('visit'), may hold values from 0.2 to 1
- correlations: int32 [32, 2], replicated, may hold values from 0 to 7, all different within a row; in each aligned block of 4 rows (0 to 3, 4 to 7, ...) at most 2 rows name the same one
- row_start: int32 [32, 2, 1024], replicated, may hold values from -514 to 4614, as said below
- row_frac: float32 [32, 2, 1024], replicated, may hold values from 0 to 1
- col_start: int32 [32, 2, 4096], replicated, may hold values from -2050 to 4132, as said below
- col_frac: float32 [32, 2, 4096], replicated, may hold values from 0 to 1
Outputs:
- coadd: float32 [8, 1024, 4096], P('visit', None, 'region')
- weight_map: float32 [8, 1024, 4096], P('visit', None, 'region')
The draws below stay inside these ranges and needn't reach their ends.
Inputs may be any that keep to these rules, and one draw needn't show every extreme that they name: `correlations`: each exposure names 2 different patches. Among the 4 exposures of one index of visit (aligned blocks of 4 rows) no patch is named more than 2 times, a bound that some block reaches. Along one correlation's patch rows, row_start never falls and rises by at most 2 from one row to the next. Along one correlation's patch columns, col_start never falls and rises by at most 2 from one column to the next.
All inputs are finite; a program needn't handle non-finite values.
Results may differ from the reference program's by a relative error of at most 0.0042.
Values may be sent and summed in bfloat16 or wider, within the bound.
No kernel may reach another device: no remote copies, remote signals or barrier semaphores. Data moves between devices by JAX's collectives and lax.ppermute only.
A program may use at most 192 MiB of HBM per device.

```python
import math
import jax
import jax.numpy as jnp
import numpy as np
from jax import lax

EXP_DEV = 4
COLS = 2048
PATCH_ROWS = 1024
RADIUS = 10
NBASIS = 3
OVL = 2
MOST = 2
EXPOSURES = 32
ROWS = 4096
PATCHES = 8
PATCH_COLS = 4096


def band_starts(key, out_count, extent):
    shift_key, stretch_key = jax.random.split(key)
    lowest = -(out_count // 2)
    highest = extent - out_count // 2
    offset = jax.random.randint(shift_key, (EXPOSURES, OVL, 1), lowest, highest + 1)
    stretch = jax.random.randint(stretch_key, (EXPOSURES, OVL, 1), -40, 41)
    offset = offset.at[0, 0, 0].set(lowest).at[EXPOSURES - 1, OVL - 1, 0].set(highest)
    stretch = stretch.at[EXPOSURES - 1, OVL - 1, 0].set(40)
    position = jnp.arange(out_count, dtype=jnp.int32)[None, None, :]
    return (offset + position + position * stretch // 4096 - 2).astype(jnp.int32)


def draw_row_start(key, part):
    key = jax.random.fold_in(key, 11)
    return band_starts(key, PATCH_ROWS, ROWS)


def draw_col_start(key, part):
    key = jax.random.fold_in(key, 23)
    return band_starts(key, PATCH_COLS, COLS)


def draw_variance(key, part):
    key = jax.random.fold_in(key, 37)
    level_key, slope_key, band_key, pixel_key = jax.random.split(key, 4)
    sky_level = jnp.exp(jax.random.uniform(level_key, (EXPOSURES, 1, 1), jnp.float32, jnp.log(1.2), jnp.log(2.8)))
    slope = jax.random.uniform(slope_key, (EXPOSURES, 1, 1), jnp.float32, -0.5, 2.0)
    profile = 1.0 + slope * jnp.arange(ROWS, dtype=jnp.float32)[None, :, None] / (ROWS - 1)
    band_len = max(ROWS // 32, 1)
    band_count = ROWS // band_len + 1
    band_at = jnp.arange(ROWS, dtype=jnp.int32) // band_len
    band_table = jnp.exp(jax.random.uniform(band_key, (EXPOSURES, band_count), jnp.float32, jnp.log(0.75), jnp.log(1.35)))
    pixel_scale = jnp.exp(jax.random.uniform(pixel_key, (EXPOSURES, ROWS, COLS), jnp.float32, jnp.log(0.6), jnp.log(1.8)))
    banded = band_table[:, band_at][:, :, None]
    return (sky_level * profile * banded * pixel_scale).astype(jnp.bfloat16)


def steps_of(stream_key, shape, shards, smallest, largest):
    factor_of, own = 1.0, jax.random.fold_in(stream_key, 6)
    for dim, parts in shards:
        draws = jnp.exp(jax.random.uniform(jax.random.fold_in(own, dim), (parts,), jnp.float32, smallest / len(shards), largest / len(shards)))
        factor_of = factor_of * jnp.repeat(draws, shape[dim] // parts).reshape([-1 if axis == dim else 1 for axis in range(len(shape))])
    return factor_of


def assign_block(rng, own, number, rows, amount, top, bound, skew):
    ranking = jax.random.permutation(rng, amount)
    packed, ordinary = shares(amount, rows * top, bound, skew, True), shares(amount, rows * top, bound, skew, False)
    places = jnp.arange(amount)

    def named(lengths, rotation):
        used = int((lengths > 0).sum())
        fixed = max(1, used // 4)
        moved = fixed + (places - fixed + rotation * (used - fixed)) % max(1, amount - fixed)
        return jnp.zeros((amount,), jnp.int32).at[ranking[jnp.where(places < fixed, places, moved)]].set(jnp.asarray(lengths, jnp.int32))

    lengths = jnp.where(number % 4 == 0, named(packed, number // 4), named(ordinary, number - number // 4 - 1))
    mixed = jax.random.permutation(jax.random.fold_in(own, 3), amount)
    source_of, taker = mixed[0:amount // 2 * 2:2], mixed[1:amount // 2 * 2:2]
    slack = jnp.minimum(lengths[source_of] - 1, bound - lengths[taker]) // 2
    slack = jnp.where((source_of == ranking[0]) | (taker == ranking[0]) | (lengths[taker] == 0), 0, jnp.maximum(slack, 0))
    moved = jax.random.randint(jax.random.fold_in(own, 4), (amount // 2,), 0, 1 << 20) % (slack + 1)
    lengths = lengths.at[source_of].add(-moved).at[taker].add(moved)
    items = jnp.searchsorted(jnp.cumsum(lengths), jnp.arange(rows * top), side="right").astype(jnp.int32)
    table = items.reshape(top, rows).T
    table = table[jax.random.permutation(jax.random.fold_in(own, 1), rows)]
    rotation = jax.random.randint(jax.random.fold_in(own, 2), (rows, 1), 0, top)
    return jnp.take_along_axis(table, (jnp.arange(top)[None, :] + rotation) % top, axis=1)


def shares(amount, total, reach, lean, full):
    portions = [(1 << 20) // math.isqrt(standing ** lean) + 1 for standing in range(1, amount + 1)]
    largest = reach if full else min(reach, max(-(-total // amount), total * portions[0] // sum(portions)))
    least = 1 if total - largest >= amount - 1 else 0
    holding, spare = [largest] + [least] * (amount - 1), total - largest - least * (amount - 1)
    while spare > 0:
        movable = [i for i in range(1, amount) if holding[i] < largest] or [i for i in range(1, amount) if holding[i] < reach]
        pool, remaining = sum([portions[i] for i in movable]), spare
        for i in movable:
            more = min(reach - holding[i], max(1, remaining * portions[i] // pool), spare)
            holding[i] = holding[i] + more
            spare = spare - more
    return np.array(holding)


def bell_draw(rng, dims, deviation, reach, pieces=(), held_as=jnp.bfloat16):
    loudness = steps_of(rng, dims, pieces, -0.22, 0.18) if pieces else 1.0
    values = jax.random.normal(rng, dims, jnp.float32) * deviation * loudness
    return jnp.minimum(jnp.maximum(values, -reach), reach).astype(held_as)


def setup_inputs(seed: int = 0) -> dict:
    keys = jax.random.split(jax.random.key(seed), 9)
    image = bell_draw(keys[0], (EXPOSURES, ROWS, COLS), 1.0, 8.0, ((0, 8), (1, 16)))
    variance = draw_variance(jax.random.fold_in(keys[8], 71), 0)
    psf_coef = jnp.clip(jnp.exp(math.log(1.0) - 1.609438 * jax.random.uniform(keys[2], (EXPOSURES, NBASIS), jnp.float32) ** steps_of(keys[2], (EXPOSURES, NBASIS), ((0, 8),), -0.2, 0.2)), 0.2, 1.0)
    correlations_keys = jax.random.split(jax.random.fold_in(keys[3], 1), EXPOSURES // EXP_DEV)
    correlations_turns = jax.random.permutation(jax.random.fold_in(keys[3], 3), EXPOSURES // EXP_DEV)
    correlations = jax.vmap(lambda own, number: assign_block(jax.random.fold_in(keys[3], 2), own, number, EXP_DEV, PATCHES, OVL, MOST, 2))(correlations_keys, correlations_turns).reshape((EXPOSURES, OVL))
    row_start = draw_row_start(jax.random.fold_in(keys[8], 71), 0)
    row_frac = jnp.clip(jax.random.uniform(keys[5], (EXPOSURES, OVL, PATCH_ROWS), jnp.float32, 0.0, 1.0), 0.0, 1.0)
    col_start = draw_col_start(jax.random.fold_in(keys[8], 71), 0)
    col_frac = jnp.clip(jax.random.uniform(keys[7], (EXPOSURES, OVL, PATCH_COLS), jnp.float32, 0.0, 1.0), 0.0, 1.0)
    return {"image": image, "variance": variance, "psf_coef": psf_coef, "correlations": correlations, "row_start": row_start, "row_frac": row_frac, "col_start": col_start, "col_frac": col_frac}


tap_count = 6
sigma_list = (1.0, 2.0, 4.0)
floor_share = 0.5


def psf_kernel(coefficient):
    offsets = jnp.arange(-RADIUS, RADIUS + 1).astype(coefficient.dtype)
    sigmas = jnp.array(sigma_list, dtype=coefficient.dtype)
    gaussians = jnp.exp(-(offsets[None, :] * offsets[None, :]) / (2.0 * sigmas[:, None] * sigmas[:, None]))
    kernel = jnp.sum(coefficient[:, :, None] * gaussians[None, :, :], axis=1)
    return kernel / jnp.sum(kernel, axis=1, keepdims=True)


def lanczos_taps(fraction):
    tap_index = jnp.arange(tap_count).astype(fraction.dtype)
    distance = 2.0 + fraction[..., None, :] - tap_index[:, None]
    kernel_val = jnp.sinc(distance) * jnp.sinc(distance / 3.0)
    kernel_val = kernel_val / jnp.sum(kernel_val, axis=-2, keepdims=True)
    return kernel_val.astype(jnp.bfloat16)


def coverage(start_at, tap_weights, extent):
    running = jnp.zeros(start_at.shape, jnp.float32)
    for tap_at in range(tap_count):
        position = start_at + tap_at
        inside = (position >= 0) & (position < extent)
        running = running + jnp.where(inside, tap_weights[..., tap_at, :].astype(jnp.float32), 0.0)
    return running


def blur(image_one, kernel):
    source = image_one.astype(kernel.dtype)
    padded = jnp.pad(source, ((RADIUS, RADIUS), (0, 0)))
    running = jnp.zeros(source.shape, kernel.dtype)
    for tap_at in range(2 * RADIUS + 1):
        running = running + kernel[tap_at] * padded[tap_at:tap_at + source.shape[0], :]
    widened = jnp.pad(running, ((0, 0), (RADIUS, RADIUS)))
    blurred = jnp.zeros(source.shape, kernel.dtype)
    for tap_at in range(2 * RADIUS + 1):
        blurred = blurred + kernel[tap_at] * widened[:, tap_at:tap_at + source.shape[1]]
    return blurred.astype(jnp.bfloat16)


def resample_ref(source, start_at, tap_weights, along_axis):
    extent = source.shape[along_axis]
    if along_axis == 1:
        running = jnp.zeros((source.shape[0], start_at.shape[0]), jnp.float32)
    else:
        running = jnp.zeros((start_at.shape[0], source.shape[1]), jnp.float32)
    for tap_at in range(tap_count):
        position = start_at + tap_at
        inside = (position >= 0) & (position < extent)
        picked = jnp.take(source, jnp.clip(position, 0, extent - 1), axis=along_axis).astype(jnp.float32)
        factor = jnp.where(inside, tap_weights[tap_at].astype(jnp.float32), 0.0)
        if along_axis == 1:
            running = running + picked * factor[None, :]
        else:
            running = running + picked * factor[:, None]
    return running


def reference(image, variance, psf_coef, correlations, row_start, row_frac, col_start, col_frac):
    kernels = psf_kernel(psf_coef)
    mean_variance = jnp.sum(variance.astype(jnp.float32), axis=(1, 2)) / (ROWS * COLS)
    weight = 1.0 / mean_variance
    mean_weight = jnp.mean(weight)
    row_taps = lanczos_taps(row_frac)
    col_taps = lanczos_taps(col_frac)
    owner_index = correlations.astype(jnp.int32)
    row_cover = coverage(row_start, row_taps, ROWS)
    col_cover = coverage(col_start, col_taps, COLS)

    def one_exposure(running_sums, exposure_data):
        summed, weight_sum = running_sums
        image_one, kernel, weight_one, row_starts, row_weights, col_starts, col_weights, owners, rows_cover, cols_cover = exposure_data
        matched = blur(image_one, kernel)
        for slot_at in range(OVL):
            warped_cols = resample_ref(matched, col_starts[slot_at], col_weights[slot_at], 1).astype(jnp.bfloat16)
            warped = resample_ref(warped_cols, row_starts[slot_at], row_weights[slot_at], 0)
            summed = summed.at[owners[slot_at]].add(weight_one * warped)
            scaled = weight_one * rows_cover[slot_at][:, None]
            weight_sum = weight_sum.at[owners[slot_at]].add(scaled * cols_cover[slot_at][None, :])
        return (summed, weight_sum), None

    empty_sum = jnp.zeros((PATCHES, PATCH_ROWS, PATCH_COLS), jnp.float32)
    (summed, weight_map), unused = lax.scan(one_exposure, (empty_sum, empty_sum), (image, kernels, weight, row_start, row_taps, col_start, col_taps, owner_index, row_cover, col_cover))
    coadd = summed / jnp.maximum(weight_map, floor_share * mean_weight)
    return coadd, weight_map
```

```python
import functools
import math

import jax
import jax.numpy as jnp
from jax import lax
from jax.experimental import pallas as pl
from jax.experimental.pallas import tpu as pltpu
from jax.sharding import PartitionSpec as P

RADIUS = 10
TAPS = 6
SIGMAS = (1.0, 2.0, 4.0)
FLOOR_SHARE = 0.5
BF16 = jnp.bfloat16
F32 = jnp.float32

ROW_BLOCK = 128
ROW_STEP = 224
ROW_SPAN = 256
COL_BLOCK = 128
COL_STEP = 256
COL_GROUP = 4
BLUR_BLOCK = 256
BLUR_STEP = 512
BLUR_BAND = (112, 400)
LANES = 128
CHUNKS = 2


def psf_kernel(coefficient):
    offsets = jnp.arange(-RADIUS, RADIUS + 1).astype(coefficient.dtype)
    sigmas = jnp.array(SIGMAS, dtype=coefficient.dtype)
    gaussians = jnp.exp(
        -(offsets[None, :] * offsets[None, :]) / (2.0 * sigmas[:, None] * sigmas[:, None])
    )
    kernel = jnp.sum(coefficient[:, :, None] * gaussians[None, :, :], axis=1)
    return kernel / jnp.sum(kernel, axis=1, keepdims=True)


def lanczos_taps(f):
    g = 1.0 - f
    third = math.pi / 3.0
    tiny = 1e-6
    a = jnp.sin(third * f)
    b = jnp.sin(third * g)
    c = a + b
    fg = f * g
    a_over_f = jnp.where(f < tiny, third, a / jnp.maximum(f, tiny))
    b_over_g = jnp.where(g < tiny, third, b / jnp.maximum(g, tiny))
    values = [
        b * fg / ((f + 2.0) * (f + 2.0)),
        -c * fg / ((f + 1.0) * (f + 1.0)),
        a_over_f * g,
        b_over_g * f,
        -c * fg / ((2.0 - f) * (2.0 - f)),
        a * fg / ((3.0 - f) * (3.0 - f)),
    ]
    total = functools.reduce(jnp.add, values)
    return [lax.reduce_precision(value / total, 8, 7) for value in values]


def coverage(starts, taps, extent):
    running = jnp.zeros(starts.shape, F32)
    for tap_at, tap in enumerate(taps):
        position = starts + tap_at
        inside = (position >= 0) & (position < extent)
        running = running + jnp.where(inside, tap, 0.0)
    return running


def band_tables(starts, taps):
    place = jnp.arange(8, dtype=jnp.int32)[:, None]
    diff = place - starts[..., None, :]
    at = diff & 7
    turned = jnp.zeros(diff.shape, F32)
    for tap_at, tap in enumerate(taps):
        turned = turned + jnp.where(at == tap_at, tap[..., None, :], 0.0)
    return turned, diff - at


def toeplitz(kernels, rows, cols, shift):
    diff = (
        lax.broadcasted_iota(jnp.int32, (rows, cols), 0)
        - lax.broadcasted_iota(jnp.int32, (rows, cols), 1)
        + shift
    )
    full = jnp.zeros(kernels.shape[:-1] + (rows, cols), F32)
    for tap_at in range(2 * RADIUS + 1):
        full = full + jnp.where(diff == tap_at, kernels[..., tap_at, None, None], 0.0)
    return full


def dot(a, b):
    return jnp.dot(a, b, preferred_element_type=F32)


def dot_t(a, b):
    return lax.dot_general(a, b, (((0,), (0,)), ((), ())), preferred_element_type=F32)


def two_parts(value):
    high = value.astype(BF16)
    return high, (value - high.astype(F32)).astype(BF16)


def halves_sum(value, axis):
    half = value.shape[axis] // 2
    return lax.slice_in_dim(value, 0, half, axis=axis) + lax.slice_in_dim(
        value, half, 2 * half, axis=axis
    )


def row_body(slots, low_ref, num_ref, x_ref, blur_ref, turned_ref, key_ref, out_ref, blur):
    extent = x_ref.shape[0]
    owner_rows = out_ref.shape[2]
    blocks = turned_ref.shape[0] // slots
    last = extent - ROW_STEP
    groups = ROW_SPAN // 8
    blur_high, blur_rest = two_parts(blur_ref[...])
    blur[pl.ds(0, ROW_STEP), :] = blur_high
    blur[pl.ds(ROW_STEP, ROW_STEP), :] = blur_rest

    def part(index, start, masked):
        first = pl.multiple_of(jnp.minimum(start, last), 16)
        key = key_ref[index] + (first - 16)
        turned = turned_ref[index]
        pieces = []
        for g in range(groups):
            value = jnp.where(key == -8 * g, turned, 0.0)
            if g < 2:
                value = jnp.where(first > 0, value, 0.0)
            if g >= groups - 2:
                value = jnp.where(first < last, value, 0.0)
            pieces.append(value)
        band = jnp.concatenate(pieces, axis=0).astype(BF16)
        both = halves_sum(dot(blur[...], band), 0)
        if masked:
            row = lax.broadcasted_iota(jnp.int32, both.shape, 0) + first
            both = jnp.where(row >= start, both, 0.0)
        parts = jnp.concatenate(two_parts(both), axis=1)
        return halves_sum(dot_t(parts, x_ref[pl.ds(first, ROW_STEP), :]), 0)

    def block(at, carry):
        sums = [
            part(slot * blocks + at, low_ref[slot * blocks + at], False) for slot in range(slots)
        ]
        for slot in range(slots):
            index = slot * blocks + at

            def more(i, total, index=index):
                return total + part(index, low_ref[index] + i * ROW_STEP, True)

            total = lax.fori_loop(1, num_ref[index], more, sums[slot]).astype(BF16)
            for owner in range(ROW_BLOCK // owner_rows):
                out_ref[at * (ROW_BLOCK // owner_rows) + owner, slot] = total[
                    owner * owner_rows : (owner + 1) * owner_rows
                ]
        return carry

    lax.fori_loop(0, blocks, block, 0)


def row_warp(x, low, num, blur, turned, key, slots, owners):
    width = x.shape[1]
    owner_rows = turned.shape[0] // slots * ROW_BLOCK // owners
    vmem = pl.BlockSpec(memory_space=pltpu.VMEM)
    smem = pl.BlockSpec(memory_space=pltpu.SMEM)
    return pl.pallas_call(
        functools.partial(row_body, slots),
        out_shape=jax.ShapeDtypeStruct((owners, slots, owner_rows, width), BF16),
        in_specs=[smem, smem, vmem, vmem, vmem, vmem],
        out_specs=vmem,
        scratch_shapes=[pltpu.VMEM((2 * ROW_STEP, ROW_SPAN), BF16)],
        compiler_params=pltpu.CompilerParams(vmem_limit_bytes=40 * 1024 * 1024),
        cost_estimate=pl.CostEstimate(
            flops=8_000_000_000, bytes_accessed=8 * 1024 * 1024, transcendentals=0
        ),
        name="row_warp",
    )(low, num, x, blur, turned, key)


def col_body(cols, slots, count_ref, list_ref, low_ref, num_ref, any_ref, weight_ref, z_ref,
             blur_ref, turned_ref, key_ref, out_ref, padded, blur, blurred):
    rows = z_ref.shape[2]
    width = z_ref.shape[3]
    sources = cols // width
    exposures = z_ref.shape[0] // sources
    patch = pl.program_id(0)
    begin, end = BLUR_BAND

    @pl.when(patch == 0)
    def _():
        pad = jnp.zeros((slots * rows, LANES), BF16)
        padded[:, 0:LANES] = pad
        padded[:, LANES + cols : 2 * LANES + cols] = pad
        for n in range(2):
            blur[n, 0:begin] = jnp.zeros((begin, BLUR_BLOCK), BF16)
            blur[n, end:BLUR_STEP] = jnp.zeros((BLUR_STEP - end, BLUR_BLOCK), BF16)
        for e in range(exposures):
            blur_high, blur_rest = two_parts(blur_ref[e])
            blur[0, begin:end] = blur_high
            blur[1, begin:end] = blur_rest
            for s in range(sources):
                padded[:, LANES + s * width : LANES + (s + 1) * width] = z_ref[
                    e * sources + s
                ].reshape(slots * rows, width)
            windows = jnp.concatenate(
                [
                    padded[:, b * BLUR_BLOCK : b * BLUR_BLOCK + BLUR_STEP]
                    for b in range(cols // BLUR_BLOCK)
                ],
                axis=0,
            )
            high, rest = two_parts(dot(windows, blur[0]) + dot(windows, blur[1]))
            for b in range(cols // BLUR_BLOCK):
                for j in range(slots):
                    at = (b * slots + j) * rows
                    span = slice(b * BLUR_BLOCK, (b + 1) * BLUR_BLOCK)
                    blurred[e * slots + j, 0:rows, span] = high[at : at + rows]
                    blurred[e * slots + j, rows : 2 * rows, span] = rest[at : at + rows]
            for j in range(slots):
                blurred[e * slots + j, :, cols : cols + COL_STEP] = jnp.zeros(
                    (2 * rows, COL_STEP), BF16
                )

    def part(slot, b, start):
        first = pl.multiple_of(start, LANES)
        key = key_ref[slot, b] + first
        turned = turned_ref[slot, b]
        band = jnp.concatenate(
            [jnp.where(key == -8 * g, turned, 0.0) for g in range(COL_STEP // 8)], axis=0
        ).astype(BF16)
        return halves_sum(dot(blurred[slot, :, pl.ds(first, COL_STEP)], band), 0)

    def group(c, carry):
        def add_slot(i, totals):
            slot = list_ref[patch, i]

            def work(totals):
                blocks = [c * COL_GROUP + h for h in range(COL_GROUP)]
                sums = [part(slot, b, low_ref[slot, b]) for b in blocks]
                for h, b in enumerate(blocks):

                    def more(n, total, b=b):
                        return total + part(slot, b, low_ref[slot, b] + n * COL_STEP)

                    sums[h] = lax.fori_loop(1, num_ref[slot, b], more, sums[h])
                return tuple(t + weight_ref[slot] * s for t, s in zip(totals, sums))

            return lax.cond(any_ref[slot, c] > 0, work, lambda t: t, totals)

        zero = jnp.zeros((rows, COL_BLOCK), F32)
        totals = lax.fori_loop(0, count_ref[patch], add_slot, (zero,) * COL_GROUP)
        per_owner = out_ref.shape[3] // COL_BLOCK
        for h, total in enumerate(totals):
            out_ref[
                0,
                c * (COL_GROUP // per_owner) + h // per_owner,
                :,
                (h % per_owner) * COL_BLOCK : (h % per_owner + 1) * COL_BLOCK,
            ] = total.astype(BF16)
        return carry

    lax.fori_loop(0, turned_ref.shape[1] // COL_GROUP, group, 0)


def col_warp(z, count, listed, low, num, some, weight, blur, turned, key, cols, patches, owners):
    slots, rows = z.shape[1:3]
    slot_total, blocks = turned.shape[:2]
    own_cols = blocks * COL_BLOCK // owners
    vmem = pl.BlockSpec(memory_space=pltpu.VMEM)
    smem = pl.BlockSpec(memory_space=pltpu.SMEM)
    return pl.pallas_call(
        functools.partial(col_body, cols, slots),
        out_shape=jax.ShapeDtypeStruct((patches, owners, rows, own_cols), BF16),
        grid=(patches,),
        in_specs=[smem] * 6 + [vmem] * 4,
        out_specs=pl.BlockSpec((1, owners, rows, own_cols), lambda k: (k, 0, 0, 0)),
        scratch_shapes=[
            pltpu.VMEM((slots * rows, cols + 2 * LANES), BF16),
            pltpu.VMEM((2, BLUR_STEP, BLUR_BLOCK), BF16),
            pltpu.VMEM((slot_total, 2 * rows, cols + COL_STEP), BF16),
        ],
        compiler_params=pltpu.CompilerParams(
            dimension_semantics=("arbitrary",), vmem_limit_bytes=40 * 1024 * 1024
        ),
        cost_estimate=pl.CostEstimate(
            flops=8_000_000_000, bytes_accessed=8 * 1024 * 1024, transcendentals=0
        ),
        name="col_warp",
    )(count, listed, low, num, some, weight, z, blur, turned, key)


def local(image, variance, psf_coef, correlations, row_start, row_frac, col_start, col_frac):
    exp_dev, height, width = image.shape
    exposures, slots = correlations.shape
    patch_rows = row_start.shape[2]
    patch_cols = col_start.shape[2]
    visits = lax.axis_size("visit")
    regions = lax.axis_size("region")
    extent = height * regions
    parts = regions // exp_dev
    part_cols = width // parts
    own_cols = patch_cols // regions
    visit_at = lax.axis_index("visit")
    region_at = lax.axis_index("region")
    first_exp = visit_at * exp_dev
    own_exp = region_at // parts

    sent = image.reshape(exp_dev, height, parts, part_cols).transpose(0, 2, 1, 3)
    sent = sent.reshape(regions, height, part_cols)
    columns = lax.all_to_all(sent, "region", split_axis=0, concat_axis=0, tiled=True)
    columns = columns.reshape(extent, part_cols)

    local_sums = jnp.sum(variance.astype(F32), axis=(1, 2))
    tile = jnp.zeros((8, LANES), F32).at[0, :exp_dev].set(local_sums)
    gathered = lax.all_gather(tile, ("visit", "region"), axis=0, tiled=False)
    gathered = gathered[:, 0, :exp_dev].reshape(visits, regions, exp_dev)
    totals = jnp.sum(gathered, axis=1).reshape(exposures)
    weight = 1.0 / (totals / (extent * width))
    mean_weight = jnp.mean(weight)
    own_weight = lax.dynamic_slice_in_dim(weight, first_exp, exp_dev, 0)

    kernels = psf_kernel(psf_coef)

    starts = lax.dynamic_index_in_dim(row_start, first_exp + own_exp, 0, keepdims=False)
    fracs = lax.dynamic_index_in_dim(row_frac, first_exp + own_exp, 0, keepdims=False)
    blocks = patch_rows // ROW_BLOCK // CHUNKS
    chunked = (slots, CHUNKS, blocks, ROW_BLOCK)
    starts = starts.reshape(chunked).transpose(1, 0, 2, 3).reshape(CHUNKS, slots * blocks, ROW_BLOCK)
    fracs = fracs.reshape(chunked).transpose(1, 0, 2, 3).reshape(CHUNKS, slots * blocks, ROW_BLOCK)
    row_turned, row_key = band_tables(starts, lanczos_taps(fracs))
    row_low = jnp.clip(starts[..., 0] - RADIUS, 0, extent - ROW_STEP) // 16 * 16
    row_end = jnp.minimum(starts[..., -1] + TAPS + RADIUS, extent)
    row_num = jnp.maximum(row_end - row_low + ROW_STEP - 1, 0) // ROW_STEP
    row_blur = toeplitz(
        lax.dynamic_index_in_dim(kernels, own_exp, 0, keepdims=False),
        ROW_STEP, ROW_SPAN, 16 + RADIUS,
    )

    slot_total = exp_dev * slots
    col_blocks = patch_cols // COL_BLOCK
    own_starts = lax.dynamic_slice_in_dim(col_start, first_exp, exp_dev, 0)
    own_fracs = lax.dynamic_slice_in_dim(col_frac, first_exp, exp_dev, 0)
    own_starts = own_starts.reshape(slot_total, col_blocks, COL_BLOCK)
    own_fracs = own_fracs.reshape(slot_total, col_blocks, COL_BLOCK)
    col_turned, col_key = band_tables(own_starts, lanczos_taps(own_fracs))
    col_low = jnp.clip(own_starts[:, :, 0], 0, width) // LANES * LANES
    col_end = jnp.minimum(own_starts[:, :, -1] + TAPS, width)
    col_num = jnp.maximum(col_end - col_low + COL_STEP - 1, 0) // COL_STEP
    col_some = jnp.sum(col_num.reshape(slot_total, col_blocks // COL_GROUP, COL_GROUP), axis=2)
    col_blur = toeplitz(
        kernels, BLUR_BAND[1] - BLUR_BAND[0], BLUR_BLOCK, BLUR_BAND[0] - LANES + RADIUS
    )
    owners = lax.dynamic_slice_in_dim(correlations, first_exp, exp_dev, 0).reshape(slot_total)
    named = owners[None, :] == jnp.arange(visits, dtype=jnp.int32)[:, None]
    count = jnp.sum(named.astype(jnp.int32), axis=1)
    rank = jnp.cumsum(named.astype(jnp.int32), axis=1) - 1
    slot_ids = jnp.arange(slot_total, dtype=jnp.int32)
    listed = jnp.stack(
        [
            jnp.sum(jnp.where(named & (rank == i), slot_ids[None, :], 0), axis=1)
            for i in range(slot_total)
        ],
        axis=1,
    ).astype(jnp.int32)
    slot_weight = jnp.repeat(own_weight, slots)

    pieces = []
    for h in range(CHUNKS):
        row_warped = row_warp(
            columns, row_low[h], row_num[h], row_blur, row_turned[h], row_key[h], slots, regions
        )
        rows = lax.all_to_all(row_warped, "region", split_axis=0, concat_axis=0, tiled=True)
        partial = col_warp(
            rows, count, listed, col_low, col_num, col_some, slot_weight, col_blur,
            col_turned, col_key, width, visits, regions,
        )
        summed = lax.psum_scatter(partial, "visit", scatter_dimension=0, tiled=True)
        summed = lax.all_to_all(summed[0], "region", split_axis=0, concat_axis=0, tiled=True)
        pieces.append(summed.reshape(1, patch_rows // CHUNKS, own_cols))
    summed = jnp.concatenate(pieces, axis=1).astype(F32)

    total_slots = exposures * slots
    row_cover = coverage(
        row_start.reshape(total_slots, patch_rows),
        lanczos_taps(row_frac.reshape(total_slots, patch_rows)),
        extent,
    )
    at = region_at * own_cols
    col_cover = coverage(
        lax.dynamic_slice_in_dim(col_start, at, own_cols, 2).reshape(total_slots, own_cols),
        lanczos_taps(
            lax.dynamic_slice_in_dim(col_frac, at, own_cols, 2).reshape(total_slots, own_cols)
        ),
        width,
    )
    scale = jnp.where(
        correlations.reshape(total_slots) == visit_at, jnp.repeat(weight, slots), 0.0
    )
    weight_map = lax.dot_general(
        row_cover,
        col_cover * scale[:, None],
        (((0,), (0,)), ((), ())),
        precision=lax.Precision.HIGHEST,
        preferred_element_type=F32,
    ).reshape(1, patch_rows, own_cols)
    coadd = summed / jnp.maximum(weight_map, FLOOR_SHARE * mean_weight)
    return coadd, weight_map


def solution(mesh):
    placed = (
        P("visit", "region", None),
        P("visit", "region", None),
        P("visit", None),
        P(),
        P(),
        P(),
        P(),
        P(),
    )
    return jax.shard_map(
        local,
        mesh=mesh,
        in_specs=placed,
        out_specs=(P("visit", None, "region"), P("visit", None, "region")),
        check_vma=False,
    )
```

```python
import functools
import math

import jax
import jax.numpy as jnp
from jax import lax
from jax.experimental import pallas as pl
from jax.experimental.pallas import tpu as pltpu
from jax.sharding import PartitionSpec as P

RADIUS = 10
TAPS = 6
SIGMAS = (1.0, 2.0, 4.0)
FLOOR_SHARE = 0.5
BF16 = jnp.bfloat16
F32 = jnp.float32

ROW_BLOCK = 128
ROW_STEP = 256
ROW_SPAN = 288
COL_BLOCK = 128
COL_STEP = 384
COL_GROUP = 4
BLUR_BLOCK = 256
BLUR_STEP = 512
BLUR_BAND = (112, 400)
LANES = 128
GROUPS = 1
LIMIT = 28 * 1024 * 1024


def psf_kernel(coefficient):
    offsets = jnp.arange(-RADIUS, RADIUS + 1).astype(coefficient.dtype)
    sigmas = jnp.array(SIGMAS, dtype=coefficient.dtype)
    gaussians = jnp.exp(
        -(offsets[None, :] * offsets[None, :]) / (2.0 * sigmas[:, None] * sigmas[:, None])
    )
    kernel = jnp.sum(coefficient[:, :, None] * gaussians[None, :, :], axis=1)
    return kernel / jnp.sum(kernel, axis=1, keepdims=True)


def lanczos_taps(f):
    g = 1.0 - f
    third = math.pi / 3.0
    tiny = 1e-6
    a = jnp.sin(third * f)
    b = jnp.sin(third * g)
    c = a + b
    fg = f * g
    a_over_f = jnp.where(f < tiny, third, a / jnp.maximum(f, tiny))
    b_over_g = jnp.where(g < tiny, third, b / jnp.maximum(g, tiny))
    values = [
        b * fg / ((f + 2.0) * (f + 2.0)),
        -c * fg / ((f + 1.0) * (f + 1.0)),
        a_over_f * g,
        b_over_g * f,
        -c * fg / ((2.0 - f) * (2.0 - f)),
        a * fg / ((3.0 - f) * (3.0 - f)),
    ]
    total = functools.reduce(jnp.add, values)
    return [lax.reduce_precision(value / total, 8, 7) for value in values]


def coverage(starts, taps, extent):
    running = jnp.zeros(starts.shape, F32)
    for tap_at, tap in enumerate(taps):
        position = starts + tap_at
        inside = (position >= 0) & (position < extent)
        running = running + jnp.where(inside, tap, 0.0)
    return running


def band_tables(starts, taps):
    place = jnp.arange(8, dtype=jnp.int32)[:, None]
    diff = place - starts[..., None, :]
    at = diff & 7
    turned = jnp.zeros(diff.shape, F32)
    for tap_at, tap in enumerate(taps):
        turned = turned + jnp.where(at == tap_at, tap[..., None, :], 0.0)
    return turned, diff - at


def toeplitz(kernel_ref, at, rows, cols, shift):
    diff = (
        lax.broadcasted_iota(jnp.int32, (rows, cols), 0)
        - lax.broadcasted_iota(jnp.int32, (rows, cols), 1)
    )
    full = jnp.zeros((rows, cols), F32)
    for tap_at in range(2 * RADIUS + 1):
        full = jnp.where(diff == tap_at - shift, kernel_ref[at, tap_at], full)
    return full


def dot(a, b):
    return jnp.dot(a, b, preferred_element_type=F32)


def two_parts(value):
    high = value.astype(BF16)
    return high, (value - high.astype(F32)).astype(BF16)


def halves_sum(value):
    half = value.shape[0] // 2
    return value[:half] + value[half:]


def band_of(turned, key, first, groups):
    moved = key + first
    return [jnp.where(moved == -8 * g, turned, 0.0) for g in range(groups)]


def row_matrix(blur_ref, turned, key, start, extent, masked):
    last = extent - ROW_STEP
    first = jnp.minimum(start, last)
    groups = ROW_SPAN // 8
    pieces = band_of(turned, key, first - 16, groups)
    for g in range(2):
        pieces[g] = jnp.where(first > 0, pieces[g], 0.0)
        pieces[groups - 1 - g] = jnp.where(first < last, pieces[groups - 1 - g], 0.0)
    band = jnp.concatenate(pieces, axis=0).astype(BF16)
    both = halves_sum(dot(blur_ref[...], band))
    if masked:
        row = lax.broadcasted_iota(jnp.int32, both.shape, 0) + first
        both = jnp.where(row >= start, both, 0.0)
    return jnp.concatenate(two_parts(both.T), axis=0)


def prepare_body(extent, own_ref, kernel_ref, low_ref, turned_ref, key_ref, rows_ref, blur_ref,
                 cols_ref, blur):
    step = pl.program_id(0)
    blocks = turned_ref.shape[1]
    high, rest = two_parts(
        toeplitz(kernel_ref, own_ref[step], ROW_STEP, ROW_SPAN, 16 + RADIUS)
    )
    blur[0:ROW_STEP] = high
    blur[ROW_STEP : 2 * ROW_STEP] = rest
    blur_ref[0] = blur[...]

    def block(at, carry):
        rows_ref[0, at] = row_matrix(
            blur, turned_ref[0, at], key_ref[0, at], low_ref[step, at], extent, False
        )
        return carry

    lax.fori_loop(0, blocks, block, 0)
    begin, end = BLUR_BAND
    for e in range(cols_ref.shape[0]):
        high, rest = two_parts(
            toeplitz(
                kernel_ref,
                step * cols_ref.shape[0] + e,
                end - begin,
                BLUR_BLOCK,
                begin - LANES + RADIUS,
            )
        )
        for n, part in enumerate((high, rest)):
            cols_ref[e, n, 0:begin] = jnp.zeros((begin, BLUR_BLOCK), BF16)
            cols_ref[e, n, begin:end] = part
            cols_ref[e, n, end:BLUR_STEP] = jnp.zeros((BLUR_STEP - end, BLUR_BLOCK), BF16)


def prepare(own, kernels, low, turned, key, extent):
    exposures = kernels.shape[0]
    blocks = turned.shape[1]
    smem = pl.BlockSpec(memory_space=pltpu.SMEM)
    table = pl.BlockSpec((1, blocks, 8, ROW_BLOCK), lambda g: (g, 0, 0, 0))
    return pl.pallas_call(
        functools.partial(prepare_body, extent),
        out_shape=(
            jax.ShapeDtypeStruct((GROUPS, blocks, 2 * ROW_BLOCK, ROW_STEP), BF16),
            jax.ShapeDtypeStruct((GROUPS, 2 * ROW_STEP, ROW_SPAN), BF16),
            jax.ShapeDtypeStruct((exposures, 2, BLUR_STEP, BLUR_BLOCK), BF16),
        ),
        grid=(GROUPS,),
        in_specs=[smem, smem, smem, table, table],
        out_specs=(
            pl.BlockSpec((1, blocks, 2 * ROW_BLOCK, ROW_STEP), lambda g: (g, 0, 0, 0)),
            pl.BlockSpec((1, 2 * ROW_STEP, ROW_SPAN), lambda g: (g, 0, 0)),
            pl.BlockSpec((exposures // GROUPS, 2, BLUR_STEP, BLUR_BLOCK), lambda g: (g, 0, 0, 0)),
        ),
        scratch_shapes=[pltpu.VMEM((2 * ROW_STEP, ROW_SPAN), BF16)],
        compiler_params=pltpu.CompilerParams(
            dimension_semantics=("arbitrary",), vmem_limit_bytes=LIMIT
        ),
        cost_estimate=pl.CostEstimate(
            flops=4_000_000_000, bytes_accessed=8 * 1024 * 1024, transcendentals=0
        ),
        name="prepare",
    )(own, kernels, low, turned, key)


def row_body(slots, low_ref, num_ref, x_ref, rows_ref, blur_ref, turned_ref, key_ref, out_ref):
    extent = x_ref.shape[0]
    owner_rows = out_ref.shape[2]
    blocks = turned_ref.shape[1] // slots

    def times(matrix, start):
        first = pl.multiple_of(jnp.minimum(start, extent - ROW_STEP), 16)
        return halves_sum(dot(matrix, x_ref[pl.ds(first, ROW_STEP), :]))

    def block(at, carry):
        indices = [slot * blocks + at for slot in range(slots)]
        sums = [times(rows_ref[0, index], low_ref[index]) for index in indices]
        for slot, index in enumerate(indices):

            def more(i, total, index=index):
                start = low_ref[index] + i * ROW_STEP
                matrix = row_matrix(
                    blur_ref.at[0], turned_ref[0, index], key_ref[0, index], start, extent, True
                )
                return total + times(matrix, start)

            total = lax.fori_loop(1, num_ref[index], more, sums[slot]).astype(BF16)
            for owner in range(ROW_BLOCK // owner_rows):
                out_ref[at * (ROW_BLOCK // owner_rows) + owner, slot] = total[
                    owner * owner_rows : (owner + 1) * owner_rows
                ]
        return carry

    lax.fori_loop(0, blocks, block, 0)


def row_warp(g, x, low, num, matrices, blur, turned, key, slots, owners):
    width = x.shape[1]
    blocks = turned.shape[1]
    owner_rows = blocks // slots * ROW_BLOCK // owners
    vmem = pl.BlockSpec(memory_space=pltpu.VMEM)
    smem = pl.BlockSpec(memory_space=pltpu.SMEM)

    def own(array):
        shape = (1,) + array.shape[1:]
        return pl.BlockSpec(shape, lambda i: (g,) + (0,) * (len(shape) - 1))

    return pl.pallas_call(
        functools.partial(row_body, slots),
        out_shape=jax.ShapeDtypeStruct((owners, slots, owner_rows, width), BF16),
        grid=(1,),
        in_specs=[smem, smem, vmem, own(matrices), own(blur), own(turned), own(key)],
        out_specs=vmem,
        compiler_params=pltpu.CompilerParams(
            dimension_semantics=("arbitrary",), vmem_limit_bytes=LIMIT
        ),
        cost_estimate=pl.CostEstimate(
            flops=2_000_000_000, bytes_accessed=8 * 1024 * 1024, transcendentals=0
        ),
        name="row_warp",
    )(low, num, x, matrices, blur, turned, key)


def col_body(g, cols, slots, has_prior, count_ref, list_ref, low_ref, most_ref, from_ref, to_ref,
             weight_ref, z_ref, blur_ref, turned_ref, key_ref, *refs):
    if has_prior:
        prior_ref, out_ref, padded, blurred, held = refs
    else:
        out_ref, padded, blurred, held = refs
    rows = z_ref.shape[2]
    width = z_ref.shape[3]
    sources = cols // width
    exposures = z_ref.shape[0] // sources
    base = g * exposures * slots
    patch = pl.program_id(0)

    @pl.when(patch == 0)
    def _():
        pad = jnp.zeros((slots * rows, LANES), BF16)
        padded[:, 0:LANES] = pad
        padded[:, LANES + cols : 2 * LANES + cols] = pad
        for e in range(exposures):
            for s in range(sources):
                padded[:, LANES + s * width : LANES + (s + 1) * width] = z_ref[
                    e * sources + s
                ].reshape(slots * rows, width)
            windows = jnp.concatenate(
                [
                    padded[:, b * BLUR_BLOCK : b * BLUR_BLOCK + BLUR_STEP]
                    for b in range(cols // BLUR_BLOCK)
                ],
                axis=0,
            )
            high, rest = two_parts(dot(windows, blur_ref[e, 0]) + dot(windows, blur_ref[e, 1]))
            for b in range(cols // BLUR_BLOCK):
                for j in range(slots):
                    at = (b * slots + j) * rows
                    span = slice(b * BLUR_BLOCK, (b + 1) * BLUR_BLOCK)
                    blurred[e * slots + j, 0:rows, span] = high[at : at + rows]
                    blurred[e * slots + j, rows : 2 * rows, span] = rest[at : at + rows]
            for j in range(slots):
                blurred[e * slots + j, :, cols : cols + COL_STEP] = jnp.zeros(
                    (2 * rows, COL_STEP), BF16
                )

    held[...] = prior_ref[0] if has_prior else jnp.zeros(held.shape, F32)

    def part(slot, b, n):
        first = pl.multiple_of(
            jnp.minimum(low_ref[base + slot, b] + n * COL_STEP, cols), LANES
        )
        band = band_of(turned_ref[slot, b], key_ref[slot, b], first, COL_STEP // 8)
        band = jnp.concatenate(band, axis=0).astype(BF16)
        return halves_sum(dot(blurred[slot, :, pl.ds(first, COL_STEP)], band))

    per_owner = held.shape[2] // COL_BLOCK

    def add_slot(i, carry):
        slot = list_ref[patch, i]
        weight = weight_ref[base + slot]

        def add_group(c, carry):
            def add_parts(n):
                for h in range(COL_GROUP):
                    owner = c * (COL_GROUP // per_owner) + h // per_owner
                    span = slice((h % per_owner) * COL_BLOCK, (h % per_owner + 1) * COL_BLOCK)
                    held[owner, :, span] += weight * part(slot, c * COL_GROUP + h, n)

            add_parts(0)

            def more(n, carry):
                add_parts(n)
                return carry

            lax.fori_loop(1, most_ref[base + slot, c], more, 0)
            return carry

        return lax.fori_loop(from_ref[base + slot], to_ref[base + slot], add_group, carry)

    lax.fori_loop(0, count_ref[patch], add_slot, 0)
    out_ref[0] = held[...].astype(out_ref.dtype)


def col_warp(g, z, count, listed, low, most, begin, end, weight, blur, turned, key, cols, patches,
             prior, out_type):
    owners, slots, rows = z.shape[:3]
    exposures = z.shape[0] * z.shape[3] // cols
    group_slots = exposures * slots
    blocks = turned.shape[1]
    own_cols = blocks * COL_BLOCK // owners
    vmem = pl.BlockSpec(memory_space=pltpu.VMEM)
    smem = pl.BlockSpec(memory_space=pltpu.SMEM)
    table = pl.BlockSpec((group_slots, blocks, 8, COL_BLOCK), lambda k: (g, 0, 0, 0))
    block = pl.BlockSpec((1, owners, rows, own_cols), lambda k: (k, 0, 0, 0))
    return pl.pallas_call(
        functools.partial(col_body, g, cols, slots, prior is not None),
        out_shape=jax.ShapeDtypeStruct((patches, owners, rows, own_cols), out_type),
        grid=(patches,),
        in_specs=[smem] * 7
        + [
            vmem,
            pl.BlockSpec((exposures, 2, BLUR_STEP, BLUR_BLOCK), lambda k: (g, 0, 0, 0)),
            table,
            table,
        ]
        + ([] if prior is None else [block]),
        out_specs=block,
        scratch_shapes=[
            pltpu.VMEM((slots * rows, cols + 2 * LANES), BF16),
            pltpu.VMEM((group_slots, 2 * rows, cols + COL_STEP), BF16),
            pltpu.VMEM((owners, rows, own_cols), F32),
        ],
        compiler_params=pltpu.CompilerParams(
            dimension_semantics=("arbitrary",), vmem_limit_bytes=LIMIT
        ),
        cost_estimate=pl.CostEstimate(
            flops=4_000_000_000, bytes_accessed=16 * 1024 * 1024, transcendentals=0
        ),
        name="col_warp",
    )(
        count, listed, low, most, begin, end, weight, z, blur, turned, key,
        *(() if prior is None else (prior,)),
    )


def split_body(parts, image_ref, out_ref, sems):
    exposures, _, width = image_ref.shape
    part = width // parts
    copies = []
    for e in range(exposures):
        for s in range(parts):
            at = e * parts + s
            copies.append(
                pltpu.make_async_copy(
                    image_ref.at[e, :, pl.ds(s * part, part)], out_ref.at[at], sems.at[at]
                )
            )
    for copy in copies:
        copy.start()
    for copy in copies:
        copy.wait()


def split_columns(image, parts):
    exposures, height, width = image.shape
    total = exposures * parts
    return pl.pallas_call(
        functools.partial(split_body, parts),
        out_shape=jax.ShapeDtypeStruct((total, height, width // parts), image.dtype),
        in_specs=[pl.BlockSpec(memory_space=pl.ANY)],
        out_specs=pl.BlockSpec(memory_space=pl.ANY),
        scratch_shapes=[pltpu.SemaphoreType.DMA((total,))],
        name="split_columns",
    )(image)


def butterfly_sum(x, axis):
    size = lax.axis_size(axis)
    step = 1
    while step < size:
        x = x + lax.ppermute(x, axis, [(i, i ^ step) for i in range(size)])
        step *= 2
    return x


def local(image, variance, psf_coef, correlations, row_start, row_frac, col_start, col_frac):
    exp_dev, height, width = image.shape
    exposures, slots = correlations.shape
    patch_rows = row_start.shape[2]
    patch_cols = col_start.shape[2]
    visits = lax.axis_size("visit")
    regions = lax.axis_size("region")
    extent = height * regions
    group_exp = exp_dev // GROUPS
    parts = regions // group_exp
    part_cols = width // parts
    own_cols = patch_cols // regions
    visit_at = lax.axis_index("visit")
    region_at = lax.axis_index("region")
    first_exp = visit_at * exp_dev

    def exchange(x, axis):
        return lax.all_to_all(x, axis, split_axis=0, concat_axis=0, tiled=True)

    columns = []
    for g in range(GROUPS):
        sent = split_columns(image[g * group_exp : (g + 1) * group_exp], parts)
        columns.append(exchange(sent, "region").reshape(extent, part_cols))

    local_sums = jnp.sum(variance.astype(F32), axis=(1, 2))
    tile = jnp.zeros((8, LANES), F32).at[0, :exp_dev].set(local_sums)
    tile = butterfly_sum(tile, "region")
    slot_weight = jnp.repeat(1.0 / (tile[0, :exp_dev] / (extent * width)), slots)

    kernels = psf_kernel(psf_coef)

    own_exp = jnp.arange(GROUPS, dtype=jnp.int32) * group_exp + region_at // parts
    starts = jnp.stack(
        [
            lax.dynamic_index_in_dim(row_start, first_exp + own_exp[g], 0, keepdims=False)
            for g in range(GROUPS)
        ]
    )
    fracs = jnp.stack(
        [
            lax.dynamic_index_in_dim(row_frac, first_exp + own_exp[g], 0, keepdims=False)
            for g in range(GROUPS)
        ]
    )
    blocks = slots * patch_rows // ROW_BLOCK
    starts = starts.reshape(GROUPS, blocks, ROW_BLOCK)
    fracs = fracs.reshape(GROUPS, blocks, ROW_BLOCK)
    row_turned, row_key = band_tables(starts, lanczos_taps(fracs))
    row_low = jnp.clip(starts[..., 0] - RADIUS, 0, extent - ROW_STEP) // 16 * 16
    row_end = jnp.minimum(starts[..., -1] + TAPS + RADIUS, extent)
    row_num = jnp.maximum(row_end - row_low + ROW_STEP - 1, 0) // ROW_STEP
    row_matrices, row_blur, col_blur = prepare(
        own_exp, kernels, row_low, row_turned, row_key, extent
    )

    slot_total = exp_dev * slots
    group_slots = group_exp * slots
    col_blocks = patch_cols // COL_BLOCK
    own_starts = lax.dynamic_slice_in_dim(col_start, first_exp, exp_dev, 0)
    own_fracs = lax.dynamic_slice_in_dim(col_frac, first_exp, exp_dev, 0)
    own_starts = own_starts.reshape(slot_total, col_blocks, COL_BLOCK)
    own_fracs = own_fracs.reshape(slot_total, col_blocks, COL_BLOCK)
    col_turned, col_key = band_tables(own_starts, lanczos_taps(own_fracs))
    col_low = jnp.clip(own_starts[:, :, 0], 0, width) // LANES * LANES
    col_end = jnp.minimum(own_starts[:, :, -1] + TAPS, width)
    col_num = jnp.maximum(col_end - col_low + COL_STEP - 1, 0) // COL_STEP
    col_most = jnp.max(col_num.reshape(slot_total, col_blocks // COL_GROUP, COL_GROUP), axis=2)
    group_at = jnp.arange(col_blocks // COL_GROUP, dtype=jnp.int32)
    col_from = jnp.min(jnp.where(col_most > 0, group_at, col_blocks // COL_GROUP), axis=1)
    col_to = jnp.max(jnp.where(col_most > 0, group_at + 1, 0), axis=1)
    owners = lax.dynamic_slice_in_dim(correlations, first_exp, exp_dev, 0)
    owners = owners.reshape(GROUPS, group_slots)
    named = owners[:, None, :] == jnp.arange(visits, dtype=jnp.int32)[:, None]
    named = named.astype(jnp.int32)
    count = jnp.sum(named, axis=2)
    slot_ids = jnp.arange(group_slots, dtype=jnp.int32)
    rank = jnp.sum(
        jnp.where(slot_ids[:, None] < slot_ids, named[..., :, None], 0), axis=2
    )
    listed = jnp.sum(
        jnp.where(
            (named[..., None, :] > 0) & (rank[..., None, :] == slot_ids[:, None]), slot_ids, 0
        ),
        axis=3,
    )

    rows = []
    for g in range(GROUPS):
        warped = row_warp(
            g, columns[g], row_low[g], row_num[g], row_matrices, row_blur, row_turned, row_key,
            slots, regions,
        )
        if g == GROUPS - 1:
            tile, warped = lax.optimization_barrier((tile, warped))
        rows.append(exchange(warped, "region"))
    tiles = jnp.zeros((visits, 8, LANES), F32)
    tiles = lax.dynamic_update_slice(tiles, tile[None], (visit_at, 0, 0))[:, 0]
    tiles = butterfly_sum(tiles, "visit")
    weight = 1.0 / (tiles[:, :exp_dev].reshape(exposures) / (extent * width))
    mean_weight = jnp.mean(weight)
    partial = None
    for g in range(GROUPS):
        partial = col_warp(
            g, rows[g], count[g], listed[g], col_low, col_most, col_from, col_to, slot_weight,
            col_blur, col_turned, col_key, width, visits, partial,
            BF16 if g == GROUPS - 1 else F32,
        )
    summed = lax.psum_scatter(partial, "visit", scatter_dimension=0, tiled=True)
    summed = exchange(summed[0], "region").reshape(1, patch_rows, own_cols).astype(F32)

    total_slots = exposures * slots
    row_cover = coverage(
        row_start.reshape(total_slots, patch_rows),
        lanczos_taps(row_frac.reshape(total_slots, patch_rows)),
        extent,
    )
    at = region_at * own_cols
    col_cover = coverage(
        lax.dynamic_slice_in_dim(col_start, at, own_cols, 2).reshape(total_slots, own_cols),
        lanczos_taps(
            lax.dynamic_slice_in_dim(col_frac, at, own_cols, 2).reshape(total_slots, own_cols)
        ),
        width,
    )
    scale = jnp.where(
        correlations.reshape(total_slots) == visit_at, jnp.repeat(weight, slots), 0.0
    )
    weight_map = lax.dot_general(
        row_cover,
        col_cover * scale[:, None],
        (((0,), (0,)), ((), ())),
        precision=lax.Precision.HIGHEST,
        preferred_element_type=F32,
    ).reshape(1, patch_rows, own_cols)
    coadd = summed / jnp.maximum(weight_map, FLOOR_SHARE * mean_weight)
    return coadd, weight_map


def solution(mesh):
    placed = (
        P("visit", "region", None),
        P("visit", "region", None),
        P("visit", None),
        P(),
        P(),
        P(),
        P(),
        P(),
    )
    return jax.shard_map(
        local,
        mesh=mesh,
        in_specs=placed,
        out_specs=(P("visit", None, "region"), P("visit", None, "region")),
        check_vma=False,
    )
```

```python
import functools
import math

import jax
import jax.numpy as jnp
from jax import lax
from jax.experimental import pallas as pl
from jax.experimental.pallas import tpu as pltpu
from jax.sharding import PartitionSpec as P

RADIUS = 10
TAPS = 6
SIGMAS = (1.0, 2.0, 4.0)
FLOOR_SHARE = 0.5
BF16 = jnp.bfloat16
F32 = jnp.float32

ROW_BLOCK = 128
ROW_STEP = 256
ROW_SPAN = 288
COL_BLOCK = 128
COL_STEP = 256
COL_GROUP = 8
BLUR_BLOCK = 256
BLUR_STEP = 512
BLUR_BAND = (112, 400)
LANES = 128
LIMIT = 28 * 1024 * 1024


def psf_kernel(coefficient):
    offsets = jnp.arange(-RADIUS, RADIUS + 1).astype(coefficient.dtype)
    sigmas = jnp.array(SIGMAS, dtype=coefficient.dtype)
    gaussians = jnp.exp(
        -(offsets[None, :] * offsets[None, :]) / (2.0 * sigmas[:, None] * sigmas[:, None])
    )
    kernel = jnp.sum(coefficient[:, :, None] * gaussians[None, :, :], axis=1)
    return kernel / jnp.sum(kernel, axis=1, keepdims=True)


def lanczos_taps(f):
    g = 1.0 - f
    third = math.pi / 3.0
    tiny = 1e-6
    a = jnp.sin(third * f)
    b = jnp.sin(third * g)
    c = a + b
    fg = f * g
    a_over_f = jnp.where(f < tiny, third, a / jnp.maximum(f, tiny))
    b_over_g = jnp.where(g < tiny, third, b / jnp.maximum(g, tiny))
    values = [
        b * fg / ((f + 2.0) * (f + 2.0)),
        -c * fg / ((f + 1.0) * (f + 1.0)),
        a_over_f * g,
        b_over_g * f,
        -c * fg / ((2.0 - f) * (2.0 - f)),
        a * fg / ((3.0 - f) * (3.0 - f)),
    ]
    total = functools.reduce(jnp.add, values)
    return [lax.reduce_precision(value / total, 8, 7) for value in values]


def coverage(starts, taps, extent):
    running = jnp.zeros(starts.shape, F32)
    for tap_at, tap in enumerate(taps):
        position = starts + tap_at
        inside = (position >= 0) & (position < extent)
        running = running + jnp.where(inside, tap, 0.0)
    return running


def band_tables(starts, taps):
    place = jnp.arange(8, dtype=jnp.int32)[:, None]
    diff = place - starts[..., None, :]
    at = diff & 7
    turned = jnp.zeros(diff.shape, F32)
    for tap_at, tap in enumerate(taps):
        turned = turned + jnp.where(at == tap_at, tap[..., None, :], 0.0)
    return turned, diff - at


def toeplitz(kernel_ref, at, rows, cols, shift):
    diff = (
        lax.broadcasted_iota(jnp.int32, (rows, cols), 0)
        - lax.broadcasted_iota(jnp.int32, (rows, cols), 1)
    )
    full = jnp.zeros((rows, cols), F32)
    for tap_at in range(2 * RADIUS + 1):
        full = jnp.where(diff == tap_at - shift, kernel_ref[at, tap_at], full)
    return full


def dot(a, b):
    return jnp.dot(a, b, preferred_element_type=F32)


def two_parts(value):
    high = value.astype(BF16)
    return high, (value - high.astype(F32)).astype(BF16)


def halves_sum(value):
    half = value.shape[0] // 2
    return value[:half] + value[half:]


def band_of(turned, key, first, groups):
    moved = key + first
    return [jnp.where(moved == -8 * g, turned, 0.0) for g in range(groups)]


def row_matrix(blur_ref, turned, key, start, extent, masked):
    last = extent - ROW_STEP
    first = jnp.minimum(start, last)
    groups = ROW_SPAN // 8
    pieces = band_of(turned, key, first - 16, groups)
    for g in range(2):
        pieces[g] = jnp.where(first > 0, pieces[g], 0.0)
        pieces[groups - 1 - g] = jnp.where(first < last, pieces[groups - 1 - g], 0.0)
    band = jnp.concatenate(pieces, axis=0).astype(BF16)
    both = halves_sum(dot(blur_ref[...], band))
    if masked:
        row = lax.broadcasted_iota(jnp.int32, both.shape, 0) + first
        both = jnp.where(row >= start, both, 0.0)
    return jnp.concatenate(two_parts(both.T), axis=0)


def prepare_body(extent, row_kernel_ref, kernel_ref, low_ref, turned_ref, key_ref, rows_ref,
                 blur_ref, cols_ref):
    high, rest = two_parts(toeplitz(row_kernel_ref, 0, ROW_STEP, ROW_SPAN, 16 + RADIUS))
    blur_ref[0:ROW_STEP] = high
    blur_ref[ROW_STEP : 2 * ROW_STEP] = rest

    def block(at, carry):
        rows_ref[at] = row_matrix(
            blur_ref, turned_ref[at], key_ref[at], low_ref[at], extent, False
        )
        return carry

    lax.fori_loop(0, turned_ref.shape[0], block, 0)
    begin, end = BLUR_BAND
    for e in range(cols_ref.shape[0]):
        high, rest = two_parts(
            toeplitz(kernel_ref, e, end - begin, BLUR_BLOCK, begin - LANES + RADIUS)
        )
        cols_ref[e, 0] = high
        cols_ref[e, 1] = rest


def prepare(row_kernel, kernels, low, turned, key, extent):
    exposures = kernels.shape[0]
    blocks = turned.shape[0]
    vmem = pl.BlockSpec(memory_space=pltpu.VMEM)
    smem = pl.BlockSpec(memory_space=pltpu.SMEM)
    return pl.pallas_call(
        functools.partial(prepare_body, extent),
        out_shape=(
            jax.ShapeDtypeStruct((blocks, 2 * ROW_BLOCK, ROW_STEP), BF16),
            jax.ShapeDtypeStruct((2 * ROW_STEP, ROW_SPAN), BF16),
            jax.ShapeDtypeStruct((exposures, 2, BLUR_BAND[1] - BLUR_BAND[0], BLUR_BLOCK), BF16),
        ),
        in_specs=[smem, smem, smem, vmem, vmem],
        out_specs=(vmem, vmem, vmem),
        compiler_params=pltpu.CompilerParams(vmem_limit_bytes=LIMIT),
        cost_estimate=pl.CostEstimate(
            flops=4_000_000_000, bytes_accessed=8 * 1024 * 1024, transcendentals=0
        ),
        name="prepare",
    )(row_kernel, kernels, low, turned, key)


def row_body(slots, low_ref, num_ref, x_ref, rows_ref, blur_ref, turned_ref, key_ref, out_ref):
    extent = x_ref.shape[0]
    owner_rows = out_ref.shape[2]
    blocks = turned_ref.shape[0] // slots

    def times(matrix, start):
        first = pl.multiple_of(jnp.minimum(start, extent - ROW_STEP), 16)
        return halves_sum(dot(matrix, x_ref[pl.ds(first, ROW_STEP), :]))

    def block(at, carry):
        indices = [slot * blocks + at for slot in range(slots)]
        sums = [times(rows_ref[index], low_ref[index]) for index in indices]
        for slot, index in enumerate(indices):

            def more(i, total, index=index):
                start = low_ref[index] + i * ROW_STEP
                matrix = row_matrix(
                    blur_ref, turned_ref[index], key_ref[index], start, extent, True
                )
                return total + times(matrix, start)

            total = lax.fori_loop(1, num_ref[index], more, sums[slot]).astype(BF16)
            for owner in range(ROW_BLOCK // owner_rows):
                out_ref[at * (ROW_BLOCK // owner_rows) + owner, slot] = total[
                    owner * owner_rows : (owner + 1) * owner_rows
                ]
        return carry

    lax.fori_loop(0, blocks, block, 0)


def row_warp(x, low, num, matrices, blur, turned, key, slots, owners):
    width = x.shape[1]
    owner_rows = turned.shape[0] // slots * ROW_BLOCK // owners
    vmem = pl.BlockSpec(memory_space=pltpu.VMEM)
    smem = pl.BlockSpec(memory_space=pltpu.SMEM)
    return pl.pallas_call(
        functools.partial(row_body, slots),
        out_shape=jax.ShapeDtypeStruct((owners, slots, owner_rows, width), BF16),
        in_specs=[smem, smem] + [vmem] * 5,
        out_specs=vmem,
        compiler_params=pltpu.CompilerParams(vmem_limit_bytes=LIMIT),
        cost_estimate=pl.CostEstimate(
            flops=2_000_000_000, bytes_accessed=8 * 1024 * 1024, transcendentals=0
        ),
        name="row_warp",
    )(low, num, x, matrices, blur, turned, key)


def col_body(cols, slots, count_ref, list_ref, low_ref, most_ref, from_ref, to_ref, weight_ref,
             z_ref, blur_ref, turned_ref, key_ref, out_ref, padded, blur, blurred, held):
    rows = z_ref.shape[2]
    width = z_ref.shape[3]
    sources = cols // width
    exposures = z_ref.shape[0] // sources
    patch = pl.program_id(0)
    begin, end = BLUR_BAND

    @pl.when(patch == 0)
    def _():
        pad = jnp.zeros((slots * rows, LANES), BF16)
        padded[:, 0:LANES] = pad
        padded[:, LANES + cols : 2 * LANES + cols] = pad
        for n in range(2):
            blur[n, 0:begin] = jnp.zeros((begin, BLUR_BLOCK), BF16)
            blur[n, end:BLUR_STEP] = jnp.zeros((BLUR_STEP - end, BLUR_BLOCK), BF16)
        for e in range(exposures):
            for n in range(2):
                blur[n, begin:end] = blur_ref[e, n]
            for s in range(sources):
                padded[:, LANES + s * width : LANES + (s + 1) * width] = z_ref[
                    e * sources + s
                ].reshape(slots * rows, width)
            windows = jnp.concatenate(
                [
                    padded[:, b * BLUR_BLOCK : b * BLUR_BLOCK + BLUR_STEP]
                    for b in range(cols // BLUR_BLOCK)
                ],
                axis=0,
            )
            high, rest = two_parts(dot(windows, blur[0]) + dot(windows, blur[1]))
            for b in range(cols // BLUR_BLOCK):
                for j in range(slots):
                    at = (b * slots + j) * rows
                    span = slice(b * BLUR_BLOCK, (b + 1) * BLUR_BLOCK)
                    blurred[e * slots + j, 0:rows, span] = high[at : at + rows]
                    blurred[e * slots + j, rows : 2 * rows, span] = rest[at : at + rows]
            for j in range(slots):
                blurred[e * slots + j, :, cols : cols + COL_STEP] = jnp.zeros(
                    (2 * rows, COL_STEP), BF16
                )

    held[...] = jnp.zeros(held.shape, F32)

    def part(slot, b, n):
        first = pl.multiple_of(jnp.minimum(low_ref[slot, b] + n * COL_STEP, cols), LANES)
        band = band_of(turned_ref[slot, b], key_ref[slot, b], first, COL_STEP // 8)
        band = jnp.concatenate(band, axis=0).astype(BF16)
        return halves_sum(dot(blurred[slot, :, pl.ds(first, COL_STEP)], band))

    per_owner = held.shape[2] // COL_BLOCK

    def add_slot(i, carry):
        slot = list_ref[patch, i]
        weight = weight_ref[slot]

        def add_group(c, carry):
            def add_parts(n):
                sums = [part(slot, c * COL_GROUP + h, n) for h in range(COL_GROUP)]
                for h, total in enumerate(sums):
                    owner = c * (COL_GROUP // per_owner) + h // per_owner
                    span = slice((h % per_owner) * COL_BLOCK, (h % per_owner + 1) * COL_BLOCK)
                    held[owner, :, span] += weight * total

            add_parts(0)

            def more(n, carry):
                add_parts(n)
                return carry

            lax.fori_loop(1, most_ref[slot, c], more, 0)
            return carry

        return lax.fori_loop(from_ref[slot], to_ref[slot], add_group, carry)

    lax.fori_loop(0, count_ref[patch], add_slot, 0)
    out_ref[0] = held[...].astype(out_ref.dtype)


def col_warp(z, count, listed, low, most, begin, end, weight, blur, turned, key, cols, patches,
             owners):
    slots, rows = z.shape[1:3]
    slot_total, blocks = turned.shape[:2]
    own_cols = blocks * COL_BLOCK // owners
    vmem = pl.BlockSpec(memory_space=pltpu.VMEM)
    smem = pl.BlockSpec(memory_space=pltpu.SMEM)
    return pl.pallas_call(
        functools.partial(col_body, cols, slots),
        out_shape=jax.ShapeDtypeStruct((patches, owners, rows, own_cols), BF16),
        grid=(patches,),
        in_specs=[smem] * 7 + [vmem] * 4,
        out_specs=pl.BlockSpec((1, owners, rows, own_cols), lambda k: (k, 0, 0, 0)),
        scratch_shapes=[
            pltpu.VMEM((slots * rows, cols + 2 * LANES), BF16),
            pltpu.VMEM((2, BLUR_STEP, BLUR_BLOCK), BF16),
            pltpu.VMEM((slot_total, 2 * rows, cols + COL_STEP), BF16),
            pltpu.VMEM((owners, rows, own_cols), F32),
        ],
        compiler_params=pltpu.CompilerParams(
            dimension_semantics=("arbitrary",), vmem_limit_bytes=LIMIT
        ),
        cost_estimate=pl.CostEstimate(
            flops=8_000_000_000, bytes_accessed=16 * 1024 * 1024, transcendentals=0
        ),
        name="col_warp",
    )(count, listed, low, most, begin, end, weight, z, blur, turned, key)


def butterfly_sum(x, axis):
    size = lax.axis_size(axis)
    step = 1
    while step < size:
        x = x + lax.ppermute(x, axis, [(i, i ^ step) for i in range(size)])
        step *= 2
    return x


def local(image, variance, psf_coef, correlations, row_start, row_frac, col_start, col_frac):
    exp_dev, height, width = image.shape
    exposures, slots = correlations.shape
    patch_rows = row_start.shape[2]
    patch_cols = col_start.shape[2]
    cores = lax.axis_size("core")
    visits = lax.axis_size("y") * cores
    regions = lax.axis_size("region")
    extent = height * regions
    parts = regions // exp_dev
    part_cols = width // parts
    own_cols = patch_cols // regions
    pair_at = lax.axis_index("y")
    core_at = lax.axis_index("core")
    visit_at = pair_at * cores + core_at
    region_at = lax.axis_index("region")

    def exchange(x, axis):
        return lax.all_to_all(x, axis, split_axis=0, concat_axis=0, tiled=True)

    sent = image.reshape(exp_dev, height, parts, part_cols).transpose(0, 2, 1, 3)
    sent, variance = lax.optimization_barrier(
        (sent.reshape(regions, height, part_cols), variance)
    )
    columns = exchange(sent, "region").reshape(extent, part_cols)

    kernels = psf_kernel(psf_coef)
    tile = jnp.zeros((8, LANES), F32).at[:exp_dev, : 2 * RADIUS + 1].set(kernels)
    other = lax.ppermute(tile, "core", [(i, i ^ 1) for i in range(cores)])
    other = other[:exp_dev, : 2 * RADIUS + 1]
    pair_kernels = jnp.concatenate(
        [jnp.where(core_at == 0, kernels, other), jnp.where(core_at == 0, other, kernels)]
    )
    local_sums = jnp.sum(variance.astype(F32), axis=(1, 2))
    tile = jnp.zeros((8, LANES), F32).at[0, :exp_dev].set(local_sums)
    tile = butterfly_sum(tile, "region")
    at_visit = lax.broadcasted_iota(jnp.int32, (8, LANES), 0) == visit_at
    tile = jnp.where(at_visit, tile[0:1], 0.0)
    tile = butterfly_sum(tile, "core")
    pair_exp = cores * exp_dev
    first_exp = pair_at * pair_exp
    pair_sums = lax.dynamic_slice_in_dim(tile, pair_at * cores, cores, 0)[:, :exp_dev]
    slot_weight = jnp.repeat(1.0 / (pair_sums.reshape(pair_exp) / (extent * width)), slots)

    own_exp = region_at // parts
    at_exp = visit_at * exp_dev + own_exp
    blocks = slots * patch_rows // ROW_BLOCK
    starts = lax.dynamic_index_in_dim(row_start, at_exp, 0, keepdims=False)
    fracs = lax.dynamic_index_in_dim(row_frac, at_exp, 0, keepdims=False)
    starts = starts.reshape(blocks, ROW_BLOCK)
    row_turned, row_key = band_tables(starts, lanczos_taps(fracs.reshape(blocks, ROW_BLOCK)))
    row_low = jnp.clip(starts[:, 0] - RADIUS, 0, extent - ROW_STEP) // 16 * 16
    row_end = jnp.minimum(starts[:, -1] + TAPS + RADIUS, extent)
    row_num = jnp.maximum(row_end - row_low + ROW_STEP - 1, 0) // ROW_STEP
    row_matrices, row_blur, col_blur = prepare(
        lax.dynamic_slice_in_dim(kernels, own_exp, 1, 0), pair_kernels, row_low, row_turned,
        row_key, extent,
    )

    slot_total = pair_exp * slots
    col_blocks = patch_cols // COL_BLOCK
    own_starts = lax.dynamic_slice_in_dim(col_start, first_exp, pair_exp, 0)
    own_fracs = lax.dynamic_slice_in_dim(col_frac, first_exp, pair_exp, 0)
    own_starts = own_starts.reshape(slot_total, col_blocks, COL_BLOCK)
    own_fracs = own_fracs.reshape(slot_total, col_blocks, COL_BLOCK)
    col_turned, col_key = band_tables(own_starts, lanczos_taps(own_fracs))
    col_low = jnp.clip(own_starts[:, :, 0], 0, width) // LANES * LANES
    col_end = jnp.minimum(own_starts[:, :, -1] + TAPS, width)
    col_num = jnp.maximum(col_end - col_low + COL_STEP - 1, 0) // COL_STEP
    col_most = jnp.max(col_num.reshape(slot_total, col_blocks // COL_GROUP, COL_GROUP), axis=2)
    group_at = jnp.arange(col_blocks // COL_GROUP, dtype=jnp.int32)
    col_from = jnp.min(jnp.where(col_most > 0, group_at, col_blocks // COL_GROUP), axis=1)
    col_to = jnp.max(jnp.where(col_most > 0, group_at + 1, 0), axis=1)
    owners = lax.dynamic_slice_in_dim(correlations, first_exp, pair_exp, 0).reshape(slot_total)
    named = owners == jnp.arange(visits, dtype=jnp.int32)[:, None]
    named = named.astype(jnp.int32)
    count = jnp.sum(named, axis=1)
    slot_ids = jnp.arange(slot_total, dtype=jnp.int32)
    rank = jnp.sum(jnp.where(slot_ids[:, None] < slot_ids, named[:, :, None], 0), axis=1)
    listed = jnp.sum(
        jnp.where((named[:, None, :] > 0) & (rank[:, None, :] == slot_ids[:, None]), slot_ids, 0),
        axis=2,
    )

    warped = row_warp(
        columns, row_low, row_num, row_matrices, row_blur, row_turned, row_key, slots,
        cores * regions,
    )
    tile, warped = lax.optimization_barrier((tile, warped))
    rows = exchange(warped, ("core", "region"))
    tile = butterfly_sum(tile, "y")
    weight = 1.0 / (tile[:visits, :exp_dev].reshape(exposures) / (extent * width))
    mean_weight = jnp.mean(weight)
    partial = col_warp(
        rows, count, listed, col_low, col_most, col_from, col_to, slot_weight, col_blur,
        col_turned, col_key, width, visits, regions,
    )
    pieces = exchange(
        partial.reshape((visits * regions,) + partial.shape[2:]), ("y", "core", "region")
    )
    summed = jnp.sum(
        pieces.reshape(visits // cores, patch_rows, own_cols).astype(F32), axis=0, keepdims=True
    )

    total_slots = exposures * slots
    row_cover = coverage(
        row_start.reshape(total_slots, patch_rows),
        lanczos_taps(row_frac.reshape(total_slots, patch_rows)),
        extent,
    )
    at = region_at * own_cols
    col_cover = coverage(
        lax.dynamic_slice_in_dim(col_start, at, own_cols, 2).reshape(total_slots, own_cols),
        lanczos_taps(
            lax.dynamic_slice_in_dim(col_frac, at, own_cols, 2).reshape(total_slots, own_cols)
        ),
        width,
    )
    scale = jnp.where(
        correlations.reshape(total_slots) == visit_at, jnp.repeat(weight, slots), 0.0
    )
    weight_map = lax.dot_general(
        row_cover,
        col_cover * scale[:, None],
        (((0,), (0,)), ((), ())),
        precision=lax.Precision.HIGHEST,
        preferred_element_type=F32,
    ).reshape(1, patch_rows, own_cols)
    coadd = summed / jnp.maximum(weight_map, FLOOR_SHARE * mean_weight)
    return coadd, weight_map


def solution(mesh):
    visits, regions = mesh.devices.shape
    split = jax.sharding.Mesh(
        mesh.devices.reshape(visits // 2, 2, regions), ("y", "core", "region")
    )
    visit = ("y", "core")
    placed = (
        P(visit, "region", None),
        P(visit, "region", None),
        P(visit, None),
        P(),
        P(),
        P(),
        P(),
        P(),
    )
    return jax.shard_map(
        local,
        mesh=split,
        in_specs=placed,
        out_specs=(P(visit, None, "region"), P(visit, None, "region")),
        check_vma=False,
    )
```

```python
import functools
import math

import jax
import jax.numpy as jnp
from jax import lax
from jax.experimental import pallas as pl
from jax.experimental.pallas import tpu as pltpu
from jax.sharding import PartitionSpec as P

RADIUS = 10
TAPS = 6
SIGMAS = (1.0, 2.0, 4.0)
FLOOR_SHARE = 0.5
BF16 = jnp.bfloat16
F32 = jnp.float32

ROW_BLOCK = 128
ROW_STEP = 256
ROW_SPAN = 288
COL_BLOCK = 128
COL_STEP = 256
COL_GROUP = 8
BLUR_BLOCK = 256
BLUR_STEP = 512
BLUR_BAND = (112, 400)
LANES = 128
LIMIT = 28 * 1024 * 1024
COL_LIMIT = 56 * 1024 * 1024


def psf_kernel(coefficient):
    offsets = jnp.arange(-RADIUS, RADIUS + 1).astype(coefficient.dtype)
    sigmas = jnp.array(SIGMAS, dtype=coefficient.dtype)
    gaussians = jnp.exp(
        -(offsets[None, :] * offsets[None, :]) / (2.0 * sigmas[:, None] * sigmas[:, None])
    )
    kernel = jnp.sum(coefficient[:, :, None] * gaussians[None, :, :], axis=1)
    return kernel / jnp.sum(kernel, axis=1, keepdims=True)


def lanczos_taps(f):
    g = 1.0 - f
    third = math.pi / 3.0
    tiny = 1e-6
    a = jnp.sin(third * f)
    b = jnp.sin(third * g)
    c = a + b
    fg = f * g
    a_over_f = jnp.where(f < tiny, third, a / jnp.maximum(f, tiny))
    b_over_g = jnp.where(g < tiny, third, b / jnp.maximum(g, tiny))
    values = [
        b * fg / ((f + 2.0) * (f + 2.0)),
        -c * fg / ((f + 1.0) * (f + 1.0)),
        a_over_f * g,
        b_over_g * f,
        -c * fg / ((2.0 - f) * (2.0 - f)),
        a * fg / ((3.0 - f) * (3.0 - f)),
    ]
    total = functools.reduce(jnp.add, values)
    return [lax.reduce_precision(value / total, 8, 7) for value in values]


def coverage(starts, taps, extent):
    running = jnp.zeros(starts.shape, F32)
    for tap_at, tap in enumerate(taps):
        position = starts + tap_at
        inside = (position >= 0) & (position < extent)
        running = running + jnp.where(inside, tap, 0.0)
    return running


def band_tables(starts, taps):
    place = jnp.arange(8, dtype=jnp.int32)[:, None]
    diff = place - starts[..., None, :]
    at = diff & 7
    turned = jnp.zeros(diff.shape, F32)
    for tap_at, tap in enumerate(taps):
        turned = turned + jnp.where(at == tap_at, tap[..., None, :], 0.0)
    return turned, diff - at


def toeplitz(kernel_ref, at, rows, cols, shift):
    diff = (
        lax.broadcasted_iota(jnp.int32, (rows, cols), 0)
        - lax.broadcasted_iota(jnp.int32, (rows, cols), 1)
    )
    full = jnp.zeros((rows, cols), F32)
    for tap_at in range(2 * RADIUS + 1):
        full = jnp.where(diff == tap_at - shift, kernel_ref[at, tap_at], full)
    return full


def dot(a, b):
    return jnp.dot(a, b, preferred_element_type=F32)


def two_parts(value):
    high = value.astype(BF16)
    return high, (value - high.astype(F32)).astype(BF16)


def halves_sum(value):
    half = value.shape[0] // 2
    return value[:half] + value[half:]


def band_of(turned, key, first, groups):
    moved = key + first
    return [jnp.where(moved == -8 * g, turned, 0.0) for g in range(groups)]


def row_matrix(blur_ref, turned, key, start, extent, masked):
    last = extent - ROW_STEP
    first = jnp.minimum(start, last)
    groups = ROW_SPAN // 8
    pieces = band_of(turned, key, first - 16, groups)
    for g in range(2):
        pieces[g] = jnp.where(first > 0, pieces[g], 0.0)
        pieces[groups - 1 - g] = jnp.where(first < last, pieces[groups - 1 - g], 0.0)
    band = jnp.concatenate(pieces, axis=0).astype(BF16)
    both = halves_sum(dot(blur_ref[...], band))
    if masked:
        row = lax.broadcasted_iota(jnp.int32, both.shape, 0) + first
        both = jnp.where(row >= start, both, 0.0)
    return jnp.concatenate(two_parts(both.T), axis=0)


def prepare_body(extent, row_kernel_ref, kernel_ref, low_ref, turned_ref, key_ref, rows_ref,
                 blur_ref, cols_ref):
    high, rest = two_parts(toeplitz(row_kernel_ref, 0, ROW_STEP, ROW_SPAN, 16 + RADIUS))
    blur_ref[0:ROW_STEP] = high
    blur_ref[ROW_STEP : 2 * ROW_STEP] = rest

    def block(at, carry):
        rows_ref[at] = row_matrix(
            blur_ref, turned_ref[at], key_ref[at], low_ref[at], extent, False
        )
        return carry

    lax.fori_loop(0, turned_ref.shape[0], block, 0)
    begin, end = BLUR_BAND
    for e in range(cols_ref.shape[0]):
        high, rest = two_parts(
            toeplitz(kernel_ref, e, end - begin, BLUR_BLOCK, begin - LANES + RADIUS)
        )
        cols_ref[e, 0] = high
        cols_ref[e, 1] = rest


def prepare(row_kernel, kernels, low, turned, key, extent):
    exposures = kernels.shape[0]
    blocks = turned.shape[0]
    vmem = pl.BlockSpec(memory_space=pltpu.VMEM)
    smem = pl.BlockSpec(memory_space=pltpu.SMEM)
    return pl.pallas_call(
        functools.partial(prepare_body, extent),
        out_shape=(
            jax.ShapeDtypeStruct((blocks, 2 * ROW_BLOCK, ROW_STEP), BF16),
            jax.ShapeDtypeStruct((2 * ROW_STEP, ROW_SPAN), BF16),
            jax.ShapeDtypeStruct((exposures, 2, BLUR_BAND[1] - BLUR_BAND[0], BLUR_BLOCK), BF16),
        ),
        in_specs=[smem, smem, smem, vmem, vmem],
        out_specs=(vmem, vmem, vmem),
        compiler_params=pltpu.CompilerParams(vmem_limit_bytes=LIMIT),
        cost_estimate=pl.CostEstimate(
            flops=4_000_000_000, bytes_accessed=8 * 1024 * 1024, transcendentals=0
        ),
        name="prepare",
    )(row_kernel, kernels, low, turned, key)


def row_body(slots, low_ref, num_ref, x_ref, rows_ref, blur_ref, turned_ref, key_ref, out_ref):
    extent = x_ref.shape[0]
    owner_rows = out_ref.shape[2]
    blocks = turned_ref.shape[0] // slots

    def times(matrix, start):
        first = pl.multiple_of(jnp.minimum(start, extent - ROW_STEP), 16)
        return halves_sum(dot(matrix, x_ref[pl.ds(first, ROW_STEP), :]))

    def block(at, carry):
        indices = [slot * blocks + at for slot in range(slots)]
        sums = [times(rows_ref[index], low_ref[index]) for index in indices]
        for slot, index in enumerate(indices):

            def more(i, total, index=index):
                start = low_ref[index] + i * ROW_STEP
                matrix = row_matrix(
                    blur_ref, turned_ref[index], key_ref[index], start, extent, True
                )
                return total + times(matrix, start)

            total = lax.fori_loop(1, num_ref[index], more, sums[slot]).astype(BF16)
            for owner in range(ROW_BLOCK // owner_rows):
                out_ref[at * (ROW_BLOCK // owner_rows) + owner, slot] = total[
                    owner * owner_rows : (owner + 1) * owner_rows
                ]
        return carry

    lax.fori_loop(0, blocks, block, 0)


def row_warp(x, low, num, matrices, blur, turned, key, slots, owners):
    width = x.shape[1]
    owner_rows = turned.shape[0] // slots * ROW_BLOCK // owners
    vmem = pl.BlockSpec(memory_space=pltpu.VMEM)
    smem = pl.BlockSpec(memory_space=pltpu.SMEM)
    return pl.pallas_call(
        functools.partial(row_body, slots),
        out_shape=jax.ShapeDtypeStruct((owners, slots, owner_rows, width), BF16),
        in_specs=[smem, smem] + [vmem] * 5,
        out_specs=vmem,
        compiler_params=pltpu.CompilerParams(vmem_limit_bytes=LIMIT),
        cost_estimate=pl.CostEstimate(
            flops=2_000_000_000, bytes_accessed=8 * 1024 * 1024, transcendentals=0
        ),
        name="row_warp",
    )(low, num, x, matrices, blur, turned, key)


def col_body(cols, count_ref, list_ref, low_ref, most_ref, from_ref, to_ref, weight_ref, z_hbm,
             blur_hbm, turned_hbm, key_hbm, out_ref, padded, blur, turned_ref, key_ref, blurred,
             held, z_sems, blur_sems, table_sems):
    slots, rows, width = z_hbm.shape[1:]
    sources = cols // width
    exposures = z_hbm.shape[0] // sources
    patch = pl.program_id(0)
    begin, end = BLUR_BAND

    @pl.when(patch == 0)
    def _():
        waits = []
        for e in range(exposures):
            copies = []
            for s in range(sources):
                for j in range(slots):
                    copies.append(
                        pltpu.make_async_copy(
                            z_hbm.at[e * sources + s, j],
                            padded.at[
                                e, pl.ds(j * rows, rows), pl.ds(LANES + s * width, width)
                            ],
                            z_sems.at[e, s, j],
                        )
                    )
            for n in range(2):
                copies.append(
                    pltpu.make_async_copy(
                        blur_hbm.at[e, n],
                        blur.at[e, n, pl.ds(begin, end - begin)],
                        blur_sems.at[e, n],
                    )
                )
            for copy in copies:
                copy.start()
            waits.append(copies)
        tables = [
            pltpu.make_async_copy(turned_hbm, turned_ref, table_sems.at[0]),
            pltpu.make_async_copy(key_hbm, key_ref, table_sems.at[1]),
        ]
        for copy in tables:
            copy.start()
        pad = jnp.zeros((slots * rows, LANES), BF16)
        for e in range(exposures):
            padded[e, :, 0:LANES] = pad
            padded[e, :, LANES + cols : 2 * LANES + cols] = pad
            for n in range(2):
                blur[e, n, 0:begin] = jnp.zeros((begin, BLUR_BLOCK), BF16)
                blur[e, n, end:BLUR_STEP] = jnp.zeros((BLUR_STEP - end, BLUR_BLOCK), BF16)
            for j in range(slots):
                blurred[e * slots + j, :, cols : cols + COL_STEP] = jnp.zeros(
                    (2 * rows, COL_STEP), BF16
                )
        for e in range(exposures):
            for copy in waits[e]:
                copy.wait()
            windows = jnp.concatenate(
                [
                    padded[e, :, b * BLUR_BLOCK : b * BLUR_BLOCK + BLUR_STEP]
                    for b in range(cols // BLUR_BLOCK)
                ],
                axis=0,
            )
            high, rest = two_parts(dot(windows, blur[e, 0]) + dot(windows, blur[e, 1]))
            for b in range(cols // BLUR_BLOCK):
                for j in range(slots):
                    at = (b * slots + j) * rows
                    span = slice(b * BLUR_BLOCK, (b + 1) * BLUR_BLOCK)
                    blurred[e * slots + j, 0:rows, span] = high[at : at + rows]
                    blurred[e * slots + j, rows : 2 * rows, span] = rest[at : at + rows]
        for copy in tables:
            copy.wait()

    held[...] = jnp.zeros(held.shape, F32)

    def part(slot, b, n):
        first = pl.multiple_of(jnp.minimum(low_ref[slot, b] + n * COL_STEP, cols), LANES)
        band = band_of(turned_ref[slot, b], key_ref[slot, b], first, COL_STEP // 8)
        band = jnp.concatenate(band, axis=0).astype(BF16)
        return halves_sum(dot(blurred[slot, :, pl.ds(first, COL_STEP)], band))

    per_owner = held.shape[2] // COL_BLOCK

    def add_slot(i, carry):
        slot = list_ref[patch, i]
        weight = weight_ref[slot]

        def add_group(c, carry):
            def add_parts(n):
                sums = [part(slot, c * COL_GROUP + h, n) for h in range(COL_GROUP)]
                for h, total in enumerate(sums):
                    owner = c * (COL_GROUP // per_owner) + h // per_owner
                    span = slice((h % per_owner) * COL_BLOCK, (h % per_owner + 1) * COL_BLOCK)
                    held[owner, :, span] += weight * total

            add_parts(0)

            def more(n, carry):
                add_parts(n)
                return carry

            lax.fori_loop(1, most_ref[slot, c], more, 0)
            return carry

        return lax.fori_loop(from_ref[slot], to_ref[slot], add_group, carry)

    lax.fori_loop(0, count_ref[patch], add_slot, 0)
    out_ref[0] = held[...].astype(out_ref.dtype)


def col_warp(z, count, listed, low, most, begin, end, weight, blur, turned, key, cols, patches,
             owners):
    slots, rows, width = z.shape[1:]
    slot_total, blocks = turned.shape[:2]
    exposures = blur.shape[0]
    own_cols = blocks * COL_BLOCK // owners
    smem = pl.BlockSpec(memory_space=pltpu.SMEM)
    return pl.pallas_call(
        functools.partial(col_body, cols),
        out_shape=jax.ShapeDtypeStruct((patches, owners, rows, own_cols), BF16),
        grid=(patches,),
        in_specs=[smem] * 7 + [pl.BlockSpec(memory_space=pl.ANY)] * 4,
        out_specs=pl.BlockSpec((1, owners, rows, own_cols), lambda k: (k, 0, 0, 0)),
        scratch_shapes=[
            pltpu.VMEM((exposures, slots * rows, cols + 2 * LANES), BF16),
            pltpu.VMEM((exposures, 2, BLUR_STEP, BLUR_BLOCK), BF16),
            pltpu.VMEM(turned.shape, F32),
            pltpu.VMEM(key.shape, jnp.int32),
            pltpu.VMEM((slot_total, 2 * rows, cols + COL_STEP), BF16),
            pltpu.VMEM((owners, rows, own_cols), F32),
            pltpu.SemaphoreType.DMA((exposures, cols // width, slots)),
            pltpu.SemaphoreType.DMA((exposures, 2)),
            pltpu.SemaphoreType.DMA((2,)),
        ],
        compiler_params=pltpu.CompilerParams(
            dimension_semantics=("arbitrary",), vmem_limit_bytes=COL_LIMIT
        ),
        cost_estimate=pl.CostEstimate(
            flops=8_000_000_000, bytes_accessed=16 * 1024 * 1024, transcendentals=0
        ),
        name="col_warp",
    )(count, listed, low, most, begin, end, weight, z, blur, turned, key)


def split_body(image_ref, out_ref):
    out_ref[...] = image_ref[...]


def split_columns(image, parts):
    exposures, height, width = image.shape
    block = (1, height, width // parts)
    return pl.pallas_call(
        split_body,
        out_shape=jax.ShapeDtypeStruct((exposures * parts,) + block[1:], image.dtype),
        grid=(exposures * parts,),
        in_specs=[pl.BlockSpec(block, lambda i: (i // parts, 0, i % parts))],
        out_specs=pl.BlockSpec(block, lambda i: (i, 0, 0)),
        compiler_params=pltpu.CompilerParams(
            dimension_semantics=("arbitrary",), vmem_limit_bytes=COL_LIMIT
        ),
        name="split_columns",
    )(image)


def ring_sum(x, axis, count, stride):
    size = lax.axis_size(axis)
    total = x
    for step in range(1, count):
        pairs = []
        for i in range(size):
            at = i // stride % count
            pairs.append((i, i + ((at + step) % count - at) * stride))
        total = total + lax.ppermute(x, axis, pairs)
    return total


def butterfly_sum(x, axis):
    size = lax.axis_size(axis)
    step = 1
    while step < size:
        x = x + lax.ppermute(x, axis, [(i, i ^ step) for i in range(size)])
        step *= 2
    return x


def local(image, variance, psf_coef, correlations, row_start, row_frac, col_start, col_frac):
    exp_dev, height, width = image.shape
    exposures, slots = correlations.shape
    patch_rows = row_start.shape[2]
    patch_cols = col_start.shape[2]
    cores = lax.axis_size("core")
    visits = lax.axis_size("y") * cores
    regions = lax.axis_size("region")
    extent = height * regions
    parts = regions // exp_dev
    part_cols = width // parts
    own_cols = patch_cols // regions
    pair_at = lax.axis_index("y")
    core_at = lax.axis_index("core")
    visit_at = pair_at * cores + core_at
    region_at = lax.axis_index("region")

    def exchange(x, axis):
        return lax.all_to_all(x, axis, split_axis=0, concat_axis=0, tiled=True)

    sent, variance = lax.optimization_barrier((split_columns(image, parts), variance))
    columns = exchange(sent, "region").reshape(extent, part_cols)

    kernels = psf_kernel(psf_coef)
    tile = jnp.zeros((8, LANES), F32).at[:exp_dev, : 2 * RADIUS + 1].set(kernels)
    other = lax.ppermute(tile, "core", [(i, i ^ 1) for i in range(cores)])
    other = other[:exp_dev, : 2 * RADIUS + 1]
    pair_kernels = jnp.concatenate(
        [jnp.where(core_at == 0, kernels, other), jnp.where(core_at == 0, other, kernels)]
    )
    local_sums = jnp.sum(variance.astype(F32), axis=(1, 2))
    tile = jnp.zeros((8, LANES), F32).at[0, :exp_dev].set(local_sums)
    inner = 4
    tile = ring_sum(tile, "region", inner, 1)
    pair_exp = cores * exp_dev
    first_exp = pair_at * pair_exp

    own_exp = region_at // parts
    at_exp = visit_at * exp_dev + own_exp
    blocks = slots * patch_rows // ROW_BLOCK
    starts = lax.dynamic_index_in_dim(row_start, at_exp, 0, keepdims=False)
    fracs = lax.dynamic_index_in_dim(row_frac, at_exp, 0, keepdims=False)
    starts = starts.reshape(blocks, ROW_BLOCK)
    row_turned, row_key = band_tables(starts, lanczos_taps(fracs.reshape(blocks, ROW_BLOCK)))
    row_low = jnp.clip(starts[:, 0] - RADIUS, 0, extent - ROW_STEP) // 16 * 16
    row_end = jnp.minimum(starts[:, -1] + TAPS + RADIUS, extent)
    row_num = jnp.maximum(row_end - row_low + ROW_STEP - 1, 0) // ROW_STEP
    row_matrices, row_blur, col_blur = prepare(
        lax.dynamic_slice_in_dim(kernels, own_exp, 1, 0), pair_kernels, row_low, row_turned,
        row_key, extent,
    )
    tile, row_matrices, row_blur, col_blur = lax.optimization_barrier(
        (tile, row_matrices, row_blur, col_blur)
    )
    tile = ring_sum(tile, "region", regions // inner, inner)

    slot_total = pair_exp * slots
    col_blocks = patch_cols // COL_BLOCK
    own_starts = lax.dynamic_slice_in_dim(col_start, first_exp, pair_exp, 0)
    own_fracs = lax.dynamic_slice_in_dim(col_frac, first_exp, pair_exp, 0)
    own_starts = own_starts.reshape(slot_total, col_blocks, COL_BLOCK)
    own_fracs = own_fracs.reshape(slot_total, col_blocks, COL_BLOCK)
    col_turned, col_key = band_tables(own_starts, lanczos_taps(own_fracs))
    col_low = jnp.clip(own_starts[:, :, 0], 0, width) // LANES * LANES
    col_end = jnp.minimum(own_starts[:, :, -1] + TAPS, width)
    col_num = jnp.maximum(col_end - col_low + COL_STEP - 1, 0) // COL_STEP
    col_most = jnp.max(col_num.reshape(slot_total, col_blocks // COL_GROUP, COL_GROUP), axis=2)
    group_at = jnp.arange(col_blocks // COL_GROUP, dtype=jnp.int32)
    col_from = jnp.min(jnp.where(col_most > 0, group_at, col_blocks // COL_GROUP), axis=1)
    col_to = jnp.max(jnp.where(col_most > 0, group_at + 1, 0), axis=1)
    owners = lax.dynamic_slice_in_dim(correlations, first_exp, pair_exp, 0).reshape(slot_total)
    named = owners == jnp.arange(visits, dtype=jnp.int32)[:, None]
    named = named.astype(jnp.int32)
    count = jnp.sum(named, axis=1)
    slot_ids = jnp.arange(slot_total, dtype=jnp.int32)
    rank = jnp.sum(jnp.where(slot_ids[:, None] < slot_ids, named[:, :, None], 0), axis=1)
    listed = jnp.sum(
        jnp.where((named[:, None, :] > 0) & (rank[:, None, :] == slot_ids[:, None]), slot_ids, 0),
        axis=2,
    )

    warped = row_warp(
        columns, row_low, row_num, row_matrices, row_blur, row_turned, row_key, slots,
        cores * regions,
    )
    tile, warped = lax.optimization_barrier((tile, warped))
    rows = exchange(warped, ("core", "region"))
    at_visit = lax.broadcasted_iota(jnp.int32, (8, LANES), 0) == visit_at
    tile = jnp.where(at_visit, tile[0:1], 0.0)
    tile = butterfly_sum(tile, "core")
    pair_sums = lax.dynamic_slice_in_dim(tile, pair_at * cores, cores, 0)[:, :exp_dev]
    slot_weight = jnp.repeat(1.0 / (pair_sums.reshape(pair_exp) / (extent * width)), slots)
    tile = butterfly_sum(tile, "y")
    weight = 1.0 / (tile[:visits, :exp_dev].reshape(exposures) / (extent * width))
    mean_weight = jnp.mean(weight)
    partial = col_warp(
        rows, count, listed, col_low, col_most, col_from, col_to, slot_weight, col_blur,
        col_turned, col_key, width, visits, regions,
    )
    pieces = exchange(
        partial.reshape((visits * regions,) + partial.shape[2:]), ("y", "core", "region")
    )
    summed = jnp.sum(
        pieces.reshape(visits // cores, patch_rows, own_cols).astype(F32), axis=0, keepdims=True
    )

    total_slots = exposures * slots
    row_cover = coverage(
        row_start.reshape(total_slots, patch_rows),
        lanczos_taps(row_frac.reshape(total_slots, patch_rows)),
        extent,
    )
    at = region_at * own_cols
    col_cover = coverage(
        lax.dynamic_slice_in_dim(col_start, at, own_cols, 2).reshape(total_slots, own_cols),
        lanczos_taps(
            lax.dynamic_slice_in_dim(col_frac, at, own_cols, 2).reshape(total_slots, own_cols)
        ),
        width,
    )
    scale = jnp.where(
        correlations.reshape(total_slots) == visit_at, jnp.repeat(weight, slots), 0.0
    )
    weight_map = lax.dot_general(
        row_cover,
        col_cover * scale[:, None],
        (((0,), (0,)), ((), ())),
        precision=lax.Precision.HIGHEST,
        preferred_element_type=F32,
    ).reshape(1, patch_rows, own_cols)
    coadd = summed / jnp.maximum(weight_map, FLOOR_SHARE * mean_weight)
    return coadd, weight_map


def solution(mesh):
    visits, regions = mesh.devices.shape
    split = jax.sharding.Mesh(
        mesh.devices.reshape(visits // 2, 2, regions), ("y", "core", "region")
    )
    visit = ("y", "core")
    placed = (
        P(visit, "region", None),
        P(visit, "region", None),
        P(visit, None),
        P(),
        P(),
        P(),
        P(),
        P(),
    )
    return jax.shard_map(
        local,
        mesh=split,
        in_specs=placed,
        out_specs=(P(visit, None, "region"), P(visit, None, "region")),
        check_vma=False,
    )
```

```python
import functools
import math

import jax
import jax.numpy as jnp
from jax import lax
from jax.experimental import pallas as pl
from jax.experimental.pallas import tpu as pltpu
from jax.sharding import PartitionSpec as P

RADIUS = 10
TAPS = 6
SIGMAS = (1.0, 2.0, 4.0)
FLOOR_SHARE = 0.5
BF16 = jnp.bfloat16
F32 = jnp.float32

ROW_BLOCK = 128
ROW_STEP = 256
ROW_SPAN = 288
COL_BLOCK = 128
COL_STEP = 256
COL_GROUP = 9
BLUR_BLOCK = 256
BLUR_STEP = 512
BLUR_BAND = (112, 400)
LANES = 128
LIMIT = 14 * 1024 * 1024
COL_LIMIT = 56 * 1024 * 1024


def psf_kernel(coefficient):
    offsets = jnp.arange(-RADIUS, RADIUS + 1).astype(coefficient.dtype)
    sigmas = jnp.array(SIGMAS, dtype=coefficient.dtype)
    gaussians = jnp.exp(
        -(offsets[None, :] * offsets[None, :]) / (2.0 * sigmas[:, None] * sigmas[:, None])
    )
    kernel = jnp.sum(coefficient[:, :, None] * gaussians[None, :, :], axis=1)
    return kernel / jnp.sum(kernel, axis=1, keepdims=True)


def lanczos_taps(f):
    g = 1.0 - f
    third = math.pi / 3.0
    tiny = 1e-6
    a = jnp.sin(third * f)
    b = jnp.sin(third * g)
    c = a + b
    fg = f * g
    a_over_f = jnp.where(f < tiny, third, a / jnp.maximum(f, tiny))
    b_over_g = jnp.where(g < tiny, third, b / jnp.maximum(g, tiny))
    values = [
        b * fg / ((f + 2.0) * (f + 2.0)),
        -c * fg / ((f + 1.0) * (f + 1.0)),
        a_over_f * g,
        b_over_g * f,
        -c * fg / ((2.0 - f) * (2.0 - f)),
        a * fg / ((3.0 - f) * (3.0 - f)),
    ]
    total = functools.reduce(jnp.add, values)
    return [lax.reduce_precision(value / total, 8, 7) for value in values]


def coverage(starts, taps, extent):
    running = jnp.zeros(starts.shape, F32)
    for tap_at, tap in enumerate(taps):
        position = starts + tap_at
        inside = (position >= 0) & (position < extent)
        running = running + jnp.where(inside, tap, 0.0)
    return running


def band_tables(starts, taps):
    place = jnp.arange(8, dtype=jnp.int32)[:, None]
    diff = place - starts[..., None, :]
    at = diff & 7
    turned = jnp.zeros(diff.shape, F32)
    for tap_at, tap in enumerate(taps):
        turned = turned + jnp.where(at == tap_at, tap[..., None, :], 0.0)
    return turned, diff - at


def toeplitz(kernel_ref, at, rows, cols, shift):
    diff = (
        lax.broadcasted_iota(jnp.int32, (rows, cols), 0)
        - lax.broadcasted_iota(jnp.int32, (rows, cols), 1)
    )
    full = jnp.zeros((rows, cols), F32)
    for tap_at in range(2 * RADIUS + 1):
        full = jnp.where(diff == tap_at - shift, kernel_ref[at, tap_at], full)
    return full


def dot(a, b):
    return jnp.dot(a, b, preferred_element_type=F32)


def two_parts(value):
    high = value.astype(BF16)
    return high, (value - high.astype(F32)).astype(BF16)


def halves_sum(value):
    half = value.shape[0] // 2
    return value[:half] + value[half:]


def band_of(turned, key, first, groups):
    moved = key + first
    return [jnp.where(moved == -8 * g, turned, 0.0) for g in range(groups)]


def row_matrix(blur_ref, turned, key, start, extent, masked):
    last = extent - ROW_STEP
    first = jnp.minimum(start, last)
    groups = ROW_SPAN // 8
    pieces = band_of(turned, key, first - 16, groups)
    for g in range(2):
        pieces[g] = jnp.where(first > 0, pieces[g], 0.0)
        pieces[groups - 1 - g] = jnp.where(first < last, pieces[groups - 1 - g], 0.0)
    band = jnp.concatenate(pieces, axis=0).astype(BF16)
    both = halves_sum(dot(blur_ref[...], band))
    if masked:
        row = lax.broadcasted_iota(jnp.int32, both.shape, 0) + first
        both = jnp.where(row >= start, both, 0.0)
    return jnp.concatenate(two_parts(both.T), axis=0)


def row_matrices_body(extent, kernel_ref, low_ref, turned_ref, key_ref, rows_ref, blur_ref):
    high, rest = two_parts(toeplitz(kernel_ref, 0, ROW_STEP, ROW_SPAN, 16 + RADIUS))
    blur_ref[0:ROW_STEP] = high
    blur_ref[ROW_STEP : 2 * ROW_STEP] = rest

    def block(at, carry):
        rows_ref[at] = row_matrix(
            blur_ref, turned_ref[at], key_ref[at], low_ref[at], extent, False
        )
        return carry

    lax.fori_loop(0, turned_ref.shape[0], block, 0)


def make_row_matrices(kernel, low, turned, key, extent):
    blocks = turned.shape[0]
    vmem = pl.BlockSpec(memory_space=pltpu.VMEM)
    smem = pl.BlockSpec(memory_space=pltpu.SMEM)
    return pl.pallas_call(
        functools.partial(row_matrices_body, extent),
        out_shape=(
            jax.ShapeDtypeStruct((blocks, 2 * ROW_BLOCK, ROW_STEP), BF16),
            jax.ShapeDtypeStruct((2 * ROW_STEP, ROW_SPAN), BF16),
        ),
        in_specs=[smem, smem, vmem, vmem],
        out_specs=(vmem, vmem),
        compiler_params=pltpu.CompilerParams(vmem_limit_bytes=LIMIT),
        name="row_matrices",
    )(kernel, low, turned, key)


def col_matrices_body(kernel_ref, cols_ref):
    begin, end = BLUR_BAND
    for e in range(cols_ref.shape[0]):
        high, rest = two_parts(
            toeplitz(kernel_ref, e, end - begin, BLUR_BLOCK, begin - LANES + RADIUS)
        )
        cols_ref[e, 0] = high
        cols_ref[e, 1] = rest


def make_col_matrices(kernels):
    return pl.pallas_call(
        col_matrices_body,
        out_shape=jax.ShapeDtypeStruct(
            (kernels.shape[0], 2, BLUR_BAND[1] - BLUR_BAND[0], BLUR_BLOCK), BF16
        ),
        in_specs=[pl.BlockSpec(memory_space=pltpu.SMEM)],
        out_specs=pl.BlockSpec(memory_space=pltpu.VMEM),
        compiler_params=pltpu.CompilerParams(vmem_limit_bytes=COL_LIMIT),
        name="col_matrices",
    )(kernels)


def row_body(slots, low_ref, num_ref, x_ref, rows_ref, blur_ref, turned_ref, key_ref, out_ref):
    extent = x_ref.shape[0]
    owner_rows = out_ref.shape[2]
    blocks = turned_ref.shape[0] // slots

    def times(matrix, start):
        first = pl.multiple_of(jnp.minimum(start, extent - ROW_STEP), 16)
        return halves_sum(dot(matrix, x_ref[pl.ds(first, ROW_STEP), :]))

    def block(at, carry):
        indices = [slot * blocks + at for slot in range(slots)]
        sums = [times(rows_ref[index], low_ref[index]) for index in indices]
        for slot, index in enumerate(indices):

            def more(i, total, index=index):
                start = low_ref[index] + i * ROW_STEP
                matrix = row_matrix(
                    blur_ref, turned_ref[index], key_ref[index], start, extent, True
                )
                return total + times(matrix, start)

            total = lax.fori_loop(1, num_ref[index], more, sums[slot]).astype(BF16)
            for owner in range(ROW_BLOCK // owner_rows):
                out_ref[at * (ROW_BLOCK // owner_rows) + owner, slot] = total[
                    owner * owner_rows : (owner + 1) * owner_rows
                ]
        return carry

    lax.fori_loop(0, blocks, block, 0)


def row_warp(x, low, num, matrices, blur, turned, key, slots, owners):
    width = x.shape[1]
    owner_rows = turned.shape[0] // slots * ROW_BLOCK // owners
    vmem = pl.BlockSpec(memory_space=pltpu.VMEM)
    smem = pl.BlockSpec(memory_space=pltpu.SMEM)
    return pl.pallas_call(
        functools.partial(row_body, slots),
        out_shape=jax.ShapeDtypeStruct((owners, slots, owner_rows, width), BF16),
        in_specs=[smem, smem] + [vmem] * 5,
        out_specs=vmem,
        compiler_params=pltpu.CompilerParams(vmem_limit_bytes=LIMIT),
        cost_estimate=pl.CostEstimate(
            flops=2_000_000_000, bytes_accessed=8 * 1024 * 1024, transcendentals=0
        ),
        name="row_warp",
    )(low, num, x, matrices, blur, turned, key)


def col_body(cols, count_ref, list_ref, low_ref, num_ref, from_ref, to_ref, weight_ref, z_hbm,
             blur_hbm, turned_hbm, key_hbm, out_ref, padded, blur, turned_ref, key_ref, blurred,
             held, z_sems, blur_sems, table_sems):
    slots, rows, width = z_hbm.shape[1:]
    sources = cols // width
    exposures = z_hbm.shape[0] // sources
    patch = pl.program_id(0)
    begin, end = BLUR_BAND

    @pl.when(patch == 0)
    def _():
        waits = []
        for e in range(exposures):
            copies = [
                pltpu.make_async_copy(
                    z_hbm.at[e * sources + s],
                    padded.at[e, :, :, pl.ds(LANES + s * width, width)],
                    z_sems.at[e, s],
                )
                for s in range(sources)
            ]
            copies.append(
                pltpu.make_async_copy(
                    blur_hbm.at[e], blur.at[e, :, pl.ds(begin, end - begin)], blur_sems.at[e]
                )
            )
            for copy in copies:
                copy.start()
            waits.append(copies)
        tables = [
            pltpu.make_async_copy(turned_hbm, turned_ref, table_sems.at[0]),
            pltpu.make_async_copy(key_hbm, key_ref, table_sems.at[1]),
        ]
        for copy in tables:
            copy.start()
        pad = jnp.zeros((slots, rows, LANES), BF16)
        for e in range(exposures):
            padded[e, :, :, 0:LANES] = pad
            padded[e, :, :, LANES + cols : 2 * LANES + cols] = pad
            for n in range(2):
                blur[e, n, 0:begin] = jnp.zeros((begin, BLUR_BLOCK), BF16)
                blur[e, n, end:BLUR_STEP] = jnp.zeros((BLUR_STEP - end, BLUR_BLOCK), BF16)
            for j in range(slots):
                blurred[e * slots + j, :, cols : cols + COL_STEP] = jnp.zeros(
                    (2 * rows, COL_STEP), BF16
                )
        for e in range(exposures):
            for copy in waits[e]:
                copy.wait()
            windows = jnp.concatenate(
                [
                    padded[e, :, :, b * BLUR_BLOCK : b * BLUR_BLOCK + BLUR_STEP].reshape(
                        slots * rows, BLUR_STEP
                    )
                    for b in range(cols // BLUR_BLOCK)
                ],
                axis=0,
            )
            high, rest = two_parts(dot(windows, blur[e, 0]) + dot(windows, blur[e, 1]))
            for b in range(cols // BLUR_BLOCK):
                for j in range(slots):
                    at = (b * slots + j) * rows
                    span = slice(b * BLUR_BLOCK, (b + 1) * BLUR_BLOCK)
                    blurred[e * slots + j, 0:rows, span] = high[at : at + rows]
                    blurred[e * slots + j, rows : 2 * rows, span] = rest[at : at + rows]
        for copy in tables:
            copy.wait()

    held[...] = jnp.zeros(held.shape, F32)

    blocks = turned_ref.shape[1]

    def part(slot, b, n):
        first = pl.multiple_of(jnp.minimum(low_ref[slot, b] + n * COL_STEP, cols), LANES)
        band = band_of(turned_ref[slot, b], key_ref[slot, b], first, COL_STEP // 8)
        band = jnp.concatenate(band, axis=0).astype(BF16)
        return halves_sum(dot(blurred[slot, :, pl.ds(first, COL_STEP)], band))

    def add_slot(i, carry):
        slot = list_ref[patch, i]
        begin, end = from_ref[slot], to_ref[slot]

        def add_group(c, carry):
            at = begin + c * COL_GROUP
            spots = [jnp.minimum(at + h, blocks - 1) for h in range(COL_GROUP)]
            weights = [jnp.where(at + h < end, weight_ref[slot], 0.0) for h in range(COL_GROUP)]

            def add_parts(n):
                sums = [part(slot, b, n) for b in spots]
                for b, weight, total in zip(spots, weights, sums):
                    span = pl.ds(pl.multiple_of(b * COL_BLOCK, COL_BLOCK), COL_BLOCK)
                    held[:, span] += weight * total

            add_parts(0)
            most = num_ref[slot, spots[0]]
            for b in spots[1:]:
                most = jnp.maximum(most, num_ref[slot, b])

            def more(n, carry):
                add_parts(n)
                return carry

            lax.fori_loop(1, most, more, 0)
            return carry

        steps = (end - begin + COL_GROUP - 1) // COL_GROUP
        return lax.fori_loop(0, steps, add_group, carry)

    lax.fori_loop(0, count_ref[patch], add_slot, 0)
    own_cols = out_ref.shape[3]
    for owner in range(out_ref.shape[1]):
        out_ref[0, owner] = held[:, owner * own_cols : (owner + 1) * own_cols].astype(BF16)


def col_warp(z, count, listed, low, num, begin, end, weight, blur, turned, key, cols, patches,
             owners):
    slots, rows, width = z.shape[1:]
    slot_total, blocks = turned.shape[:2]
    exposures = blur.shape[0]
    own_cols = blocks * COL_BLOCK // owners
    smem = pl.BlockSpec(memory_space=pltpu.SMEM)
    return pl.pallas_call(
        functools.partial(col_body, cols),
        out_shape=jax.ShapeDtypeStruct((patches, owners, rows, own_cols), BF16),
        grid=(patches,),
        in_specs=[smem] * 7 + [pl.BlockSpec(memory_space=pl.ANY)] * 4,
        out_specs=pl.BlockSpec((1, owners, rows, own_cols), lambda k: (k, 0, 0, 0)),
        scratch_shapes=[
            pltpu.VMEM((exposures, slots, rows, cols + 2 * LANES), BF16),
            pltpu.VMEM((exposures, 2, BLUR_STEP, BLUR_BLOCK), BF16),
            pltpu.VMEM(turned.shape, F32),
            pltpu.VMEM(key.shape, jnp.int32),
            pltpu.VMEM((slot_total, 2 * rows, cols + COL_STEP), BF16),
            pltpu.VMEM((rows, owners * own_cols), F32),
            pltpu.SemaphoreType.DMA((exposures, cols // width)),
            pltpu.SemaphoreType.DMA((exposures,)),
            pltpu.SemaphoreType.DMA((2,)),
        ],
        compiler_params=pltpu.CompilerParams(
            dimension_semantics=("arbitrary",), vmem_limit_bytes=COL_LIMIT
        ),
        cost_estimate=pl.CostEstimate(
            flops=8_000_000_000, bytes_accessed=16 * 1024 * 1024, transcendentals=0
        ),
        name="col_warp",
    )(count, listed, low, num, begin, end, weight, z, blur, turned, key)


def split_body(parts, image_ref, out_ref, sems):
    width = out_ref.shape[2]
    copies = [
        pltpu.make_async_copy(
            image_ref.at[at // parts, :, pl.ds(at % parts * width, width)],
            out_ref.at[at],
            sems.at[at],
        )
        for at in range(out_ref.shape[0])
    ]
    for copy in copies:
        copy.start()
    for copy in copies:
        copy.wait()


def split_columns(image, parts):
    exposures, height, width = image.shape
    total = exposures * parts
    return pl.pallas_call(
        functools.partial(split_body, parts),
        out_shape=jax.ShapeDtypeStruct((total, height, width // parts), image.dtype),
        in_specs=[pl.BlockSpec(memory_space=pl.ANY)],
        out_specs=pl.BlockSpec(memory_space=pltpu.VMEM),
        scratch_shapes=[pltpu.SemaphoreType.DMA((total,))],
        compiler_params=pltpu.CompilerParams(vmem_limit_bytes=LIMIT),
        name="split_columns",
    )(image)


def ring_sum(x, axis, count, stride):
    size = lax.axis_size(axis)
    total = x
    for step in range(1, count):
        pairs = []
        for i in range(size):
            at = i // stride % count
            pairs.append((i, i + ((at + step) % count - at) * stride))
        total = total + lax.ppermute(x, axis, pairs)
    return total


def butterfly_sum(x, axis):
    size = lax.axis_size(axis)
    step = 1
    while step < size:
        x = x + lax.ppermute(x, axis, [(i, i ^ step) for i in range(size)])
        step *= 2
    return x


def local(image, variance, psf_coef, correlations, row_start, row_frac, col_start, col_frac):
    exp_dev, height, width = image.shape
    exposures, slots = correlations.shape
    patch_rows = row_start.shape[2]
    patch_cols = col_start.shape[2]
    cores = lax.axis_size("core")
    visits = lax.axis_size("y") * cores
    regions = lax.axis_size("region")
    extent = height * regions
    parts = regions // exp_dev
    part_cols = width // parts
    own_cols = patch_cols // regions
    pair_at = lax.axis_index("y")
    core_at = lax.axis_index("core")
    visit_at = pair_at * cores + core_at
    region_at = lax.axis_index("region")

    def exchange(x, axis):
        return lax.all_to_all(x, axis, split_axis=0, concat_axis=0, tiled=True)

    columns = exchange(split_columns(image, parts), "region").reshape(extent, part_cols)

    kernels = psf_kernel(psf_coef)

    own_exp = region_at // parts
    at_exp = visit_at * exp_dev + own_exp
    blocks = slots * patch_rows // ROW_BLOCK
    starts = lax.dynamic_index_in_dim(row_start, at_exp, 0, keepdims=False)
    fracs = lax.dynamic_index_in_dim(row_frac, at_exp, 0, keepdims=False)
    starts = starts.reshape(blocks, ROW_BLOCK)
    row_turned, row_key = band_tables(starts, lanczos_taps(fracs.reshape(blocks, ROW_BLOCK)))
    row_low = jnp.clip(starts[:, 0] - RADIUS, 0, extent - ROW_STEP) // 16 * 16
    row_end = jnp.minimum(starts[:, -1] + TAPS + RADIUS, extent)
    row_num = jnp.maximum(row_end - row_low + ROW_STEP - 1, 0) // ROW_STEP
    row_matrices, row_blur = make_row_matrices(
        lax.dynamic_slice_in_dim(kernels, own_exp, 1, 0), row_low, row_turned, row_key, extent
    )

    variance, psf_tile, row_matrices = lax.optimization_barrier(
        (
            variance,
            jnp.zeros((8, LANES), F32).at[:exp_dev, : 2 * RADIUS + 1].set(kernels),
            row_matrices,
        )
    )
    other = lax.ppermute(psf_tile, "core", [(i, i ^ 1) for i in range(cores)])
    other = other[:exp_dev, : 2 * RADIUS + 1]
    col_blur = make_col_matrices(
        jnp.concatenate(
            [jnp.where(core_at == 0, kernels, other), jnp.where(core_at == 0, other, kernels)]
        )
    )
    local_sums = jnp.sum(variance.astype(F32), axis=(1, 2))
    tile = jnp.zeros((8, LANES), F32).at[0, :exp_dev].set(local_sums)
    inner = 4
    tile = ring_sum(tile, "region", inner, 1)
    tile = ring_sum(tile, "region", regions // inner, inner)
    pair_exp = cores * exp_dev
    first_exp = pair_at * pair_exp

    slot_total = pair_exp * slots
    col_blocks = patch_cols // COL_BLOCK
    own_starts = lax.dynamic_slice_in_dim(col_start, first_exp, pair_exp, 0)
    own_fracs = lax.dynamic_slice_in_dim(col_frac, first_exp, pair_exp, 0)
    own_starts = own_starts.reshape(slot_total, col_blocks, COL_BLOCK)
    own_fracs = own_fracs.reshape(slot_total, col_blocks, COL_BLOCK)
    col_turned, col_key = band_tables(own_starts, lanczos_taps(own_fracs))
    col_low = jnp.clip(own_starts[:, :, 0], 0, width) // LANES * LANES
    col_end = jnp.minimum(own_starts[:, :, -1] + TAPS, width)
    col_num = jnp.maximum(col_end - col_low + COL_STEP - 1, 0) // COL_STEP
    block_at = jnp.arange(col_blocks, dtype=jnp.int32)
    col_from = jnp.min(jnp.where(col_num > 0, block_at, col_blocks), axis=1)
    col_to = jnp.max(jnp.where(col_num > 0, block_at + 1, 0), axis=1)
    col_from = jnp.minimum(col_from, col_to)
    owners = lax.dynamic_slice_in_dim(correlations, first_exp, pair_exp, 0).reshape(slot_total)
    named = owners == jnp.arange(visits, dtype=jnp.int32)[:, None]
    named = named.astype(jnp.int32)
    count = jnp.sum(named, axis=1)
    slot_ids = jnp.arange(slot_total, dtype=jnp.int32)
    rank = jnp.sum(jnp.where(slot_ids[:, None] < slot_ids, named[:, :, None], 0), axis=1)
    listed = jnp.sum(
        jnp.where((named[:, None, :] > 0) & (rank[:, None, :] == slot_ids[:, None]), slot_ids, 0),
        axis=2,
    )

    warped = row_warp(
        columns, row_low, row_num, row_matrices, row_blur, row_turned, row_key, slots,
        cores * regions,
    )
    tile, warped = lax.optimization_barrier((tile, warped))
    rows = exchange(warped, ("core", "region"))
    at_visit = lax.broadcasted_iota(jnp.int32, (8, LANES), 0) == visit_at
    tile = jnp.where(at_visit, tile[0:1], 0.0)
    tile = butterfly_sum(tile, "core")
    pair_sums = lax.dynamic_slice_in_dim(tile, pair_at * cores, cores, 0)[:, :exp_dev]
    slot_weight = jnp.repeat(1.0 / (pair_sums.reshape(pair_exp) / (extent * width)), slots)
    tile = butterfly_sum(tile, "y")
    weight = 1.0 / (tile[:visits, :exp_dev].reshape(exposures) / (extent * width))
    mean_weight = jnp.mean(weight)
    partial = col_warp(
        rows, count, listed, col_low, col_num, col_from, col_to, slot_weight, col_blur,
        col_turned, col_key, width, visits, regions,
    )
    pieces = exchange(
        partial.reshape((visits * regions,) + partial.shape[2:]), ("y", "core", "region")
    )
    summed = jnp.sum(
        pieces.reshape(visits // cores, patch_rows, own_cols).astype(F32), axis=0, keepdims=True
    )

    total_slots = exposures * slots
    row_cover = coverage(
        row_start.reshape(total_slots, patch_rows),
        lanczos_taps(row_frac.reshape(total_slots, patch_rows)),
        extent,
    )
    at = region_at * own_cols
    col_cover = coverage(
        lax.dynamic_slice_in_dim(col_start, at, own_cols, 2).reshape(total_slots, own_cols),
        lanczos_taps(
            lax.dynamic_slice_in_dim(col_frac, at, own_cols, 2).reshape(total_slots, own_cols)
        ),
        width,
    )
    scale = jnp.where(
        correlations.reshape(total_slots) == visit_at, jnp.repeat(weight, slots), 0.0
    )
    weight_map = lax.dot_general(
        row_cover,
        col_cover * scale[:, None],
        (((0,), (0,)), ((), ())),
        precision=lax.Precision.HIGHEST,
        preferred_element_type=F32,
    ).reshape(1, patch_rows, own_cols)
    coadd = summed / jnp.maximum(weight_map, FLOOR_SHARE * mean_weight)
    return coadd, weight_map


def solution(mesh):
    visits, regions = mesh.devices.shape
    split = jax.sharding.Mesh(
        mesh.devices.reshape(visits // 2, 2, regions), ("y", "core", "region")
    )
    visit = ("y", "core")
    placed = (
        P(visit, "region", None),
        P(visit, "region", None),
        P(visit, None),
        P(),
        P(),
        P(),
        P(),
        P(),
    )
    return jax.shard_map(
        local,
        mesh=split,
        in_specs=placed,
        out_specs=(P(visit, None, "region"), P(visit, None, "region")),
        check_vma=False,
    )
```

```python
import functools
import math

import jax
import jax.numpy as jnp
from jax import lax
from jax.experimental import pallas as pl
from jax.experimental.pallas import tpu as pltpu
from jax.sharding import PartitionSpec as P

RADIUS = 10
TAPS = 6
SIGMAS = (1.0, 2.0, 4.0)
FLOOR_SHARE = 0.5
BF16 = jnp.bfloat16
F32 = jnp.float32

ROW_BLOCK = 128
ROW_STEP = 256
ROW_SPAN = 288
COL_BLOCK = 128
COL_STEP = 256
COL_GROUP = 18
BLUR_BLOCK = 256
BLUR_STEP = 512
BLUR_BAND = (112, 400)
LANES = 128
TAIL = 16
LIMIT = 14 * 1024 * 1024
COL_LIMIT = 56 * 1024 * 1024


def psf_kernel(coefficient):
    offsets = jnp.arange(-RADIUS, RADIUS + 1).astype(coefficient.dtype)
    sigmas = jnp.array(SIGMAS, dtype=coefficient.dtype)
    gaussians = jnp.exp(
        -(offsets[None, :] * offsets[None, :]) / (2.0 * sigmas[:, None] * sigmas[:, None])
    )
    kernel = jnp.sum(coefficient[:, :, None] * gaussians[None, :, :], axis=1)
    return kernel / jnp.sum(kernel, axis=1, keepdims=True)


def lanczos_taps(f):
    g = 1.0 - f
    third = math.pi / 3.0
    tiny = 1e-6
    a = jnp.sin(third * f)
    b = jnp.sin(third * g)
    c = a + b
    fg = f * g
    a_over_f = jnp.where(f < tiny, third, a / jnp.maximum(f, tiny))
    b_over_g = jnp.where(g < tiny, third, b / jnp.maximum(g, tiny))
    values = [
        b * fg / ((f + 2.0) * (f + 2.0)),
        -c * fg / ((f + 1.0) * (f + 1.0)),
        a_over_f * g,
        b_over_g * f,
        -c * fg / ((2.0 - f) * (2.0 - f)),
        a * fg / ((3.0 - f) * (3.0 - f)),
    ]
    total = functools.reduce(jnp.add, values)
    return [lax.reduce_precision(value / total, 8, 7) for value in values]


def coverage(starts, taps, extent):
    running = jnp.zeros(starts.shape, F32)
    for tap_at, tap in enumerate(taps):
        position = starts + tap_at
        inside = (position >= 0) & (position < extent)
        running = running + jnp.where(inside, tap, 0.0)
    return running


def band_tables(starts, taps):
    place = jnp.arange(8, dtype=jnp.int32)[:, None]
    diff = place - starts[..., None, :]
    at = diff & 7
    turned = jnp.zeros(diff.shape, F32)
    for tap_at, tap in enumerate(taps):
        turned = turned + jnp.where(at == tap_at, tap[..., None, :], 0.0)
    return turned, diff - at


def toeplitz(kernel_ref, at, rows, cols, shift):
    diff = (
        lax.broadcasted_iota(jnp.int32, (rows, cols), 0)
        - lax.broadcasted_iota(jnp.int32, (rows, cols), 1)
    )
    full = jnp.zeros((rows, cols), F32)
    for tap_at in range(2 * RADIUS + 1):
        full = jnp.where(diff == tap_at - shift, kernel_ref[at, tap_at], full)
    return full


def dot(a, b):
    return jnp.dot(a, b, preferred_element_type=F32)


def two_parts(value):
    high = value.astype(BF16)
    return high, (value - high.astype(F32)).astype(BF16)


def halves_sum(value):
    half = value.shape[0] // 2
    return value[:half] + value[half:]


def band_of(turned, key, first, groups):
    moved = key + first
    return [jnp.where(moved == -8 * g, turned, 0.0) for g in range(groups)]


def row_matrix(blur_ref, turned, key, start, extent, masked):
    last = extent - ROW_STEP
    first = jnp.minimum(start, last)
    groups = ROW_SPAN // 8
    pieces = band_of(turned, key, first - 16, groups)
    for g in range(2):
        pieces[g] = jnp.where(first > 0, pieces[g], 0.0)
        pieces[groups - 1 - g] = jnp.where(first < last, pieces[groups - 1 - g], 0.0)
    band = jnp.concatenate(pieces, axis=0).astype(BF16)
    both = halves_sum(dot(blur_ref[...], band))
    if masked:
        row = lax.broadcasted_iota(jnp.int32, both.shape, 0) + first
        both = jnp.where(row >= start, both, 0.0)
    return jnp.concatenate(two_parts(both.T), axis=0)


def row_matrices_body(extent, kernel_ref, low_ref, turned_ref, key_ref, rows_ref, blur_ref):
    high, rest = two_parts(toeplitz(kernel_ref, 0, ROW_STEP, ROW_SPAN, 16 + RADIUS))
    blur_ref[0:ROW_STEP] = high
    blur_ref[ROW_STEP : 2 * ROW_STEP] = rest

    def block(at, carry):
        rows_ref[at] = row_matrix(
            blur_ref, turned_ref[at], key_ref[at], low_ref[at], extent, False
        )
        return carry

    lax.fori_loop(0, turned_ref.shape[0], block, 0)


def make_row_matrices(kernel, low, turned, key, extent):
    blocks = turned.shape[0]
    vmem = pl.BlockSpec(memory_space=pltpu.VMEM)
    smem = pl.BlockSpec(memory_space=pltpu.SMEM)
    return pl.pallas_call(
        functools.partial(row_matrices_body, extent),
        out_shape=(
            jax.ShapeDtypeStruct((blocks, 2 * ROW_BLOCK, ROW_STEP), BF16),
            jax.ShapeDtypeStruct((2 * ROW_STEP, ROW_SPAN), BF16),
        ),
        in_specs=[smem, smem, vmem, vmem],
        out_specs=(vmem, vmem),
        compiler_params=pltpu.CompilerParams(vmem_limit_bytes=LIMIT),
        name="row_matrices",
    )(kernel, low, turned, key)


def col_matrices_body(kernel_ref, cols_ref):
    begin, end = BLUR_BAND
    for e in range(cols_ref.shape[0]):
        high, rest = two_parts(
            toeplitz(kernel_ref, e, end - begin, BLUR_BLOCK, begin - LANES + RADIUS)
        )
        cols_ref[e, 0] = high
        cols_ref[e, 1] = rest


def make_col_matrices(kernels):
    return pl.pallas_call(
        col_matrices_body,
        out_shape=jax.ShapeDtypeStruct(
            (kernels.shape[0], 2, BLUR_BAND[1] - BLUR_BAND[0], BLUR_BLOCK), BF16
        ),
        in_specs=[pl.BlockSpec(memory_space=pltpu.SMEM)],
        out_specs=pl.BlockSpec(memory_space=pltpu.VMEM),
        compiler_params=pltpu.CompilerParams(vmem_limit_bytes=COL_LIMIT),
        name="col_matrices",
    )(kernels)


def row_body(slots, low_ref, num_ref, x_ref, rows_ref, blur_ref, turned_ref, key_ref, tail_ref,
             out_ref):
    extent, width = x_ref.shape
    owners = out_ref.shape[0]
    blocks = turned_ref.shape[0] // slots
    owner_rows = blocks * ROW_BLOCK // owners
    data_rows = out_ref.shape[1] - TAIL
    for owner in range(owners):
        out_ref[owner, data_rows : data_rows + TAIL, :] = tail_ref[...]

    def times(matrix, start):
        first = pl.multiple_of(jnp.minimum(start, extent - ROW_STEP), 16)
        return halves_sum(dot(matrix, x_ref[pl.ds(first, ROW_STEP), :]))

    def block(at, carry):
        indices = [slot * blocks + at for slot in range(slots)]
        sums = [times(rows_ref[index], low_ref[index]) for index in indices]
        for slot, index in enumerate(indices):

            def more(i, total, index=index):
                start = low_ref[index] + i * ROW_STEP
                matrix = row_matrix(
                    blur_ref, turned_ref[index], key_ref[index], start, extent, True
                )
                return total + times(matrix, start)

            total = lax.fori_loop(1, num_ref[index], more, sums[slot]).astype(BF16)
            for owner in range(ROW_BLOCK // owner_rows):
                for t in range(width // LANES):
                    place = (t * slots + slot) * owner_rows
                    out_ref[
                        at * (ROW_BLOCK // owner_rows) + owner, place : place + owner_rows, :
                    ] = total[
                        owner * owner_rows : (owner + 1) * owner_rows,
                        t * LANES : (t + 1) * LANES,
                    ]
        return carry

    lax.fori_loop(0, blocks, block, 0)


def row_warp(x, low, num, matrices, blur, turned, key, tail, slots, owners):
    width = x.shape[1]
    owner_rows = turned.shape[0] // slots * ROW_BLOCK // owners
    vmem = pl.BlockSpec(memory_space=pltpu.VMEM)
    smem = pl.BlockSpec(memory_space=pltpu.SMEM)
    return pl.pallas_call(
        functools.partial(row_body, slots),
        out_shape=jax.ShapeDtypeStruct(
            (owners, width // LANES * slots * owner_rows + TAIL, LANES), BF16
        ),
        in_specs=[smem, smem] + [vmem] * 6,
        out_specs=vmem,
        compiler_params=pltpu.CompilerParams(vmem_limit_bytes=LIMIT),
        cost_estimate=pl.CostEstimate(
            flops=2_000_000_000, bytes_accessed=8 * 1024 * 1024, transcendentals=0
        ),
        name="row_warp",
    )(low, num, x, matrices, blur, turned, key, tail)


def col_body(cols, slots, pixels, count_ref, list_ref, low_ref, num_ref, from_ref, to_ref, z_hbm,
             blur_hbm, turned_hbm, key_hbm, out_ref, padded, blur, turned_ref, key_ref, tails,
             blurred, held, weight_ref, z_sems, blur_sems, table_sems):
    data_rows = z_hbm.shape[1] - TAIL
    exposures = blur_hbm.shape[0]
    sources = z_hbm.shape[0] // exposures
    tile_rows = data_rows // (cols // sources // LANES)
    rows = tile_rows // slots
    patch = pl.program_id(0)
    begin, end = BLUR_BAND

    @pl.when(patch == 0)
    def _():
        waits = []
        for e in range(exposures):
            copies = [
                pltpu.make_async_copy(
                    z_hbm.at[e * sources + s, pl.ds(0, data_rows)],
                    padded.at[e, pl.ds(tile_rows + s * data_rows, data_rows)],
                    z_sems.at[e, s],
                )
                for s in range(sources)
            ]
            copies.append(
                pltpu.make_async_copy(
                    blur_hbm.at[e], blur.at[e, :, pl.ds(begin, end - begin)], blur_sems.at[e]
                )
            )
            for copy in copies:
                copy.start()
            waits.append(copies)
        tables = [
            pltpu.make_async_copy(turned_hbm, turned_ref, table_sems.at[0]),
            pltpu.make_async_copy(key_hbm, key_ref, table_sems.at[1]),
            pltpu.make_async_copy(
                z_hbm.at[:, pl.ds(data_rows, TAIL)], tails, table_sems.at[2]
            ),
        ]
        for copy in tables:
            copy.start()
        pad = jnp.zeros((tile_rows, LANES), BF16)
        last = padded.shape[1] - tile_rows
        for e in range(exposures):
            padded[e, 0:tile_rows] = pad
            padded[e, last : last + tile_rows] = pad
            for n in range(2):
                blur[e, n, 0:begin] = jnp.zeros((begin, BLUR_BLOCK), BF16)
                blur[e, n, end:BLUR_STEP] = jnp.zeros((BLUR_STEP - end, BLUR_BLOCK), BF16)
            for j in range(slots):
                blurred[e * slots + j, :, cols : cols + COL_STEP] = jnp.zeros(
                    (2 * rows, COL_STEP), BF16
                )
        for e in range(exposures):
            for copy in waits[e]:
                copy.wait()
            windows = jnp.concatenate(
                [
                    jnp.concatenate(
                        [
                            padded[e, t * tile_rows : (t + 1) * tile_rows]
                            for t in range(
                                b * BLUR_BLOCK // LANES, (b * BLUR_BLOCK + BLUR_STEP) // LANES
                            )
                        ],
                        axis=1,
                    )
                    for b in range(cols // BLUR_BLOCK)
                ],
                axis=0,
            )
            high, rest = two_parts(dot(windows, blur[e, 0]) + dot(windows, blur[e, 1]))
            for b in range(cols // BLUR_BLOCK):
                for j in range(slots):
                    at = (b * slots + j) * rows
                    span = slice(b * BLUR_BLOCK, (b + 1) * BLUR_BLOCK)
                    blurred[e * slots + j, 0:rows, span] = high[at : at + rows]
                    blurred[e * slots + j, rows : 2 * rows, span] = rest[at : at + rows]
        for copy in tables:
            copy.wait()
        sums = jnp.sum(tails[...].astype(F32), axis=1)
        cores = 2
        visit_exp = exposures // cores
        lane = lax.broadcasted_iota(jnp.int32, (1, LANES), 1)
        for core in range(cores):
            per_core = sums.shape[0] // cores
            total = jnp.sum(
                sums[core * per_core : (core + 1) * per_core], axis=0, keepdims=True
            )
            for e in range(visit_exp):
                variance = jnp.sum(
                    jnp.where((lane < 3 * visit_exp) & (lane % visit_exp == e), total, 0.0)
                )
                for j in range(slots):
                    weight_ref[(core * visit_exp + e) * slots + j] = 1.0 / (variance / pixels)

    held[...] = jnp.zeros(held.shape, F32)

    blocks = turned_ref.shape[1]

    def part(slot, b, n):
        first = pl.multiple_of(jnp.minimum(low_ref[slot, b] + n * COL_STEP, cols), LANES)
        band = band_of(turned_ref[slot, b], key_ref[slot, b], first, COL_STEP // 8)
        band = jnp.concatenate(band, axis=0).astype(BF16)
        return halves_sum(dot(blurred[slot, :, pl.ds(first, COL_STEP)], band))

    def add_slot(i, carry):
        slot = list_ref[patch, i]
        begin, end = from_ref[slot], to_ref[slot]

        def add_group(c, carry):
            at = begin + c * COL_GROUP
            spots = [jnp.minimum(at + h, blocks - 1) for h in range(COL_GROUP)]
            weights = [jnp.where(at + h < end, weight_ref[slot], 0.0) for h in range(COL_GROUP)]

            def add_parts(n):
                sums = [part(slot, b, n) for b in spots]
                for b, weight, total in zip(spots, weights, sums):
                    span = pl.ds(pl.multiple_of(b * COL_BLOCK, COL_BLOCK), COL_BLOCK)
                    held[:, span] += weight * total

            add_parts(0)
            most = num_ref[slot, spots[0]]
            for b in spots[1:]:
                most = jnp.maximum(most, num_ref[slot, b])

            def more(n, carry):
                add_parts(n)
                return carry

            lax.fori_loop(1, most, more, 0)
            return carry

        steps = (end - begin + COL_GROUP - 1) // COL_GROUP
        return lax.fori_loop(0, steps, add_group, carry)

    lax.fori_loop(0, count_ref[patch], add_slot, 0)
    own_cols = out_ref.shape[3]
    for owner in range(out_ref.shape[1]):
        out_ref[0, owner] = held[:, owner * own_cols : (owner + 1) * own_cols].astype(BF16)


def col_warp(z, count, listed, low, num, begin, end, blur, turned, key, cols, slots, patches,
             owners, pixels):
    slot_total, blocks = turned.shape[:2]
    exposures = blur.shape[0]
    sources = z.shape[0] // exposures
    tile_rows = (z.shape[1] - TAIL) // (cols // sources // LANES)
    rows = tile_rows // slots
    own_cols = blocks * COL_BLOCK // owners
    smem = pl.BlockSpec(memory_space=pltpu.SMEM)
    return pl.pallas_call(
        functools.partial(col_body, cols, slots, pixels),
        out_shape=jax.ShapeDtypeStruct((patches, owners, rows, own_cols), BF16),
        grid=(patches,),
        in_specs=[smem] * 6 + [pl.BlockSpec(memory_space=pl.ANY)] * 4,
        out_specs=pl.BlockSpec((1, owners, rows, own_cols), lambda k: (k, 0, 0, 0)),
        scratch_shapes=[
            pltpu.VMEM((exposures, (cols // LANES + 2) * tile_rows, LANES), BF16),
            pltpu.VMEM((exposures, 2, BLUR_STEP, BLUR_BLOCK), BF16),
            pltpu.VMEM(turned.shape, F32),
            pltpu.VMEM(key.shape, jnp.int32),
            pltpu.VMEM((z.shape[0], TAIL, LANES), BF16),
            pltpu.VMEM((slot_total, 2 * rows, cols + COL_STEP), BF16),
            pltpu.VMEM((rows, owners * own_cols), F32),
            pltpu.SMEM((slot_total,), F32),
            pltpu.SemaphoreType.DMA((exposures, sources)),
            pltpu.SemaphoreType.DMA((exposures,)),
            pltpu.SemaphoreType.DMA((3,)),
        ],
        compiler_params=pltpu.CompilerParams(
            dimension_semantics=("arbitrary",), vmem_limit_bytes=COL_LIMIT
        ),
        cost_estimate=pl.CostEstimate(
            flops=8_000_000_000, bytes_accessed=16 * 1024 * 1024, transcendentals=0
        ),
        name="col_warp",
    )(count, listed, low, num, begin, end, z, blur, turned, key)


def split_body(parts, image_ref, out_ref, held, in_sems, out_sems):
    total, _, width = out_ref.shape
    reads = [
        pltpu.make_async_copy(
            image_ref.at[at // parts, :, pl.ds(at % parts * width, width)],
            held.at[at],
            in_sems.at[at],
        )
        for at in range(total)
    ]
    writes = [
        pltpu.make_async_copy(held.at[at], out_ref.at[at], out_sems.at[at])
        for at in range(total)
    ]
    for read in reads:
        read.start()
    for read, write in zip(reads, writes):
        read.wait()
        write.start()
    for write in writes:
        write.wait()


def split_columns(image, parts):
    exposures, height, width = image.shape
    total = exposures * parts
    shape = (total, height, width // parts)
    return pl.pallas_call(
        functools.partial(split_body, parts),
        out_shape=jax.ShapeDtypeStruct(shape, image.dtype),
        in_specs=[pl.BlockSpec(memory_space=pl.ANY)],
        out_specs=pl.BlockSpec(memory_space=pl.ANY),
        scratch_shapes=[
            pltpu.VMEM(shape, image.dtype),
            pltpu.SemaphoreType.DMA((total,)),
            pltpu.SemaphoreType.DMA((total,)),
        ],
        compiler_params=pltpu.CompilerParams(vmem_limit_bytes=COL_LIMIT),
        name="split_columns",
    )(image)


def butterfly_sum(x, axis):
    size = lax.axis_size(axis)
    step = 1
    while step < size:
        x = x + lax.ppermute(x, axis, [(i, i ^ step) for i in range(size)])
        step *= 2
    return x


def local(image, variance, psf_coef, correlations, row_start, row_frac, col_start, col_frac):
    exp_dev, height, width = image.shape
    exposures, slots = correlations.shape
    patch_rows = row_start.shape[2]
    patch_cols = col_start.shape[2]
    cores = lax.axis_size("core")
    visits = lax.axis_size("y") * cores
    regions = lax.axis_size("region")
    extent = height * regions
    parts = regions // exp_dev
    part_cols = width // parts
    own_cols = patch_cols // regions
    pair_at = lax.axis_index("y")
    core_at = lax.axis_index("core")
    visit_at = pair_at * cores + core_at
    region_at = lax.axis_index("region")

    def exchange(x, axis):
        return lax.all_to_all(x, axis, split_axis=0, concat_axis=0, tiled=True)

    sent = split_columns(image, parts)
    (sent, variance, psf_coef, row_start, row_frac, col_start, col_frac) = lax.optimization_barrier(
        (sent, variance, psf_coef, row_start, row_frac, col_start, col_frac)
    )
    columns = exchange(sent, "region").reshape(extent, part_cols)

    kernels = psf_kernel(psf_coef)

    own_exp = region_at // parts
    at_exp = visit_at * exp_dev + own_exp
    blocks = slots * patch_rows // ROW_BLOCK
    starts = lax.dynamic_index_in_dim(row_start, at_exp, 0, keepdims=False)
    fracs = lax.dynamic_index_in_dim(row_frac, at_exp, 0, keepdims=False)
    starts = starts.reshape(blocks, ROW_BLOCK)
    row_turned, row_key = band_tables(starts, lanczos_taps(fracs.reshape(blocks, ROW_BLOCK)))
    row_low = jnp.clip(starts[:, 0] - RADIUS, 0, extent - ROW_STEP) // 16 * 16
    row_end = jnp.minimum(starts[:, -1] + TAPS + RADIUS, extent)
    row_num = jnp.maximum(row_end - row_low + ROW_STEP - 1, 0) // ROW_STEP
    row_matrices, row_blur = make_row_matrices(
        lax.dynamic_slice_in_dim(kernels, own_exp, 1, 0), row_low, row_turned, row_key, extent
    )

    rest = jnp.sum(variance.astype(F32), axis=(1, 2))
    sum_parts = []
    for _ in range(3):
        sum_parts.append(lax.reduce_precision(rest, 8, 7))
        rest = rest - sum_parts[-1]
    tail = jnp.zeros((TAIL, LANES), F32).at[0, : 3 * exp_dev].set(jnp.concatenate(sum_parts))
    tail = tail.astype(BF16)
    pair_exp = cores * exp_dev
    first_exp = pair_at * pair_exp

    slot_total = pair_exp * slots
    col_blocks = patch_cols // COL_BLOCK
    own_starts = lax.dynamic_slice_in_dim(col_start, first_exp, pair_exp, 0)
    own_fracs = lax.dynamic_slice_in_dim(col_frac, first_exp, pair_exp, 0)
    own_starts = own_starts.reshape(slot_total, col_blocks, COL_BLOCK)
    own_fracs = own_fracs.reshape(slot_total, col_blocks, COL_BLOCK)
    col_turned, col_key = band_tables(own_starts, lanczos_taps(own_fracs))
    col_low = jnp.clip(own_starts[:, :, 0], 0, width) // LANES * LANES
    col_end = jnp.minimum(own_starts[:, :, -1] + TAPS, width)
    col_num = jnp.maximum(col_end - col_low + COL_STEP - 1, 0) // COL_STEP
    block_at = jnp.arange(col_blocks, dtype=jnp.int32)
    col_from = jnp.min(jnp.where(col_num > 0, block_at, col_blocks), axis=1)
    col_to = jnp.max(jnp.where(col_num > 0, block_at + 1, 0), axis=1)
    col_from = jnp.minimum(col_from, col_to)
    owners = lax.dynamic_slice_in_dim(correlations, first_exp, pair_exp, 0).reshape(slot_total)
    named = owners == jnp.arange(visits, dtype=jnp.int32)[:, None]
    named = named.astype(jnp.int32)
    count = jnp.sum(named, axis=1)
    slot_ids = jnp.arange(slot_total, dtype=jnp.int32)
    rank = jnp.sum(jnp.where(slot_ids[:, None] < slot_ids, named[:, :, None], 0), axis=1)
    listed = jnp.sum(
        jnp.where((named[:, None, :] > 0) & (rank[:, None, :] == slot_ids[:, None]), slot_ids, 0),
        axis=2,
    )

    warped = row_warp(
        columns, row_low, row_num, row_matrices, row_blur, row_turned, row_key, tail, slots,
        cores * regions,
    )
    psf_tile = jnp.zeros((8, LANES), F32).at[:exp_dev, : 2 * RADIUS + 1].set(kernels)
    psf_tile, warped = lax.optimization_barrier((psf_tile, warped))
    rows = exchange(warped, ("core", "region"))
    other = lax.ppermute(psf_tile, "core", [(i, i ^ 1) for i in range(cores)])
    other = other[:exp_dev, : 2 * RADIUS + 1]
    col_blur = make_col_matrices(
        jnp.concatenate(
            [jnp.where(core_at == 0, kernels, other), jnp.where(core_at == 0, other, kernels)]
        )
    )
    partial = col_warp(
        rows, count, listed, col_low, col_num, col_from, col_to, col_blur, col_turned, col_key,
        width, slots, visits, regions, extent * width,
    )
    tile = rows[:, -TAIL, : 3 * exp_dev].astype(F32).reshape(cores, regions, 3, exp_dev)
    tile = jnp.sum(jnp.sum(tile, axis=2), axis=1)
    own = lax.broadcasted_iota(jnp.int32, (8, LANES), 0) // cores == pair_at
    placed = jnp.zeros((8, LANES), F32).at[:, :exp_dev].set(jnp.tile(tile, (8 // cores, 1)))
    tile = butterfly_sum(jnp.where(own, placed, 0.0), "y")
    weight = 1.0 / (tile[:visits, :exp_dev].reshape(exposures) / (extent * width))
    mean_weight = jnp.mean(weight)
    pieces = exchange(
        partial.reshape((visits * regions,) + partial.shape[2:]), ("y", "core", "region")
    )
    summed = jnp.sum(
        pieces.reshape(visits // cores, patch_rows, own_cols).astype(F32), axis=0, keepdims=True
    )

    total_slots = exposures * slots
    row_cover = coverage(
        row_start.reshape(total_slots, patch_rows),
        lanczos_taps(row_frac.reshape(total_slots, patch_rows)),
        extent,
    )
    at = region_at * own_cols
    col_cover = coverage(
        lax.dynamic_slice_in_dim(col_start, at, own_cols, 2).reshape(total_slots, own_cols),
        lanczos_taps(
            lax.dynamic_slice_in_dim(col_frac, at, own_cols, 2).reshape(total_slots, own_cols)
        ),
        width,
    )
    scale = jnp.where(
        correlations.reshape(total_slots) == visit_at, jnp.repeat(weight, slots), 0.0
    )
    weight_map = lax.dot_general(
        row_cover,
        col_cover * scale[:, None],
        (((0,), (0,)), ((), ())),
        precision=lax.Precision.HIGHEST,
        preferred_element_type=F32,
    ).reshape(1, patch_rows, own_cols)
    coadd = summed / jnp.maximum(weight_map, FLOOR_SHARE * mean_weight)
    return coadd, weight_map


def solution(mesh):
    visits, regions = mesh.devices.shape
    split = jax.sharding.Mesh(
        mesh.devices.reshape(visits // 2, 2, regions), ("y", "core", "region")
    )
    visit = ("y", "core")
    placed = (
        P(visit, "region", None),
        P(visit, "region", None),
        P(visit, None),
        P(),
        P(),
        P(),
        P(),
        P(),
    )
    return jax.shard_map(
        local,
        mesh=split,
        in_specs=placed,
        out_specs=(P(visit, None, "region"), P(visit, None, "region")),
        check_vma=False,
    )
```

```python
import functools
import math

import jax
import jax.numpy as jnp
from jax import lax
from jax.experimental import pallas as pl
from jax.experimental.pallas import tpu as pltpu
from jax.sharding import PartitionSpec as P

RADIUS = 10
TAPS = 6
SIGMAS = (1.0, 2.0, 4.0)
FLOOR_SHARE = 0.5
BF16 = jnp.bfloat16
F32 = jnp.float32

ROW_BLOCK = 128
ROW_STEP = 256
ROW_SPAN = 288
COL_BLOCK = 128
COL_STEP = 256
COL_GROUP = 18
BLUR_BLOCK = 256
BLUR_STEP = 512
BLUR_BAND = (112, 400)
LANES = 128
TAIL = 16
LIMIT = 14 * 1024 * 1024
ROW_LIMIT = 24 * 1024 * 1024
COL_LIMIT = 56 * 1024 * 1024


def psf_kernel(coefficient):
    offsets = jnp.arange(-RADIUS, RADIUS + 1).astype(coefficient.dtype)
    sigmas = jnp.array(SIGMAS, dtype=coefficient.dtype)
    gaussians = jnp.exp(
        -(offsets[None, :] * offsets[None, :]) / (2.0 * sigmas[:, None] * sigmas[:, None])
    )
    kernel = jnp.sum(coefficient[:, :, None] * gaussians[None, :, :], axis=1)
    return kernel / jnp.sum(kernel, axis=1, keepdims=True)


def lanczos_taps(f):
    g = 1.0 - f
    third = math.pi / 3.0
    tiny = 1e-6
    a = jnp.sin(third * f)
    b = jnp.sin(third * g)
    c = a + b
    fg = f * g
    a_over_f = jnp.where(f < tiny, third, a / jnp.maximum(f, tiny))
    b_over_g = jnp.where(g < tiny, third, b / jnp.maximum(g, tiny))
    values = [
        b * fg / ((f + 2.0) * (f + 2.0)),
        -c * fg / ((f + 1.0) * (f + 1.0)),
        a_over_f * g,
        b_over_g * f,
        -c * fg / ((2.0 - f) * (2.0 - f)),
        a * fg / ((3.0 - f) * (3.0 - f)),
    ]
    total = functools.reduce(jnp.add, values)
    return [lax.reduce_precision(value / total, 8, 7) for value in values]


def coverage(starts, taps, extent):
    running = jnp.zeros(starts.shape, F32)
    for tap_at, tap in enumerate(taps):
        position = starts + tap_at
        inside = (position >= 0) & (position < extent)
        running = running + jnp.where(inside, tap, 0.0)
    return running


def band_tables(starts, taps):
    place = jnp.arange(8, dtype=jnp.int32)[:, None]
    diff = place - starts[..., None, :]
    at = diff & 7
    turned = jnp.zeros(diff.shape, F32)
    for tap_at, tap in enumerate(taps):
        turned = turned + jnp.where(at == tap_at, tap[..., None, :], 0.0)
    return turned, diff - at


def toeplitz(kernel_ref, at, rows, cols, shift):
    diff = (
        lax.broadcasted_iota(jnp.int32, (rows, cols), 0)
        - lax.broadcasted_iota(jnp.int32, (rows, cols), 1)
    )
    full = jnp.zeros((rows, cols), F32)
    for tap_at in range(2 * RADIUS + 1):
        full = jnp.where(diff == tap_at - shift, kernel_ref[at, tap_at], full)
    return full


def dot(a, b):
    return jnp.dot(a, b, preferred_element_type=F32)


def two_parts(value):
    high = value.astype(BF16)
    return high, (value - high.astype(F32)).astype(BF16)


def halves_sum(value):
    half = value.shape[0] // 2
    return value[:half] + value[half:]


def band_of(turned, key, first, groups):
    moved = key + first
    return [jnp.where(moved == -8 * g, turned, 0.0) for g in range(groups)]


def row_matrix(blur_ref, turned, key, start, extent, masked):
    last = extent - ROW_STEP
    first = jnp.minimum(start, last)
    groups = ROW_SPAN // 8
    pieces = band_of(turned, key, first - 16, groups)
    for g in range(2):
        pieces[g] = jnp.where(first > 0, pieces[g], 0.0)
        pieces[groups - 1 - g] = jnp.where(first < last, pieces[groups - 1 - g], 0.0)
    band = jnp.concatenate(pieces, axis=0).astype(BF16)
    both = halves_sum(dot(blur_ref[...], band))
    if masked:
        row = lax.broadcasted_iota(jnp.int32, both.shape, 0) + first
        both = jnp.where(row >= start, both, 0.0)
    return jnp.concatenate(two_parts(both.T), axis=0)


def row_matrices_body(extent, kernel_ref, low_ref, turned_ref, key_ref, rows_ref, blur_ref):
    high, rest = two_parts(toeplitz(kernel_ref, 0, ROW_STEP, ROW_SPAN, 16 + RADIUS))
    blur_ref[0:ROW_STEP] = high
    blur_ref[ROW_STEP : 2 * ROW_STEP] = rest

    def block(at, carry):
        rows_ref[at] = row_matrix(
            blur_ref, turned_ref[at], key_ref[at], low_ref[at], extent, False
        )
        return carry

    lax.fori_loop(0, turned_ref.shape[0], block, 0)


def make_row_matrices(kernel, low, turned, key, extent):
    blocks = turned.shape[0]
    vmem = pl.BlockSpec(memory_space=pltpu.VMEM)
    smem = pl.BlockSpec(memory_space=pltpu.SMEM)
    return pl.pallas_call(
        functools.partial(row_matrices_body, extent),
        out_shape=(
            jax.ShapeDtypeStruct((blocks, 2 * ROW_BLOCK, ROW_STEP), BF16),
            jax.ShapeDtypeStruct((2 * ROW_STEP, ROW_SPAN), BF16),
        ),
        in_specs=[smem, smem, vmem, vmem],
        out_specs=(vmem, vmem),
        compiler_params=pltpu.CompilerParams(vmem_limit_bytes=LIMIT),
        name="row_matrices",
    )(kernel, low, turned, key)


def col_matrices_body(kernel_ref, cols_ref):
    begin, end = BLUR_BAND
    for e in range(cols_ref.shape[0]):
        high, rest = two_parts(
            toeplitz(kernel_ref, e, end - begin, BLUR_BLOCK, begin - LANES + RADIUS)
        )
        cols_ref[e, 0] = high
        cols_ref[e, 1] = rest


def make_col_matrices(kernels):
    return pl.pallas_call(
        col_matrices_body,
        out_shape=jax.ShapeDtypeStruct(
            (kernels.shape[0], 2, BLUR_BAND[1] - BLUR_BAND[0], BLUR_BLOCK), BF16
        ),
        in_specs=[pl.BlockSpec(memory_space=pltpu.SMEM)],
        out_specs=pl.BlockSpec(memory_space=pltpu.VMEM),
        compiler_params=pltpu.CompilerParams(vmem_limit_bytes=COL_LIMIT),
        name="col_matrices",
    )(kernels)


def row_body(slots, pieces, low_ref, num_ref, from_ref, *refs):
    piece_refs = refs[:pieces]
    rows_ref, blur_ref, turned_ref, key_ref, tail_ref, out_ref, x_ref, sems = refs[pieces:]
    extent, width = x_ref.shape
    height = extent // pieces
    copies = [
        pltpu.make_async_copy(
            piece_ref,
            x_ref.at[pl.ds(pl.multiple_of(from_ref[at] * height, height), height)],
            sems.at[at],
        )
        for at, piece_ref in enumerate(piece_refs)
    ]
    for copy in copies:
        copy.start()
    owners = out_ref.shape[0]
    blocks = turned_ref.shape[0] // slots
    owner_rows = blocks * ROW_BLOCK // owners
    data_rows = out_ref.shape[1] - TAIL
    for owner in range(owners):
        out_ref[owner, data_rows : data_rows + TAIL, :] = tail_ref[...]
    for copy in copies:
        copy.wait()

    def times(matrix, start):
        first = pl.multiple_of(jnp.minimum(start, extent - ROW_STEP), 16)
        return halves_sum(dot(matrix, x_ref[pl.ds(first, ROW_STEP), :]))

    def block(at, carry):
        indices = [slot * blocks + at for slot in range(slots)]
        sums = [times(rows_ref[index], low_ref[index]) for index in indices]
        for slot, index in enumerate(indices):

            def more(i, total, index=index):
                start = low_ref[index] + i * ROW_STEP
                matrix = row_matrix(
                    blur_ref, turned_ref[index], key_ref[index], start, extent, True
                )
                return total + times(matrix, start)

            total = lax.fori_loop(1, num_ref[index], more, sums[slot]).astype(BF16)
            for owner in range(ROW_BLOCK // owner_rows):
                for t in range(width // LANES):
                    place = (t * slots + slot) * owner_rows
                    out_ref[
                        at * (ROW_BLOCK // owner_rows) + owner, place : place + owner_rows, :
                    ] = total[
                        owner * owner_rows : (owner + 1) * owner_rows,
                        t * LANES : (t + 1) * LANES,
                    ]
        return carry

    lax.fori_loop(0, blocks, block, 0)


def row_warp(pieces, sources, low, num, matrices, blur, turned, key, tail, slots, owners):
    height, width = pieces[0].shape
    owner_rows = turned.shape[0] // slots * ROW_BLOCK // owners
    vmem = pl.BlockSpec(memory_space=pltpu.VMEM)
    smem = pl.BlockSpec(memory_space=pltpu.SMEM)
    return pl.pallas_call(
        functools.partial(row_body, slots, len(pieces)),
        out_shape=jax.ShapeDtypeStruct(
            (owners, width // LANES * slots * owner_rows + TAIL, LANES), BF16
        ),
        in_specs=[smem] * 3 + [pl.BlockSpec(memory_space=pl.ANY)] * len(pieces) + [vmem] * 5,
        out_specs=vmem,
        scratch_shapes=[
            pltpu.VMEM((len(pieces) * height, width), BF16),
            pltpu.SemaphoreType.DMA((len(pieces),)),
        ],
        compiler_params=pltpu.CompilerParams(vmem_limit_bytes=ROW_LIMIT),
        cost_estimate=pl.CostEstimate(
            flops=2_000_000_000, bytes_accessed=8 * 1024 * 1024, transcendentals=0
        ),
        name="row_warp",
    )(low, num, sources, *pieces, matrices, blur, turned, key, tail)


def col_body(cols, slots, pixels, count_ref, list_ref, low_ref, num_ref, from_ref, to_ref, z_hbm,
             blur_hbm, turned_hbm, key_hbm, out_ref, padded, blur, turned_ref, key_ref, tails,
             blurred, held, weight_ref, z_sems, blur_sems, table_sems):
    data_rows = z_hbm.shape[1] - TAIL
    exposures = blur_hbm.shape[0]
    sources = z_hbm.shape[0] // exposures
    tile_rows = data_rows // (cols // sources // LANES)
    rows = tile_rows // slots
    patch = pl.program_id(0)
    begin, end = BLUR_BAND

    @pl.when(patch == 0)
    def _():
        waits = []
        for e in range(exposures):
            copies = [
                pltpu.make_async_copy(
                    z_hbm.at[e * sources + s, pl.ds(0, data_rows)],
                    padded.at[e, pl.ds(tile_rows + s * data_rows, data_rows)],
                    z_sems.at[e, s],
                )
                for s in range(sources)
            ]
            copies.append(
                pltpu.make_async_copy(
                    blur_hbm.at[e], blur.at[e, :, pl.ds(begin, end - begin)], blur_sems.at[e]
                )
            )
            for copy in copies:
                copy.start()
            waits.append(copies)
        tables = [
            pltpu.make_async_copy(turned_hbm, turned_ref, table_sems.at[0]),
            pltpu.make_async_copy(key_hbm, key_ref, table_sems.at[1]),
            pltpu.make_async_copy(
                z_hbm.at[:, pl.ds(data_rows, TAIL)], tails, table_sems.at[2]
            ),
        ]
        for copy in tables:
            copy.start()
        pad = jnp.zeros((tile_rows, LANES), BF16)
        last = padded.shape[1] - tile_rows
        for e in range(exposures):
            padded[e, 0:tile_rows] = pad
            padded[e, last : last + tile_rows] = pad
            for n in range(2):
                blur[e, n, 0:begin] = jnp.zeros((begin, BLUR_BLOCK), BF16)
                blur[e, n, end:BLUR_STEP] = jnp.zeros((BLUR_STEP - end, BLUR_BLOCK), BF16)
            for j in range(slots):
                blurred[e * slots + j, :, cols : cols + COL_STEP] = jnp.zeros(
                    (2 * rows, COL_STEP), BF16
                )
        for e in range(exposures):
            for copy in waits[e]:
                copy.wait()
            windows = jnp.concatenate(
                [
                    jnp.concatenate(
                        [
                            padded[e, t * tile_rows : (t + 1) * tile_rows]
                            for t in range(
                                b * BLUR_BLOCK // LANES, (b * BLUR_BLOCK + BLUR_STEP) // LANES
                            )
                        ],
                        axis=1,
                    )
                    for b in range(cols // BLUR_BLOCK)
                ],
                axis=0,
            )
            high, rest = two_parts(dot(windows, blur[e, 0]) + dot(windows, blur[e, 1]))
            for b in range(cols // BLUR_BLOCK):
                for j in range(slots):
                    at = (b * slots + j) * rows
                    span = slice(b * BLUR_BLOCK, (b + 1) * BLUR_BLOCK)
                    blurred[e * slots + j, 0:rows, span] = high[at : at + rows]
                    blurred[e * slots + j, rows : 2 * rows, span] = rest[at : at + rows]
        for copy in tables:
            copy.wait()
        sums = jnp.sum(tails[...].astype(F32), axis=1)
        cores = 2
        visit_exp = exposures // cores
        lane = lax.broadcasted_iota(jnp.int32, (1, LANES), 1)
        for core in range(cores):
            per_core = sums.shape[0] // cores
            total = jnp.sum(
                sums[core * per_core : (core + 1) * per_core], axis=0, keepdims=True
            )
            for e in range(visit_exp):
                variance = jnp.sum(
                    jnp.where((lane < 3 * visit_exp) & (lane % visit_exp == e), total, 0.0)
                )
                for j in range(slots):
                    weight_ref[(core * visit_exp + e) * slots + j] = 1.0 / (variance / pixels)

    held[...] = jnp.zeros(held.shape, F32)

    blocks = turned_ref.shape[1]

    def part(slot, b, n):
        first = pl.multiple_of(jnp.minimum(low_ref[slot, b] + n * COL_STEP, cols), LANES)
        band = band_of(turned_ref[slot, b], key_ref[slot, b], first, COL_STEP // 8)
        band = jnp.concatenate(band, axis=0).astype(BF16)
        return halves_sum(dot(blurred[slot, :, pl.ds(first, COL_STEP)], band))

    def add_slot(i, carry):
        slot = list_ref[patch, i]
        begin, end = from_ref[slot], to_ref[slot]

        def add_group(c, carry):
            at = begin + c * COL_GROUP
            spots = [jnp.minimum(at + h, blocks - 1) for h in range(COL_GROUP)]
            weights = [jnp.where(at + h < end, weight_ref[slot], 0.0) for h in range(COL_GROUP)]

            def add_parts(n):
                sums = [part(slot, b, n) for b in spots]
                for b, weight, total in zip(spots, weights, sums):
                    span = pl.ds(pl.multiple_of(b * COL_BLOCK, COL_BLOCK), COL_BLOCK)
                    held[:, span] += weight * total

            add_parts(0)
            most = num_ref[slot, spots[0]]
            for b in spots[1:]:
                most = jnp.maximum(most, num_ref[slot, b])

            def more(n, carry):
                add_parts(n)
                return carry

            lax.fori_loop(1, most, more, 0)
            return carry

        steps = (end - begin + COL_GROUP - 1) // COL_GROUP
        return lax.fori_loop(0, steps, add_group, carry)

    lax.fori_loop(0, count_ref[patch], add_slot, 0)
    own_cols = out_ref.shape[3]
    for owner in range(out_ref.shape[1]):
        out_ref[0, owner] = held[:, owner * own_cols : (owner + 1) * own_cols].astype(BF16)


def col_warp(z, count, listed, low, num, begin, end, blur, turned, key, cols, slots, patches,
             owners, pixels):
    slot_total, blocks = turned.shape[:2]
    exposures = blur.shape[0]
    sources = z.shape[0] // exposures
    tile_rows = (z.shape[1] - TAIL) // (cols // sources // LANES)
    rows = tile_rows // slots
    own_cols = blocks * COL_BLOCK // owners
    smem = pl.BlockSpec(memory_space=pltpu.SMEM)
    return pl.pallas_call(
        functools.partial(col_body, cols, slots, pixels),
        out_shape=jax.ShapeDtypeStruct((patches, owners, rows, own_cols), BF16),
        grid=(patches,),
        in_specs=[smem] * 6 + [pl.BlockSpec(memory_space=pl.ANY)] * 4,
        out_specs=pl.BlockSpec((1, owners, rows, own_cols), lambda k: (k, 0, 0, 0)),
        scratch_shapes=[
            pltpu.VMEM((exposures, (cols // LANES + 2) * tile_rows, LANES), BF16),
            pltpu.VMEM((exposures, 2, BLUR_STEP, BLUR_BLOCK), BF16),
            pltpu.VMEM(turned.shape, F32),
            pltpu.VMEM(key.shape, jnp.int32),
            pltpu.VMEM((z.shape[0], TAIL, LANES), BF16),
            pltpu.VMEM((slot_total, 2 * rows, cols + COL_STEP), BF16),
            pltpu.VMEM((rows, owners * own_cols), F32),
            pltpu.SMEM((slot_total,), F32),
            pltpu.SemaphoreType.DMA((exposures, sources)),
            pltpu.SemaphoreType.DMA((exposures,)),
            pltpu.SemaphoreType.DMA((3,)),
        ],
        compiler_params=pltpu.CompilerParams(
            dimension_semantics=("arbitrary",), vmem_limit_bytes=COL_LIMIT
        ),
        cost_estimate=pl.CostEstimate(
            flops=8_000_000_000, bytes_accessed=16 * 1024 * 1024, transcendentals=0
        ),
        name="col_warp",
    )(count, listed, low, num, begin, end, z, blur, turned, key)


def split_body(parts, to_ref, image_ref, *refs):
    total = len(refs) - 3
    out_refs = refs[:total]
    held, in_sems, out_sems = refs[total:]
    width = held.shape[2]
    reads = []
    for at in range(total):
        lane = pl.multiple_of(to_ref[at] % parts * width, width)
        reads.append(
            pltpu.make_async_copy(
                image_ref.at[to_ref[at] // parts, :, pl.ds(lane, width)],
                held.at[at],
                in_sems.at[at],
            )
        )
    writes = [
        pltpu.make_async_copy(held.at[at], out_refs[at], out_sems.at[at]) for at in range(total)
    ]
    for read in reads:
        read.start()
    for read, write in zip(reads, writes):
        read.wait()
        write.start()
    for write in writes:
        write.wait()


def split_columns(image, targets, parts):
    exposures, height, width = image.shape
    total = exposures * parts
    shape = (height, width // parts)
    return pl.pallas_call(
        functools.partial(split_body, parts),
        out_shape=[jax.ShapeDtypeStruct(shape, image.dtype)] * total,
        in_specs=[
            pl.BlockSpec(memory_space=pltpu.SMEM),
            pl.BlockSpec(memory_space=pl.ANY),
        ],
        out_specs=[pl.BlockSpec(memory_space=pl.ANY)] * total,
        scratch_shapes=[
            pltpu.VMEM((total,) + shape, image.dtype),
            pltpu.SemaphoreType.DMA((total,)),
            pltpu.SemaphoreType.DMA((total,)),
        ],
        compiler_params=pltpu.CompilerParams(vmem_limit_bytes=COL_LIMIT),
        name="split_columns",
    )(targets, image)


RING = 4

TWO_STEPS = {
    (2, 0): ((1, 0), (1, 0)),
    (2, 3): ((1, 0), (1, -1)),
    (2, 1): ((-1, 0), (-1, 1)),
    (2, 2): ((-1, 1), (-1, 1)),
    (0, 2): ((0, 1), (0, 1)),
    (1, 2): ((0, -1), (1, -1)),
    (3, 2): ((0, -1), (-1, -1)),
}


def region_shifts(regions):
    outer = regions // RING
    shifts = [(dx, dz) for dx in range(outer) for dz in range(RING)]
    return sorted(shifts, key=lambda s: (s == (0, 0), s not in TWO_STEPS))


def shifted(at, shift, regions):
    outer = regions // RING
    return (at // RING + shift[0]) % outer * RING + (at % RING + shift[1]) % RING


def send_shifted(x, shift, regions):
    if shift == (0, 0):
        return x
    for step in TWO_STEPS.get(shift, (shift,)):
        x = lax.ppermute(x, "region", [(i, shifted(i, step, regions)) for i in range(regions)])
    return x


def butterfly_sum(x, axis):
    size = lax.axis_size(axis)
    step = 1
    while step < size:
        x = x + lax.ppermute(x, axis, [(i, i ^ step) for i in range(size)])
        step *= 2
    return x


def local(image, variance, psf_coef, correlations, row_start, row_frac, col_start, col_frac):
    exp_dev, height, width = image.shape
    exposures, slots = correlations.shape
    patch_rows = row_start.shape[2]
    patch_cols = col_start.shape[2]
    cores = lax.axis_size("core")
    visits = lax.axis_size("y") * cores
    regions = lax.axis_size("region")
    extent = height * regions
    parts = regions // exp_dev
    part_cols = width // parts
    own_cols = patch_cols // regions
    pair_at = lax.axis_index("y")
    core_at = lax.axis_index("core")
    visit_at = pair_at * cores + core_at
    region_at = lax.axis_index("region")

    def exchange(x, axis):
        return lax.all_to_all(x, axis, split_axis=0, concat_axis=0, tiled=True)

    shifts = region_shifts(regions)
    targets = jnp.stack([shifted(region_at, shift, regions) for shift in shifts])
    sources = jnp.stack([shifted(region_at, (-dx, -dz), regions) for dx, dz in shifts])
    sent = split_columns(image, targets.astype(jnp.int32), parts)
    (first, variance, psf_coef, row_start, row_frac, col_start, col_frac) = lax.optimization_barrier(
        (sent[0], variance, psf_coef, row_start, row_frac, col_start, col_frac)
    )
    sent = [first] + list(sent[1:])
    columns = [send_shifted(x, shift, regions) for x, shift in zip(sent, shifts)]

    kernels = psf_kernel(psf_coef)

    own_exp = region_at // parts
    at_exp = visit_at * exp_dev + own_exp
    blocks = slots * patch_rows // ROW_BLOCK
    starts = lax.dynamic_index_in_dim(row_start, at_exp, 0, keepdims=False)
    fracs = lax.dynamic_index_in_dim(row_frac, at_exp, 0, keepdims=False)
    starts = starts.reshape(blocks, ROW_BLOCK)
    row_turned, row_key = band_tables(starts, lanczos_taps(fracs.reshape(blocks, ROW_BLOCK)))
    row_low = jnp.clip(starts[:, 0] - RADIUS, 0, extent - ROW_STEP) // 16 * 16
    row_end = jnp.minimum(starts[:, -1] + TAPS + RADIUS, extent)
    row_num = jnp.maximum(row_end - row_low + ROW_STEP - 1, 0) // ROW_STEP
    row_matrices, row_blur = make_row_matrices(
        lax.dynamic_slice_in_dim(kernels, own_exp, 1, 0), row_low, row_turned, row_key, extent
    )

    rest = jnp.sum(variance.astype(F32), axis=(1, 2))
    sum_parts = []
    for _ in range(3):
        sum_parts.append(lax.reduce_precision(rest, 8, 7))
        rest = rest - sum_parts[-1]
    tail = jnp.zeros((TAIL, LANES), F32).at[0, : 3 * exp_dev].set(jnp.concatenate(sum_parts))
    tail = tail.astype(BF16)
    pair_exp = cores * exp_dev
    first_exp = pair_at * pair_exp

    slot_total = pair_exp * slots
    col_blocks = patch_cols // COL_BLOCK
    own_starts = lax.dynamic_slice_in_dim(col_start, first_exp, pair_exp, 0)
    own_fracs = lax.dynamic_slice_in_dim(col_frac, first_exp, pair_exp, 0)
    own_starts = own_starts.reshape(slot_total, col_blocks, COL_BLOCK)
    own_fracs = own_fracs.reshape(slot_total, col_blocks, COL_BLOCK)
    col_turned, col_key = band_tables(own_starts, lanczos_taps(own_fracs))
    col_low = jnp.clip(own_starts[:, :, 0], 0, width) // LANES * LANES
    col_end = jnp.minimum(own_starts[:, :, -1] + TAPS, width)
    col_num = jnp.maximum(col_end - col_low + COL_STEP - 1, 0) // COL_STEP
    block_at = jnp.arange(col_blocks, dtype=jnp.int32)
    col_from = jnp.min(jnp.where(col_num > 0, block_at, col_blocks), axis=1)
    col_to = jnp.max(jnp.where(col_num > 0, block_at + 1, 0), axis=1)
    col_from = jnp.minimum(col_from, col_to)
    owners = lax.dynamic_slice_in_dim(correlations, first_exp, pair_exp, 0).reshape(slot_total)
    named = owners == jnp.arange(visits, dtype=jnp.int32)[:, None]
    named = named.astype(jnp.int32)
    count = jnp.sum(named, axis=1)
    slot_ids = jnp.arange(slot_total, dtype=jnp.int32)
    rank = jnp.sum(jnp.where(slot_ids[:, None] < slot_ids, named[:, :, None], 0), axis=1)
    listed = jnp.sum(
        jnp.where((named[:, None, :] > 0) & (rank[:, None, :] == slot_ids[:, None]), slot_ids, 0),
        axis=2,
    )

    warped = row_warp(
        columns, sources.astype(jnp.int32), row_low, row_num, row_matrices, row_blur, row_turned, row_key, tail, slots,
        cores * regions,
    )
    psf_tile = jnp.zeros((8, LANES), F32).at[:exp_dev, : 2 * RADIUS + 1].set(kernels)
    psf_tile, warped = lax.optimization_barrier((psf_tile, warped))
    rows = exchange(warped, ("core", "region"))
    other = lax.ppermute(psf_tile, "core", [(i, i ^ 1) for i in range(cores)])
    other = other[:exp_dev, : 2 * RADIUS + 1]
    col_blur = make_col_matrices(
        jnp.concatenate(
            [jnp.where(core_at == 0, kernels, other), jnp.where(core_at == 0, other, kernels)]
        )
    )
    partial = col_warp(
        rows, count, listed, col_low, col_num, col_from, col_to, col_blur, col_turned, col_key,
        width, slots, visits, regions, extent * width,
    )
    tile = rows[:, -TAIL, : 3 * exp_dev].astype(F32).reshape(cores, regions, 3, exp_dev)
    tile = jnp.sum(jnp.sum(tile, axis=2), axis=1)
    own = lax.broadcasted_iota(jnp.int32, (8, LANES), 0) // cores == pair_at
    placed = jnp.zeros((8, LANES), F32).at[:, :exp_dev].set(jnp.tile(tile, (8 // cores, 1)))
    tile = butterfly_sum(jnp.where(own, placed, 0.0), "y")
    weight = 1.0 / (tile[:visits, :exp_dev].reshape(exposures) / (extent * width))
    mean_weight = jnp.mean(weight)
    pieces = exchange(
        partial.reshape((visits * regions,) + partial.shape[2:]), ("y", "core", "region")
    )
    summed = jnp.sum(
        pieces.reshape(visits // cores, patch_rows, own_cols).astype(F32), axis=0, keepdims=True
    )

    total_slots = exposures * slots
    row_cover = coverage(
        row_start.reshape(total_slots, patch_rows),
        lanczos_taps(row_frac.reshape(total_slots, patch_rows)),
        extent,
    )
    at = region_at * own_cols
    col_cover = coverage(
        lax.dynamic_slice_in_dim(col_start, at, own_cols, 2).reshape(total_slots, own_cols),
        lanczos_taps(
            lax.dynamic_slice_in_dim(col_frac, at, own_cols, 2).reshape(total_slots, own_cols)
        ),
        width,
    )
    scale = jnp.where(
        correlations.reshape(total_slots) == visit_at, jnp.repeat(weight, slots), 0.0
    )
    weight_map = lax.dot_general(
        row_cover,
        col_cover * scale[:, None],
        (((0,), (0,)), ((), ())),
        precision=lax.Precision.HIGHEST,
        preferred_element_type=F32,
    ).reshape(1, patch_rows, own_cols)
    coadd = summed / jnp.maximum(weight_map, FLOOR_SHARE * mean_weight)
    return coadd, weight_map


def solution(mesh):
    visits, regions = mesh.devices.shape
    split = jax.sharding.Mesh(
        mesh.devices.reshape(visits // 2, 2, regions), ("y", "core", "region")
    )
    visit = ("y", "core")
    placed = (
        P(visit, "region", None),
        P(visit, "region", None),
        P(visit, None),
        P(),
        P(),
        P(),
        P(),
        P(),
    )
    return jax.shard_map(
        local,
        mesh=split,
        in_specs=placed,
        out_specs=(P(visit, None, "region"), P(visit, None, "region")),
        check_vma=False,
    )
```

```python
import functools
import math

import jax
import jax.numpy as jnp
from jax import lax
from jax.experimental import pallas as pl
from jax.experimental.pallas import tpu as pltpu
from jax.sharding import PartitionSpec as P

RADIUS = 10
TAPS = 6
SIGMAS = (1.0, 2.0, 4.0)
FLOOR_SHARE = 0.5
BF16 = jnp.bfloat16
F32 = jnp.float32

ROW_BLOCK = 128
ROW_STEP = 256
ROW_SPAN = 288
COL_BLOCK = 128
COL_STEP = 256
COL_GROUP = 18
BLUR_BLOCK = 256
BLUR_STEP = 512
BLUR_BAND = (112, 400)
LANES = 128
TAIL = 16
COL_LIMIT = 56 * 1024 * 1024


def psf_kernel(coefficient):
    offsets = jnp.arange(-RADIUS, RADIUS + 1).astype(coefficient.dtype)
    sigmas = jnp.array(SIGMAS, dtype=coefficient.dtype)
    gaussians = jnp.exp(
        -(offsets[None, :] * offsets[None, :]) / (2.0 * sigmas[:, None] * sigmas[:, None])
    )
    kernel = jnp.sum(coefficient[:, :, None] * gaussians[None, :, :], axis=1)
    return kernel / jnp.sum(kernel, axis=1, keepdims=True)


def lanczos_taps(f):
    g = 1.0 - f
    third = math.pi / 3.0
    tiny = 1e-6
    a = jnp.sin(third * f)
    b = jnp.sin(third * g)
    c = a + b
    fg = f * g
    a_over_f = jnp.where(f < tiny, third, a / jnp.maximum(f, tiny))
    b_over_g = jnp.where(g < tiny, third, b / jnp.maximum(g, tiny))
    values = [
        b * fg / ((f + 2.0) * (f + 2.0)),
        -c * fg / ((f + 1.0) * (f + 1.0)),
        a_over_f * g,
        b_over_g * f,
        -c * fg / ((2.0 - f) * (2.0 - f)),
        a * fg / ((3.0 - f) * (3.0 - f)),
    ]
    total = functools.reduce(jnp.add, values)
    return [lax.reduce_precision(value / total, 8, 7) for value in values]


def coverage(starts, taps, extent):
    running = jnp.zeros(starts.shape, F32)
    for tap_at, tap in enumerate(taps):
        position = starts + tap_at
        inside = (position >= 0) & (position < extent)
        running = running + jnp.where(inside, tap, 0.0)
    return running


def band_tables(starts, taps):
    place = jnp.arange(8, dtype=jnp.int32)[:, None]
    diff = place - starts[..., None, :]
    at = diff & 7
    turned = jnp.zeros(diff.shape, F32)
    for tap_at, tap in enumerate(taps):
        turned = turned + jnp.where(at == tap_at, tap[..., None, :], 0.0)
    return turned, diff - at


def toeplitz(kernel_ref, at, rows, cols, shift):
    diff = (
        lax.broadcasted_iota(jnp.int32, (rows, cols), 0)
        - lax.broadcasted_iota(jnp.int32, (rows, cols), 1)
    )
    full = jnp.zeros((rows, cols), F32)
    for tap_at in range(2 * RADIUS + 1):
        full = jnp.where(diff == tap_at - shift, kernel_ref[at, tap_at], full)
    return full


def dot(a, b):
    return jnp.dot(a, b, preferred_element_type=F32)


def two_parts(value):
    high = value.astype(BF16)
    return high, (value - high.astype(F32)).astype(BF16)


def halves_sum(value):
    half = value.shape[0] // 2
    return value[:half] + value[half:]


def band_of(turned, key, first, groups):
    moved = key + first
    return [jnp.where(moved == -8 * g, turned, 0.0) for g in range(groups)]


def row_matrix(blur_ref, turned, key, start, extent, masked):
    last = extent - ROW_STEP
    first = jnp.minimum(start, last)
    groups = ROW_SPAN // 8
    pieces = band_of(turned, key, first - 16, groups)
    for g in range(2):
        pieces[g] = jnp.where(first > 0, pieces[g], 0.0)
        pieces[groups - 1 - g] = jnp.where(first < last, pieces[groups - 1 - g], 0.0)
    band = jnp.concatenate(pieces, axis=0).astype(BF16)
    both = halves_sum(dot(blur_ref[...], band))
    if masked:
        row = lax.broadcasted_iota(jnp.int32, both.shape, 0) + first
        both = jnp.where(row >= start, both, 0.0)
    return jnp.concatenate(two_parts(both.T), axis=0)


def row_matrices_body(extent, kernel_ref, low_ref, turned_ref, key_ref, rows_ref, blur_ref):
    high, rest = two_parts(toeplitz(kernel_ref, 0, ROW_STEP, ROW_SPAN, 16 + RADIUS))
    blur_ref[0:ROW_STEP] = high
    blur_ref[ROW_STEP : 2 * ROW_STEP] = rest

    def block(at, carry):
        rows_ref[at] = row_matrix(
            blur_ref, turned_ref[at], key_ref[at], low_ref[at], extent, False
        )
        return carry

    lax.fori_loop(0, turned_ref.shape[0], block, 0)


def make_row_matrices(kernel, low, turned, key, extent):
    blocks = turned.shape[0]
    vmem = pl.BlockSpec(memory_space=pltpu.VMEM)
    smem = pl.BlockSpec(memory_space=pltpu.SMEM)
    return pl.pallas_call(
        functools.partial(row_matrices_body, extent),
        out_shape=(
            jax.ShapeDtypeStruct((blocks, 2 * ROW_BLOCK, ROW_STEP), BF16),
            jax.ShapeDtypeStruct((2 * ROW_STEP, ROW_SPAN), BF16),
        ),
        in_specs=[smem, smem, vmem, vmem],
        out_specs=(vmem, vmem),
        compiler_params=pltpu.CompilerParams(vmem_limit_bytes=COL_LIMIT),
        name="row_matrices",
    )(kernel, low, turned, key)


def col_matrices_body(kernel_ref, cols_ref):
    begin, end = BLUR_BAND
    for e in range(cols_ref.shape[0]):
        high, rest = two_parts(
            toeplitz(kernel_ref, e, end - begin, BLUR_BLOCK, begin - LANES + RADIUS)
        )
        cols_ref[e, 0] = high
        cols_ref[e, 1] = rest


def make_col_matrices(kernels):
    return pl.pallas_call(
        col_matrices_body,
        out_shape=jax.ShapeDtypeStruct(
            (kernels.shape[0], 2, BLUR_BAND[1] - BLUR_BAND[0], BLUR_BLOCK), BF16
        ),
        in_specs=[pl.BlockSpec(memory_space=pltpu.SMEM)],
        out_specs=pl.BlockSpec(memory_space=pltpu.VMEM),
        compiler_params=pltpu.CompilerParams(vmem_limit_bytes=COL_LIMIT),
        name="col_matrices",
    )(kernels)


def row_body(slots, pieces, low_ref, num_ref, from_ref, *refs):
    piece_refs = refs[:pieces]
    rows_ref, blur_ref, turned_ref, key_ref, tail_ref, out_ref, x_ref, sems = refs[pieces:]
    extent, width = x_ref.shape
    height = extent // pieces
    copies = [
        pltpu.make_async_copy(
            piece_ref,
            x_ref.at[pl.ds(pl.multiple_of(from_ref[at] * height, height), height)],
            sems.at[at],
        )
        for at, piece_ref in enumerate(piece_refs)
    ]
    for copy in copies:
        copy.start()
    owners = out_ref.shape[0]
    blocks = turned_ref.shape[0] // slots
    owner_rows = blocks * ROW_BLOCK // owners
    data_rows = out_ref.shape[1] - TAIL
    for owner in range(owners):
        out_ref[owner, data_rows : data_rows + TAIL, :] = tail_ref[...]
    for copy in copies:
        copy.wait()

    def times(matrix, start):
        first = pl.multiple_of(jnp.minimum(start, extent - ROW_STEP), 16)
        return halves_sum(dot(matrix, x_ref[pl.ds(first, ROW_STEP), :]))

    def block(at, carry):
        indices = [slot * blocks + at for slot in range(slots)]
        sums = [times(rows_ref[index], low_ref[index]) for index in indices]
        for slot, index in enumerate(indices):

            def more(i, total, index=index):
                start = low_ref[index] + i * ROW_STEP
                matrix = row_matrix(
                    blur_ref, turned_ref[index], key_ref[index], start, extent, True
                )
                return total + times(matrix, start)

            total = lax.fori_loop(1, num_ref[index], more, sums[slot]).astype(BF16)
            for owner in range(ROW_BLOCK // owner_rows):
                for t in range(width // LANES):
                    place = (t * slots + slot) * owner_rows
                    out_ref[
                        at * (ROW_BLOCK // owner_rows) + owner, place : place + owner_rows, :
                    ] = total[
                        owner * owner_rows : (owner + 1) * owner_rows,
                        t * LANES : (t + 1) * LANES,
                    ]
        return carry

    lax.fori_loop(0, blocks, block, 0)


def row_warp(pieces, sources, low, num, matrices, blur, turned, key, tail, slots, owners):
    height, width = pieces[0].shape
    owner_rows = turned.shape[0] // slots * ROW_BLOCK // owners
    vmem = pl.BlockSpec(memory_space=pltpu.VMEM)
    smem = pl.BlockSpec(memory_space=pltpu.SMEM)
    return pl.pallas_call(
        functools.partial(row_body, slots, len(pieces)),
        out_shape=jax.ShapeDtypeStruct(
            (owners, width // LANES * slots * owner_rows + TAIL, LANES), BF16
        ),
        in_specs=[smem] * 3 + [pl.BlockSpec(memory_space=pltpu.HBM)] * len(pieces) + [vmem] * 5,
        out_specs=vmem,
        scratch_shapes=[
            pltpu.VMEM((len(pieces) * height, width), BF16),
            pltpu.SemaphoreType.DMA((len(pieces),)),
        ],
        compiler_params=pltpu.CompilerParams(vmem_limit_bytes=COL_LIMIT),
        cost_estimate=pl.CostEstimate(
            flops=2_000_000_000, bytes_accessed=8 * 1024 * 1024, transcendentals=0
        ),
        name="row_warp",
    )(low, num, sources, *pieces, matrices, blur, turned, key, tail)


def col_body(cols, slots, pixels, count_ref, list_ref, low_ref, num_ref, from_ref, to_ref, z_hbm,
             blur_hbm, turned_hbm, key_hbm, out_ref, padded, blur, turned_ref, key_ref, tails,
             blurred, held, weight_ref, z_sems, blur_sems, table_sems):
    data_rows = z_hbm.shape[1] - TAIL
    exposures = blur_hbm.shape[0]
    sources = z_hbm.shape[0] // exposures
    tile_rows = data_rows // (cols // sources // LANES)
    rows = tile_rows // slots
    patch = pl.program_id(0)
    begin, end = BLUR_BAND

    @pl.when(patch == 0)
    def _():
        waits = []
        for e in range(exposures):
            copies = [
                pltpu.make_async_copy(
                    z_hbm.at[e * sources + s, pl.ds(0, data_rows)],
                    padded.at[e, pl.ds(tile_rows + s * data_rows, data_rows)],
                    z_sems.at[e, s],
                )
                for s in range(sources)
            ]
            copies.append(
                pltpu.make_async_copy(
                    blur_hbm.at[e], blur.at[e, :, pl.ds(begin, end - begin)], blur_sems.at[e]
                )
            )
            for copy in copies:
                copy.start()
            waits.append(copies)
        tables = [
            pltpu.make_async_copy(turned_hbm, turned_ref, table_sems.at[0]),
            pltpu.make_async_copy(key_hbm, key_ref, table_sems.at[1]),
            pltpu.make_async_copy(
                z_hbm.at[:, pl.ds(data_rows, TAIL)], tails, table_sems.at[2]
            ),
        ]
        for copy in tables:
            copy.start()
        pad = jnp.zeros((tile_rows, LANES), BF16)
        last = padded.shape[1] - tile_rows
        for e in range(exposures):
            padded[e, 0:tile_rows] = pad
            padded[e, last : last + tile_rows] = pad
            for n in range(2):
                blur[e, n, 0:begin] = jnp.zeros((begin, BLUR_BLOCK), BF16)
                blur[e, n, end:BLUR_STEP] = jnp.zeros((BLUR_STEP - end, BLUR_BLOCK), BF16)
            for j in range(slots):
                blurred[e * slots + j, :, cols : cols + COL_STEP] = jnp.zeros(
                    (2 * rows, COL_STEP), BF16
                )
        for e in range(exposures):
            for copy in waits[e]:
                copy.wait()
            windows = jnp.concatenate(
                [
                    jnp.concatenate(
                        [
                            padded[e, t * tile_rows : (t + 1) * tile_rows]
                            for t in range(
                                b * BLUR_BLOCK // LANES, (b * BLUR_BLOCK + BLUR_STEP) // LANES
                            )
                        ],
                        axis=1,
                    )
                    for b in range(cols // BLUR_BLOCK)
                ],
                axis=0,
            )
            high, rest = two_parts(dot(windows, blur[e, 0]) + dot(windows, blur[e, 1]))
            for b in range(cols // BLUR_BLOCK):
                for j in range(slots):
                    at = (b * slots + j) * rows
                    span = slice(b * BLUR_BLOCK, (b + 1) * BLUR_BLOCK)
                    blurred[e * slots + j, 0:rows, span] = high[at : at + rows]
                    blurred[e * slots + j, rows : 2 * rows, span] = rest[at : at + rows]
        for copy in tables:
            copy.wait()
        sums = jnp.sum(tails[...].astype(F32), axis=1)
        cores = 2
        visit_exp = exposures // cores
        lane = lax.broadcasted_iota(jnp.int32, (1, LANES), 1)
        for core in range(cores):
            per_core = sums.shape[0] // cores
            total = jnp.sum(
                sums[core * per_core : (core + 1) * per_core], axis=0, keepdims=True
            )
            for e in range(visit_exp):
                variance = jnp.sum(
                    jnp.where((lane < 3 * visit_exp) & (lane % visit_exp == e), total, 0.0)
                )
                for j in range(slots):
                    weight_ref[(core * visit_exp + e) * slots + j] = 1.0 / (variance / pixels)

    held[...] = jnp.zeros(held.shape, F32)

    blocks = turned_ref.shape[1]

    def part(slot, b, n):
        first = pl.multiple_of(jnp.minimum(low_ref[slot, b] + n * COL_STEP, cols), LANES)
        band = band_of(turned_ref[slot, b], key_ref[slot, b], first, COL_STEP // 8)
        band = jnp.concatenate(band, axis=0).astype(BF16)
        return halves_sum(dot(blurred[slot, :, pl.ds(first, COL_STEP)], band))

    def add_slot(i, carry):
        slot = list_ref[patch, i]
        begin, end = from_ref[slot], to_ref[slot]

        def add_group(c, carry):
            at = begin + c * COL_GROUP
            spots = [jnp.minimum(at + h, blocks - 1) for h in range(COL_GROUP)]
            weights = [jnp.where(at + h < end, weight_ref[slot], 0.0) for h in range(COL_GROUP)]

            def add_parts(n):
                sums = [part(slot, b, n) for b in spots]
                for b, weight, total in zip(spots, weights, sums):
                    span = pl.ds(pl.multiple_of(b * COL_BLOCK, COL_BLOCK), COL_BLOCK)
                    held[:, span] += weight * total

            add_parts(0)
            most = num_ref[slot, spots[0]]
            for b in spots[1:]:
                most = jnp.maximum(most, num_ref[slot, b])

            def more(n, carry):
                add_parts(n)
                return carry

            lax.fori_loop(1, most, more, 0)
            return carry

        steps = (end - begin + COL_GROUP - 1) // COL_GROUP
        return lax.fori_loop(0, steps, add_group, carry)

    lax.fori_loop(0, count_ref[patch], add_slot, 0)
    own_cols = out_ref.shape[3]
    for owner in range(out_ref.shape[1]):
        out_ref[0, owner] = held[:, owner * own_cols : (owner + 1) * own_cols].astype(BF16)


def col_warp(z, count, listed, low, num, begin, end, blur, turned, key, cols, slots, patches,
             owners, pixels):
    slot_total, blocks = turned.shape[:2]
    exposures = blur.shape[0]
    sources = z.shape[0] // exposures
    tile_rows = (z.shape[1] - TAIL) // (cols // sources // LANES)
    rows = tile_rows // slots
    own_cols = blocks * COL_BLOCK // owners
    smem = pl.BlockSpec(memory_space=pltpu.SMEM)
    return pl.pallas_call(
        functools.partial(col_body, cols, slots, pixels),
        out_shape=jax.ShapeDtypeStruct((patches, owners, rows, own_cols), BF16),
        grid=(patches,),
        in_specs=[smem] * 6 + [pl.BlockSpec(memory_space=pltpu.HBM)] * 4,
        out_specs=pl.BlockSpec((1, owners, rows, own_cols), lambda k: (k, 0, 0, 0)),
        scratch_shapes=[
            pltpu.VMEM((exposures, (cols // LANES + 2) * tile_rows, LANES), BF16),
            pltpu.VMEM((exposures, 2, BLUR_STEP, BLUR_BLOCK), BF16),
            pltpu.VMEM(turned.shape, F32),
            pltpu.VMEM(key.shape, jnp.int32),
            pltpu.VMEM((z.shape[0], TAIL, LANES), BF16),
            pltpu.VMEM((slot_total, 2 * rows, cols + COL_STEP), BF16),
            pltpu.VMEM((rows, owners * own_cols), F32),
            pltpu.SMEM((slot_total,), F32),
            pltpu.SemaphoreType.DMA((exposures, sources)),
            pltpu.SemaphoreType.DMA((exposures,)),
            pltpu.SemaphoreType.DMA((3,)),
        ],
        compiler_params=pltpu.CompilerParams(
            dimension_semantics=("arbitrary",), vmem_limit_bytes=COL_LIMIT
        ),
        cost_estimate=pl.CostEstimate(
            flops=8_000_000_000, bytes_accessed=16 * 1024 * 1024, transcendentals=0
        ),
        name="col_warp",
    )(count, listed, low, num, begin, end, z, blur, turned, key)


def split_body(parts, to_ref, image_ref, *refs):
    total = len(refs) - 3
    out_refs = refs[:total]
    held, in_sems, out_sems = refs[total:]
    width = held.shape[2]
    reads = []
    for at in range(total):
        lane = pl.multiple_of(to_ref[at] % parts * width, width)
        reads.append(
            pltpu.make_async_copy(
                image_ref.at[to_ref[at] // parts, :, pl.ds(lane, width)],
                held.at[at],
                in_sems.at[at],
            )
        )
    writes = [
        pltpu.make_async_copy(held.at[at], out_refs[at], out_sems.at[at]) for at in range(total)
    ]
    for read in reads:
        read.start()
    for read, write in zip(reads, writes):
        read.wait()
        write.start()
    for write in writes:
        write.wait()


def split_columns(image, targets, parts):
    exposures, height, width = image.shape
    total = exposures * parts
    shape = (height, width // parts)
    return pl.pallas_call(
        functools.partial(split_body, parts),
        out_shape=[jax.ShapeDtypeStruct(shape, image.dtype)] * total,
        in_specs=[
            pl.BlockSpec(memory_space=pltpu.SMEM),
            pl.BlockSpec(memory_space=pl.ANY),
        ],
        out_specs=[pl.BlockSpec(memory_space=pltpu.HBM)] * total,
        scratch_shapes=[
            pltpu.VMEM((total,) + shape, image.dtype),
            pltpu.SemaphoreType.DMA((total,)),
            pltpu.SemaphoreType.DMA((total,)),
        ],
        compiler_params=pltpu.CompilerParams(vmem_limit_bytes=COL_LIMIT),
        name="split_columns",
    )(targets, image)


RING = 4

TWO_STEPS = {
    (2, 0): ((1, 0), (1, 0)),
    (2, 3): ((1, 0), (1, -1)),
    (2, 1): ((-1, 0), (-1, 1)),
    (2, 2): ((-1, 1), (-1, 1)),
    (0, 2): ((0, 1), (0, 1)),
    (1, 2): ((0, -1), (1, -1)),
    (3, 2): ((0, -1), (-1, -1)),
}


def region_shifts(regions):
    outer = regions // RING
    shifts = [(dx, dz) for dx in range(outer) for dz in range(RING)]
    return sorted(shifts, key=lambda s: (s == (0, 0), s not in TWO_STEPS))


def shifted(at, shift, regions):
    outer = regions // RING
    return (at // RING + shift[0]) % outer * RING + (at % RING + shift[1]) % RING


def send_shifted(x, shift, regions):
    if shift == (0, 0):
        return x
    for step in TWO_STEPS.get(shift, (shift,)):
        x = lax.ppermute(x, "region", [(i, shifted(i, step, regions)) for i in range(regions)])
    return x


def butterfly_sum(x, axis):
    size = lax.axis_size(axis)
    step = 1
    while step < size:
        x = x + lax.ppermute(x, axis, [(i, i ^ step) for i in range(size)])
        step *= 2
    return x


def local(image, variance, psf_coef, correlations, row_start, row_frac, col_start, col_frac):
    exp_dev, height, width = image.shape
    exposures, slots = correlations.shape
    patch_rows = row_start.shape[2]
    patch_cols = col_start.shape[2]
    cores = lax.axis_size("core")
    visits = lax.axis_size("y") * cores
    regions = lax.axis_size("region")
    extent = height * regions
    parts = regions // exp_dev
    part_cols = width // parts
    own_cols = patch_cols // regions
    pair_at = lax.axis_index("y")
    core_at = lax.axis_index("core")
    visit_at = pair_at * cores + core_at
    region_at = lax.axis_index("region")

    def exchange(x, axis):
        return lax.all_to_all(x, axis, split_axis=0, concat_axis=0, tiled=True)

    shifts = region_shifts(regions)
    targets = jnp.stack([shifted(region_at, shift, regions) for shift in shifts])
    sources = jnp.stack([shifted(region_at, (-dx, -dz), regions) for dx, dz in shifts])
    sent = split_columns(image, targets.astype(jnp.int32), parts)
    first, variance, psf_coef, row_start, row_frac = lax.optimization_barrier(
        (sent[0], variance, psf_coef, row_start, row_frac)
    )
    sent = [first] + list(sent[1:])

    kernels = psf_kernel(psf_coef)

    own_exp = region_at // parts
    at_exp = visit_at * exp_dev + own_exp
    blocks = slots * patch_rows // ROW_BLOCK
    starts = lax.dynamic_index_in_dim(row_start, at_exp, 0, keepdims=False)
    fracs = lax.dynamic_index_in_dim(row_frac, at_exp, 0, keepdims=False)
    starts = starts.reshape(blocks, ROW_BLOCK)
    row_turned, row_key = band_tables(starts, lanczos_taps(fracs.reshape(blocks, ROW_BLOCK)))
    row_low = jnp.clip(starts[:, 0] - RADIUS, 0, extent - ROW_STEP) // 16 * 16
    row_end = jnp.minimum(starts[:, -1] + TAPS + RADIUS, extent)
    row_num = jnp.maximum(row_end - row_low + ROW_STEP - 1, 0) // ROW_STEP
    row_matrices, row_blur = make_row_matrices(
        lax.dynamic_slice_in_dim(kernels, own_exp, 1, 0), row_low, row_turned, row_key, extent
    )

    late = min(4, regions - 1)
    *held_back, row_matrices = lax.optimization_barrier(
        (*sent[regions - 1 - late : regions - 1], row_matrices)
    )
    sent[regions - 1 - late : regions - 1] = held_back
    columns = [send_shifted(x, shift, regions) for x, shift in zip(sent, shifts)]

    rest = jnp.sum(variance.astype(F32), axis=(1, 2))
    sum_parts = []
    for _ in range(3):
        sum_parts.append(lax.reduce_precision(rest, 8, 7))
        rest = rest - sum_parts[-1]
    tail = jnp.zeros((TAIL, LANES), F32).at[0, : 3 * exp_dev].set(jnp.concatenate(sum_parts))
    tail = tail.astype(BF16)
    pair_exp = cores * exp_dev
    first_exp = pair_at * pair_exp

    warped = row_warp(
        columns, sources.astype(jnp.int32), row_low, row_num, row_matrices, row_blur, row_turned,
        row_key, tail, slots, cores * regions,
    )
    psf_tile = jnp.zeros((8, LANES), F32).at[:exp_dev, : 2 * RADIUS + 1].set(kernels)
    psf_tile, warped, col_start, col_frac, correlations = lax.optimization_barrier(
        (psf_tile, warped, col_start, col_frac, correlations)
    )
    rows = exchange(warped, ("core", "region"))
    other = lax.ppermute(psf_tile, "core", [(i, i ^ 1) for i in range(cores)])
    other = other[:exp_dev, : 2 * RADIUS + 1]
    col_blur = make_col_matrices(
        jnp.concatenate(
            [jnp.where(core_at == 0, kernels, other), jnp.where(core_at == 0, other, kernels)]
        )
    )
    slot_total = pair_exp * slots
    col_blocks = patch_cols // COL_BLOCK
    own_starts = lax.dynamic_slice_in_dim(col_start, first_exp, pair_exp, 0)
    own_fracs = lax.dynamic_slice_in_dim(col_frac, first_exp, pair_exp, 0)
    own_starts = own_starts.reshape(slot_total, col_blocks, COL_BLOCK)
    own_fracs = own_fracs.reshape(slot_total, col_blocks, COL_BLOCK)
    col_turned, col_key = band_tables(own_starts, lanczos_taps(own_fracs))
    col_low = jnp.clip(own_starts[:, :, 0], 0, width) // LANES * LANES
    col_end = jnp.minimum(own_starts[:, :, -1] + TAPS, width)
    col_num = jnp.maximum(col_end - col_low + COL_STEP - 1, 0) // COL_STEP
    block_at = jnp.arange(col_blocks, dtype=jnp.int32)
    col_from = jnp.min(jnp.where(col_num > 0, block_at, col_blocks), axis=1)
    col_to = jnp.max(jnp.where(col_num > 0, block_at + 1, 0), axis=1)
    col_from = jnp.minimum(col_from, col_to)
    owners = lax.dynamic_slice_in_dim(correlations, first_exp, pair_exp, 0).reshape(slot_total)
    named = owners == jnp.arange(visits, dtype=jnp.int32)[:, None]
    named = named.astype(jnp.int32)
    count = jnp.sum(named, axis=1)
    slot_ids = jnp.arange(slot_total, dtype=jnp.int32)
    rank = jnp.sum(jnp.where(slot_ids[:, None] < slot_ids, named[:, :, None], 0), axis=1)
    listed = jnp.sum(
        jnp.where((named[:, None, :] > 0) & (rank[:, None, :] == slot_ids[:, None]), slot_ids, 0),
        axis=2,
    )

    partial = col_warp(
        rows, count, listed, col_low, col_num, col_from, col_to, col_blur, col_turned, col_key,
        width, slots, visits, regions, extent * width,
    )
    tile = rows[:, -TAIL, : 3 * exp_dev].astype(F32).reshape(cores, regions, 3, exp_dev)
    tile = jnp.sum(jnp.sum(tile, axis=2), axis=1)
    own = lax.broadcasted_iota(jnp.int32, (8, LANES), 0) // cores == pair_at
    placed = jnp.zeros((8, LANES), F32).at[:, :exp_dev].set(jnp.tile(tile, (8 // cores, 1)))
    tile = butterfly_sum(jnp.where(own, placed, 0.0), "y")
    weight = 1.0 / (tile[:visits, :exp_dev].reshape(exposures) / (extent * width))
    mean_weight = jnp.mean(weight)
    pieces = exchange(
        partial.reshape((visits * regions,) + partial.shape[2:]), ("y", "core", "region")
    )
    summed = jnp.sum(
        pieces.reshape(visits // cores, patch_rows, own_cols).astype(F32), axis=0, keepdims=True
    )

    total_slots = exposures * slots
    row_cover = coverage(
        row_start.reshape(total_slots, patch_rows),
        lanczos_taps(row_frac.reshape(total_slots, patch_rows)),
        extent,
    )
    at = region_at * own_cols
    col_cover = coverage(
        lax.dynamic_slice_in_dim(col_start, at, own_cols, 2).reshape(total_slots, own_cols),
        lanczos_taps(
            lax.dynamic_slice_in_dim(col_frac, at, own_cols, 2).reshape(total_slots, own_cols)
        ),
        width,
    )
    row_cover, col_cover = lax.optimization_barrier((row_cover, col_cover))
    scale = jnp.where(
        correlations.reshape(total_slots) == visit_at, jnp.repeat(weight, slots), 0.0
    )
    weight_map = lax.dot_general(
        row_cover,
        col_cover * scale[:, None],
        (((0,), (0,)), ((), ())),
        precision=lax.Precision.HIGHEST,
        preferred_element_type=F32,
    ).reshape(1, patch_rows, own_cols)
    coadd = summed / jnp.maximum(weight_map, FLOOR_SHARE * mean_weight)
    return coadd, weight_map


def solution(mesh):
    visits, regions = mesh.devices.shape
    split = jax.sharding.Mesh(
        mesh.devices.reshape(visits // 2, 2, regions), ("y", "core", "region")
    )
    visit = ("y", "core")
    placed = (
        P(visit, "region", None),
        P(visit, "region", None),
        P(visit, None),
        P(),
        P(),
        P(),
        P(),
        P(),
    )
    return jax.shard_map(
        local,
        mesh=split,
        in_specs=placed,
        out_specs=(P(visit, None, "region"), P(visit, None, "region")),
        check_vma=False,
    )
```

```python
import functools
import math

import jax
import jax.numpy as jnp
from jax import lax
from jax.experimental import pallas as pl
from jax.experimental.pallas import tpu as pltpu
from jax.sharding import PartitionSpec as P

RADIUS = 10
TAPS = 6
SIGMAS = (1.0, 2.0, 4.0)
FLOOR_SHARE = 0.5
BF16 = jnp.bfloat16
F32 = jnp.float32

ROW_BLOCK = 128
ROW_STEP = 256
ROW_SPAN = 288
COL_BLOCK = 128
COL_STEP = 256
COL_GROUP = 18
BLUR_BLOCK = 256
BLUR_STEP = 512
BLUR_BAND = (112, 400)
LANES = 128
TAIL = 16
LIMIT = 14 * 1024 * 1024
COL_LIMIT = 56 * 1024 * 1024


def psf_kernel(coefficient):
    offsets = jnp.arange(-RADIUS, RADIUS + 1).astype(coefficient.dtype)
    sigmas = jnp.array(SIGMAS, dtype=coefficient.dtype)
    gaussians = jnp.exp(
        -(offsets[None, :] * offsets[None, :]) / (2.0 * sigmas[:, None] * sigmas[:, None])
    )
    kernel = jnp.sum(coefficient[:, :, None] * gaussians[None, :, :], axis=1)
    return kernel / jnp.sum(kernel, axis=1, keepdims=True)


def lanczos_taps(f):
    g = 1.0 - f
    third = math.pi / 3.0
    tiny = 1e-6
    a = jnp.sin(third * f)
    b = jnp.sin(third * g)
    c = a + b
    fg = f * g
    a_over_f = jnp.where(f < tiny, third, a / jnp.maximum(f, tiny))
    b_over_g = jnp.where(g < tiny, third, b / jnp.maximum(g, tiny))
    values = [
        b * fg / ((f + 2.0) * (f + 2.0)),
        -c * fg / ((f + 1.0) * (f + 1.0)),
        a_over_f * g,
        b_over_g * f,
        -c * fg / ((2.0 - f) * (2.0 - f)),
        a * fg / ((3.0 - f) * (3.0 - f)),
    ]
    total = functools.reduce(jnp.add, values)
    return [lax.reduce_precision(value / total, 8, 7) for value in values]


def coverage(starts, taps, extent):
    running = jnp.zeros(starts.shape, F32)
    for tap_at, tap in enumerate(taps):
        position = starts + tap_at
        inside = (position >= 0) & (position < extent)
        running = running + jnp.where(inside, tap, 0.0)
    return running


def band_tables(starts, taps):
    place = jnp.arange(8, dtype=jnp.int32)[:, None]
    diff = place - starts[..., None, :]
    at = diff & 7
    turned = jnp.zeros(diff.shape, F32)
    for tap_at, tap in enumerate(taps):
        turned = turned + jnp.where(at == tap_at, tap[..., None, :], 0.0)
    return turned, diff - at


def toeplitz(kernel_ref, at, rows, cols, shift):
    diff = (
        lax.broadcasted_iota(jnp.int32, (rows, cols), 0)
        - lax.broadcasted_iota(jnp.int32, (rows, cols), 1)
    )
    full = jnp.zeros((rows, cols), F32)
    for tap_at in range(2 * RADIUS + 1):
        full = jnp.where(diff == tap_at - shift, kernel_ref[at, tap_at], full)
    return full


def dot(a, b):
    return jnp.dot(a, b, preferred_element_type=F32)


def two_parts(value):
    high = value.astype(BF16)
    return high, (value - high.astype(F32)).astype(BF16)


def halves_sum(value):
    half = value.shape[0] // 2
    return value[:half] + value[half:]


def band_of(turned, key, first, groups):
    moved = key + first
    return [jnp.where(moved == -8 * g, turned, 0.0) for g in range(groups)]


def row_matrix(blur_ref, turned, key, start, extent, masked):
    last = extent - ROW_STEP
    first = jnp.minimum(start, last)
    groups = ROW_SPAN // 8
    pieces = band_of(turned, key, first - 16, groups)
    for g in range(2):
        pieces[g] = jnp.where(first > 0, pieces[g], 0.0)
        pieces[groups - 1 - g] = jnp.where(first < last, pieces[groups - 1 - g], 0.0)
    band = jnp.concatenate(pieces, axis=0).astype(BF16)
    both = halves_sum(dot(blur_ref[...], band))
    if masked:
        row = lax.broadcasted_iota(jnp.int32, both.shape, 0) + first
        both = jnp.where(row >= start, both, 0.0)
    return jnp.concatenate(two_parts(both.T), axis=0)


def row_matrices_body(extent, kernel_ref, low_ref, turned_ref, key_ref, rows_ref, blur_ref):
    high, rest = two_parts(toeplitz(kernel_ref, 0, ROW_STEP, ROW_SPAN, 16 + RADIUS))
    blur_ref[0:ROW_STEP] = high
    blur_ref[ROW_STEP : 2 * ROW_STEP] = rest

    def block(at, carry):
        rows_ref[at] = row_matrix(
            blur_ref, turned_ref[at], key_ref[at], low_ref[at], extent, False
        )
        return carry

    lax.fori_loop(0, turned_ref.shape[0], block, 0)


def make_row_matrices(kernel, low, turned, key, extent):
    blocks = turned.shape[0]
    vmem = pl.BlockSpec(memory_space=pltpu.VMEM)
    smem = pl.BlockSpec(memory_space=pltpu.SMEM)
    return pl.pallas_call(
        functools.partial(row_matrices_body, extent),
        out_shape=(
            jax.ShapeDtypeStruct((blocks, 2 * ROW_BLOCK, ROW_STEP), BF16),
            jax.ShapeDtypeStruct((2 * ROW_STEP, ROW_SPAN), BF16),
        ),
        in_specs=[smem, smem, vmem, vmem],
        out_specs=(vmem, vmem),
        compiler_params=pltpu.CompilerParams(vmem_limit_bytes=LIMIT),
        name="row_matrices",
    )(kernel, low, turned, key)


def col_matrices_body(kernel_ref, cols_ref):
    begin, end = BLUR_BAND
    for e in range(cols_ref.shape[0]):
        high, rest = two_parts(
            toeplitz(kernel_ref, e, end - begin, BLUR_BLOCK, begin - LANES + RADIUS)
        )
        cols_ref[e, 0] = high
        cols_ref[e, 1] = rest


def make_col_matrices(kernels):
    return pl.pallas_call(
        col_matrices_body,
        out_shape=jax.ShapeDtypeStruct(
            (kernels.shape[0], 2, BLUR_BAND[1] - BLUR_BAND[0], BLUR_BLOCK), BF16
        ),
        in_specs=[pl.BlockSpec(memory_space=pltpu.SMEM)],
        out_specs=pl.BlockSpec(memory_space=pltpu.VMEM),
        compiler_params=pltpu.CompilerParams(vmem_limit_bytes=COL_LIMIT),
        name="col_matrices",
    )(kernels)


def row_body(slots, low_ref, num_ref, x_ref, rows_ref, blur_ref, turned_ref, key_ref, tail_ref,
             out_ref):
    extent, width = x_ref.shape
    owners = out_ref.shape[0]
    blocks = turned_ref.shape[0] // slots
    owner_rows = blocks * ROW_BLOCK // owners
    data_rows = out_ref.shape[1] - TAIL
    for owner in range(owners):
        out_ref[owner, data_rows : data_rows + TAIL, :] = tail_ref[...]

    def times(matrix, start):
        first = pl.multiple_of(jnp.minimum(start, extent - ROW_STEP), 16)
        return halves_sum(dot(matrix, x_ref[pl.ds(first, ROW_STEP), :]))

    def block(at, carry):
        indices = [slot * blocks + at for slot in range(slots)]
        sums = [times(rows_ref[index], low_ref[index]) for index in indices]
        for slot, index in enumerate(indices):

            def more(i, total, index=index):
                start = low_ref[index] + i * ROW_STEP
                matrix = row_matrix(
                    blur_ref, turned_ref[index], key_ref[index], start, extent, True
                )
                return total + times(matrix, start)

            total = lax.fori_loop(1, num_ref[index], more, sums[slot]).astype(BF16)
            for owner in range(ROW_BLOCK // owner_rows):
                for t in range(width // LANES):
                    place = (t * slots + slot) * owner_rows
                    out_ref[
                        at * (ROW_BLOCK // owner_rows) + owner, place : place + owner_rows, :
                    ] = total[
                        owner * owner_rows : (owner + 1) * owner_rows,
                        t * LANES : (t + 1) * LANES,
                    ]
        return carry

    lax.fori_loop(0, blocks, block, 0)


def row_warp(x, low, num, matrices, blur, turned, key, tail, slots, owners):
    width = x.shape[1]
    owner_rows = turned.shape[0] // slots * ROW_BLOCK // owners
    vmem = pl.BlockSpec(memory_space=pltpu.VMEM)
    smem = pl.BlockSpec(memory_space=pltpu.SMEM)
    return pl.pallas_call(
        functools.partial(row_body, slots),
        out_shape=jax.ShapeDtypeStruct(
            (owners, width // LANES * slots * owner_rows + TAIL, LANES), BF16
        ),
        in_specs=[smem, smem] + [vmem] * 6,
        out_specs=vmem,
        compiler_params=pltpu.CompilerParams(vmem_limit_bytes=LIMIT),
        cost_estimate=pl.CostEstimate(
            flops=2_000_000_000, bytes_accessed=8 * 1024 * 1024, transcendentals=0
        ),
        name="row_warp",
    )(low, num, x, matrices, blur, turned, key, tail)


def col_body(cols, slots, pixels, count_ref, list_ref, low_ref, num_ref, from_ref, to_ref, z_hbm,
             blur_hbm, turned_hbm, key_hbm, out_ref, padded, blur, turned_ref, key_ref, tails,
             blurred, held, weight_ref, z_sems, blur_sems, table_sems):
    data_rows = z_hbm.shape[1] - TAIL
    exposures = blur_hbm.shape[0]
    sources = z_hbm.shape[0] // exposures
    tile_rows = data_rows // (cols // sources // LANES)
    rows = tile_rows // slots
    patch = pl.program_id(0)
    begin, end = BLUR_BAND

    @pl.when(patch == 0)
    def _():
        waits = []
        for e in range(exposures):
            copies = [
                pltpu.make_async_copy(
                    z_hbm.at[e * sources + s, pl.ds(0, data_rows)],
                    padded.at[e, pl.ds(tile_rows + s * data_rows, data_rows)],
                    z_sems.at[e, s],
                )
                for s in range(sources)
            ]
            copies.append(
                pltpu.make_async_copy(
                    blur_hbm.at[e], blur.at[e, :, pl.ds(begin, end - begin)], blur_sems.at[e]
                )
            )
            for copy in copies:
                copy.start()
            waits.append(copies)
        tables = [
            pltpu.make_async_copy(turned_hbm, turned_ref, table_sems.at[0]),
            pltpu.make_async_copy(key_hbm, key_ref, table_sems.at[1]),
            pltpu.make_async_copy(
                z_hbm.at[:, pl.ds(data_rows, TAIL)], tails, table_sems.at[2]
            ),
        ]
        for copy in tables:
            copy.start()
        pad = jnp.zeros((tile_rows, LANES), BF16)
        last = padded.shape[1] - tile_rows
        for e in range(exposures):
            padded[e, 0:tile_rows] = pad
            padded[e, last : last + tile_rows] = pad
            for n in range(2):
                blur[e, n, 0:begin] = jnp.zeros((begin, BLUR_BLOCK), BF16)
                blur[e, n, end:BLUR_STEP] = jnp.zeros((BLUR_STEP - end, BLUR_BLOCK), BF16)
            for j in range(slots):
                blurred[e * slots + j, :, cols : cols + COL_STEP] = jnp.zeros(
                    (rows, COL_STEP), BF16
                )
        for e in range(exposures):
            for copy in waits[e]:
                copy.wait()
            windows = jnp.concatenate(
                [
                    jnp.concatenate(
                        [
                            padded[e, t * tile_rows : (t + 1) * tile_rows]
                            for t in range(
                                b * BLUR_BLOCK // LANES, (b * BLUR_BLOCK + BLUR_STEP) // LANES
                            )
                        ],
                        axis=1,
                    )
                    for b in range(cols // BLUR_BLOCK)
                ],
                axis=0,
            )
            matched = (dot(windows, blur[e, 0]) + dot(windows, blur[e, 1])).astype(BF16)
            for b in range(cols // BLUR_BLOCK):
                for j in range(slots):
                    at = (b * slots + j) * rows
                    span = slice(b * BLUR_BLOCK, (b + 1) * BLUR_BLOCK)
                    blurred[e * slots + j, :, span] = matched[at : at + rows]
        for copy in tables:
            copy.wait()
        sums = jnp.sum(tails[...].astype(F32), axis=1)
        cores = 2
        visit_exp = exposures // cores
        lane = lax.broadcasted_iota(jnp.int32, (1, LANES), 1)
        for core in range(cores):
            per_core = sums.shape[0] // cores
            total = jnp.sum(
                sums[core * per_core : (core + 1) * per_core], axis=0, keepdims=True
            )
            for e in range(visit_exp):
                variance = jnp.sum(
                    jnp.where((lane < 3 * visit_exp) & (lane % visit_exp == e), total, 0.0)
                )
                for j in range(slots):
                    weight_ref[(core * visit_exp + e) * slots + j] = 1.0 / (variance / pixels)

    held[...] = jnp.zeros(held.shape, F32)

    blocks = turned_ref.shape[1]

    def part(slot, b, n):
        first = pl.multiple_of(jnp.minimum(low_ref[slot, b] + n * COL_STEP, cols), LANES)
        band = band_of(turned_ref[slot, b], key_ref[slot, b], first, COL_STEP // 8)
        band = jnp.concatenate(band, axis=0).astype(BF16)
        return dot(blurred[slot, :, pl.ds(first, COL_STEP)], band)

    def add_slot(i, carry):
        slot = list_ref[patch, i]
        begin, end = from_ref[slot], to_ref[slot]

        def add_group(c, carry):
            at = begin + c * COL_GROUP
            spots = [jnp.minimum(at + h, blocks - 1) for h in range(COL_GROUP)]
            weights = [jnp.where(at + h < end, weight_ref[slot], 0.0) for h in range(COL_GROUP)]

            def add_parts(n):
                sums = [part(slot, b, n) for b in spots]
                for b, weight, total in zip(spots, weights, sums):
                    span = pl.ds(pl.multiple_of(b * COL_BLOCK, COL_BLOCK), COL_BLOCK)
                    held[:, span] += weight * total

            add_parts(0)
            most = num_ref[slot, spots[0]]
            for b in spots[1:]:
                most = jnp.maximum(most, num_ref[slot, b])

            def more(n, carry):
                add_parts(n)
                return carry

            lax.fori_loop(1, most, more, 0)
            return carry

        steps = (end - begin + COL_GROUP - 1) // COL_GROUP
        return lax.fori_loop(0, steps, add_group, carry)

    lax.fori_loop(0, count_ref[patch], add_slot, 0)
    own_cols = out_ref.shape[3]
    for owner in range(out_ref.shape[1]):
        out_ref[0, owner] = held[:, owner * own_cols : (owner + 1) * own_cols].astype(BF16)


def col_warp(z, count, listed, low, num, begin, end, blur, turned, key, cols, slots, patches,
             owners, pixels):
    slot_total, blocks = turned.shape[:2]
    exposures = blur.shape[0]
    sources = z.shape[0] // exposures
    tile_rows = (z.shape[1] - TAIL) // (cols // sources // LANES)
    rows = tile_rows // slots
    own_cols = blocks * COL_BLOCK // owners
    smem = pl.BlockSpec(memory_space=pltpu.SMEM)
    return pl.pallas_call(
        functools.partial(col_body, cols, slots, pixels),
        out_shape=jax.ShapeDtypeStruct((patches, owners, rows, own_cols), BF16),
        grid=(patches,),
        in_specs=[smem] * 6 + [pl.BlockSpec(memory_space=pl.ANY)] * 4,
        out_specs=pl.BlockSpec((1, owners, rows, own_cols), lambda k: (k, 0, 0, 0)),
        scratch_shapes=[
            pltpu.VMEM((exposures, (cols // LANES + 2) * tile_rows, LANES), BF16),
            pltpu.VMEM((exposures, 2, BLUR_STEP, BLUR_BLOCK), BF16),
            pltpu.VMEM(turned.shape, F32),
            pltpu.VMEM(key.shape, jnp.int32),
            pltpu.VMEM((z.shape[0], TAIL, LANES), BF16),
            pltpu.VMEM((slot_total, rows, cols + COL_STEP), BF16),
            pltpu.VMEM((rows, owners * own_cols), F32),
            pltpu.SMEM((slot_total,), F32),
            pltpu.SemaphoreType.DMA((exposures, sources)),
            pltpu.SemaphoreType.DMA((exposures,)),
            pltpu.SemaphoreType.DMA((3,)),
        ],
        compiler_params=pltpu.CompilerParams(
            dimension_semantics=("arbitrary",), vmem_limit_bytes=COL_LIMIT
        ),
        cost_estimate=pl.CostEstimate(
            flops=8_000_000_000, bytes_accessed=16 * 1024 * 1024, transcendentals=0
        ),
        name="col_warp",
    )(count, listed, low, num, begin, end, z, blur, turned, key)


def split_body(parts, image_ref, out_ref, held, in_sems, out_sems):
    total, _, width = out_ref.shape
    reads = [
        pltpu.make_async_copy(
            image_ref.at[at // parts, :, pl.ds(at % parts * width, width)],
            held.at[at],
            in_sems.at[at],
        )
        for at in range(total)
    ]
    writes = [
        pltpu.make_async_copy(held.at[at], out_ref.at[at], out_sems.at[at])
        for at in range(total)
    ]
    for read in reads:
        read.start()
    for read, write in zip(reads, writes):
        read.wait()
        write.start()
    for write in writes:
        write.wait()


def split_columns(image, parts):
    exposures, height, width = image.shape
    total = exposures * parts
    shape = (total, height, width // parts)
    return pl.pallas_call(
        functools.partial(split_body, parts),
        out_shape=jax.ShapeDtypeStruct(shape, image.dtype),
        in_specs=[pl.BlockSpec(memory_space=pl.ANY)],
        out_specs=pl.BlockSpec(memory_space=pl.ANY),
        scratch_shapes=[
            pltpu.VMEM(shape, image.dtype),
            pltpu.SemaphoreType.DMA((total,)),
            pltpu.SemaphoreType.DMA((total,)),
        ],
        compiler_params=pltpu.CompilerParams(vmem_limit_bytes=COL_LIMIT),
        name="split_columns",
    )(image)


def butterfly_sum(x, axis):
    size = lax.axis_size(axis)
    step = 1
    while step < size:
        x = x + lax.ppermute(x, axis, [(i, i ^ step) for i in range(size)])
        step *= 2
    return x


def local(image, variance, psf_coef, correlations, row_start, row_frac, col_start, col_frac):
    exp_dev, height, width = image.shape
    exposures, slots = correlations.shape
    patch_rows = row_start.shape[2]
    patch_cols = col_start.shape[2]
    cores = lax.axis_size("core")
    visits = lax.axis_size("y") * cores
    regions = lax.axis_size("region")
    extent = height * regions
    parts = regions // exp_dev
    part_cols = width // parts
    own_cols = patch_cols // regions
    pair_at = lax.axis_index("y")
    core_at = lax.axis_index("core")
    visit_at = pair_at * cores + core_at
    region_at = lax.axis_index("region")

    def exchange(x, axis):
        return lax.all_to_all(x, axis, split_axis=0, concat_axis=0, tiled=True)

    sent = split_columns(image, parts)
    (sent, variance, psf_coef, row_start, row_frac, col_start, col_frac) = lax.optimization_barrier(
        (sent, variance, psf_coef, row_start, row_frac, col_start, col_frac)
    )
    columns = exchange(sent, "region").reshape(extent, part_cols)

    kernels = psf_kernel(psf_coef)

    own_exp = region_at // parts
    at_exp = visit_at * exp_dev + own_exp
    blocks = slots * patch_rows // ROW_BLOCK
    starts = lax.dynamic_index_in_dim(row_start, at_exp, 0, keepdims=False)
    fracs = lax.dynamic_index_in_dim(row_frac, at_exp, 0, keepdims=False)
    starts = starts.reshape(blocks, ROW_BLOCK)
    row_turned, row_key = band_tables(starts, lanczos_taps(fracs.reshape(blocks, ROW_BLOCK)))
    row_low = jnp.clip(starts[:, 0] - RADIUS, 0, extent - ROW_STEP) // 16 * 16
    row_end = jnp.minimum(starts[:, -1] + TAPS + RADIUS, extent)
    row_num = jnp.maximum(row_end - row_low + ROW_STEP - 1, 0) // ROW_STEP
    row_matrices, row_blur = make_row_matrices(
        lax.dynamic_slice_in_dim(kernels, own_exp, 1, 0), row_low, row_turned, row_key, extent
    )

    rest = jnp.sum(variance.astype(F32), axis=(1, 2))
    sum_parts = []
    for _ in range(3):
        sum_parts.append(lax.reduce_precision(rest, 8, 7))
        rest = rest - sum_parts[-1]
    tail = jnp.zeros((TAIL, LANES), F32).at[0, : 3 * exp_dev].set(jnp.concatenate(sum_parts))
    tail = tail.astype(BF16)
    pair_exp = cores * exp_dev
    first_exp = pair_at * pair_exp

    slot_total = pair_exp * slots
    col_blocks = patch_cols // COL_BLOCK
    own_starts = lax.dynamic_slice_in_dim(col_start, first_exp, pair_exp, 0)
    own_fracs = lax.dynamic_slice_in_dim(col_frac, first_exp, pair_exp, 0)
    own_starts = own_starts.reshape(slot_total, col_blocks, COL_BLOCK)
    own_fracs = own_fracs.reshape(slot_total, col_blocks, COL_BLOCK)
    col_turned, col_key = band_tables(own_starts, lanczos_taps(own_fracs))
    col_low = jnp.clip(own_starts[:, :, 0], 0, width) // LANES * LANES
    col_end = jnp.minimum(own_starts[:, :, -1] + TAPS, width)
    col_num = jnp.maximum(col_end - col_low + COL_STEP - 1, 0) // COL_STEP
    block_at = jnp.arange(col_blocks, dtype=jnp.int32)
    col_from = jnp.min(jnp.where(col_num > 0, block_at, col_blocks), axis=1)
    col_to = jnp.max(jnp.where(col_num > 0, block_at + 1, 0), axis=1)
    col_from = jnp.minimum(col_from, col_to)
    owners = lax.dynamic_slice_in_dim(correlations, first_exp, pair_exp, 0).reshape(slot_total)
    named = owners == jnp.arange(visits, dtype=jnp.int32)[:, None]
    named = named.astype(jnp.int32)
    count = jnp.sum(named, axis=1)
    slot_ids = jnp.arange(slot_total, dtype=jnp.int32)
    rank = jnp.sum(jnp.where(slot_ids[:, None] < slot_ids, named[:, :, None], 0), axis=1)
    listed = jnp.sum(
        jnp.where((named[:, None, :] > 0) & (rank[:, None, :] == slot_ids[:, None]), slot_ids, 0),
        axis=2,
    )

    warped = row_warp(
        columns, row_low, row_num, row_matrices, row_blur, row_turned, row_key, tail, slots,
        cores * regions,
    )
    psf_tile = jnp.zeros((8, LANES), F32).at[:exp_dev, : 2 * RADIUS + 1].set(kernels)
    psf_tile, warped = lax.optimization_barrier((psf_tile, warped))
    rows = exchange(warped, ("core", "region"))
    other = lax.ppermute(psf_tile, "core", [(i, i ^ 1) for i in range(cores)])
    other = other[:exp_dev, : 2 * RADIUS + 1]
    col_blur = make_col_matrices(
        jnp.concatenate(
            [jnp.where(core_at == 0, kernels, other), jnp.where(core_at == 0, other, kernels)]
        )
    )
    partial = col_warp(
        rows, count, listed, col_low, col_num, col_from, col_to, col_blur, col_turned, col_key,
        width, slots, visits, regions, extent * width,
    )
    tile = rows[:, -TAIL, : 3 * exp_dev].astype(F32).reshape(cores, regions, 3, exp_dev)
    tile = jnp.sum(jnp.sum(tile, axis=2), axis=1)
    own = lax.broadcasted_iota(jnp.int32, (8, LANES), 0) // cores == pair_at
    placed = jnp.zeros((8, LANES), F32).at[:, :exp_dev].set(jnp.tile(tile, (8 // cores, 1)))
    tile = butterfly_sum(jnp.where(own, placed, 0.0), "y")
    weight = 1.0 / (tile[:visits, :exp_dev].reshape(exposures) / (extent * width))
    mean_weight = jnp.mean(weight)
    pieces = exchange(
        partial.reshape((visits * regions,) + partial.shape[2:]), ("y", "core", "region")
    )
    summed = jnp.sum(
        pieces.reshape(visits // cores, patch_rows, own_cols).astype(F32), axis=0, keepdims=True
    )

    total_slots = exposures * slots
    row_cover = coverage(
        row_start.reshape(total_slots, patch_rows),
        lanczos_taps(row_frac.reshape(total_slots, patch_rows)),
        extent,
    )
    at = region_at * own_cols
    col_cover = coverage(
        lax.dynamic_slice_in_dim(col_start, at, own_cols, 2).reshape(total_slots, own_cols),
        lanczos_taps(
            lax.dynamic_slice_in_dim(col_frac, at, own_cols, 2).reshape(total_slots, own_cols)
        ),
        width,
    )
    scale = jnp.where(
        correlations.reshape(total_slots) == visit_at, jnp.repeat(weight, slots), 0.0
    )
    weight_map = lax.dot_general(
        row_cover,
        col_cover * scale[:, None],
        (((0,), (0,)), ((), ())),
        precision=lax.Precision.HIGHEST,
        preferred_element_type=F32,
    ).reshape(1, patch_rows, own_cols)
    coadd = summed / jnp.maximum(weight_map, FLOOR_SHARE * mean_weight)
    return coadd, weight_map


def solution(mesh):
    visits, regions = mesh.devices.shape
    split = jax.sharding.Mesh(
        mesh.devices.reshape(visits // 2, 2, regions), ("y", "core", "region")
    )
    visit = ("y", "core")
    placed = (
        P(visit, "region", None),
        P(visit, "region", None),
        P(visit, None),
        P(),
        P(),
        P(),
        P(),
        P(),
    )
    return jax.shard_map(
        local,
        mesh=split,
        in_specs=placed,
        out_specs=(P(visit, None, "region"), P(visit, None, "region")),
        check_vma=False,
    )
```

```python
import functools
import math

import jax
import jax.numpy as jnp
from jax import lax
from jax.experimental import pallas as pl
from jax.experimental.pallas import tpu as pltpu
from jax.sharding import PartitionSpec as P

RADIUS = 10
TAPS = 6
SIGMAS = (1.0, 2.0, 4.0)
FLOOR_SHARE = 0.5
BF16 = jnp.bfloat16
F32 = jnp.float32

ROW_BLOCK = 128
ROW_STEP = 256
ROW_SPAN = 288
COL_BLOCK = 128
COL_STEP = 256
COL_GROUP = 18
BLUR_BLOCK = 256
BLUR_STEP = 512
BLUR_BAND = (112, 400)
LANES = 128
TAIL = 16
LIMIT = 14 * 1024 * 1024
COL_LIMIT = 56 * 1024 * 1024


def psf_kernel(coefficient):
    offsets = jnp.arange(-RADIUS, RADIUS + 1).astype(coefficient.dtype)
    sigmas = jnp.array(SIGMAS, dtype=coefficient.dtype)
    gaussians = jnp.exp(
        -(offsets[None, :] * offsets[None, :]) / (2.0 * sigmas[:, None] * sigmas[:, None])
    )
    kernel = jnp.sum(coefficient[:, :, None] * gaussians[None, :, :], axis=1)
    return kernel / jnp.sum(kernel, axis=1, keepdims=True)


def lanczos_taps(f):
    g = 1.0 - f
    third = math.pi / 3.0
    tiny = 1e-6
    a = jnp.sin(third * f)
    b = jnp.sin(third * g)
    c = a + b
    fg = f * g
    a_over_f = jnp.where(f < tiny, third, a / jnp.maximum(f, tiny))
    b_over_g = jnp.where(g < tiny, third, b / jnp.maximum(g, tiny))
    values = [
        b * fg / ((f + 2.0) * (f + 2.0)),
        -c * fg / ((f + 1.0) * (f + 1.0)),
        a_over_f * g,
        b_over_g * f,
        -c * fg / ((2.0 - f) * (2.0 - f)),
        a * fg / ((3.0 - f) * (3.0 - f)),
    ]
    total = functools.reduce(jnp.add, values)
    return [lax.reduce_precision(value / total, 8, 7) for value in values]


def coverage(starts, taps, extent):
    running = jnp.zeros(starts.shape, F32)
    for tap_at, tap in enumerate(taps):
        position = starts + tap_at
        inside = (position >= 0) & (position < extent)
        running = running + jnp.where(inside, tap, 0.0)
    return running


def band_tables(starts, taps):
    place = jnp.arange(8, dtype=jnp.int32)[:, None]
    diff = place - starts[..., None, :]
    at = diff & 7
    turned = jnp.zeros(diff.shape, F32)
    for tap_at, tap in enumerate(taps):
        turned = turned + jnp.where(at == tap_at, tap[..., None, :], 0.0)
    return turned, diff - at


def toeplitz(kernel_ref, at, rows, cols, shift):
    diff = (
        lax.broadcasted_iota(jnp.int32, (rows, cols), 0)
        - lax.broadcasted_iota(jnp.int32, (rows, cols), 1)
    )
    full = jnp.zeros((rows, cols), F32)
    for tap_at in range(2 * RADIUS + 1):
        full = jnp.where(diff == tap_at - shift, kernel_ref[at, tap_at], full)
    return full


def dot(a, b):
    return jnp.dot(a, b, preferred_element_type=F32)


def two_parts(value):
    high = value.astype(BF16)
    return high, (value - high.astype(F32)).astype(BF16)


def halves_sum(value):
    half = value.shape[0] // 2
    return value[:half] + value[half:]


def band_of(turned, key, first, groups):
    moved = key + first
    return [jnp.where(moved == -8 * g, turned, 0.0) for g in range(groups)]


def row_matrix(blur_ref, turned, key, start, extent, masked):
    last = extent - ROW_STEP
    first = jnp.minimum(start, last)
    groups = ROW_SPAN // 8
    pieces = band_of(turned, key, first - 16, groups)
    for g in range(2):
        pieces[g] = jnp.where(first > 0, pieces[g], 0.0)
        pieces[groups - 1 - g] = jnp.where(first < last, pieces[groups - 1 - g], 0.0)
    band = jnp.concatenate(pieces, axis=0).astype(BF16)
    both = halves_sum(dot(blur_ref[...], band))
    if masked:
        row = lax.broadcasted_iota(jnp.int32, both.shape, 0) + first
        both = jnp.where(row >= start, both, 0.0)
    return jnp.concatenate(two_parts(both.T), axis=0)


def row_matrices_body(extent, kernel_ref, low_ref, turned_ref, key_ref, rows_ref, blur_ref):
    high, rest = two_parts(toeplitz(kernel_ref, 0, ROW_STEP, ROW_SPAN, 16 + RADIUS))
    blur_ref[0:ROW_STEP] = high
    blur_ref[ROW_STEP : 2 * ROW_STEP] = rest

    def block(at, carry):
        rows_ref[at] = row_matrix(
            blur_ref, turned_ref[at], key_ref[at], low_ref[at], extent, False
        )
        return carry

    lax.fori_loop(0, turned_ref.shape[0], block, 0)


def make_row_matrices(kernel, low, turned, key, extent):
    blocks = turned.shape[0]
    vmem = pl.BlockSpec(memory_space=pltpu.VMEM)
    smem = pl.BlockSpec(memory_space=pltpu.SMEM)
    return pl.pallas_call(
        functools.partial(row_matrices_body, extent),
        out_shape=(
            jax.ShapeDtypeStruct((blocks, 2 * ROW_BLOCK, ROW_STEP), BF16),
            jax.ShapeDtypeStruct((2 * ROW_STEP, ROW_SPAN), BF16),
        ),
        in_specs=[smem, smem, vmem, vmem],
        out_specs=(vmem, vmem),
        compiler_params=pltpu.CompilerParams(vmem_limit_bytes=LIMIT),
        name="row_matrices",
    )(kernel, low, turned, key)


def col_matrices_body(kernel_ref, cols_ref):
    begin, end = BLUR_BAND
    for e in range(cols_ref.shape[0]):
        high, rest = two_parts(
            toeplitz(kernel_ref, e, end - begin, BLUR_BLOCK, begin - LANES + RADIUS)
        )
        cols_ref[e, 0] = high
        cols_ref[e, 1] = rest


def make_col_matrices(kernels):
    return pl.pallas_call(
        col_matrices_body,
        out_shape=jax.ShapeDtypeStruct(
            (kernels.shape[0], 2, BLUR_BAND[1] - BLUR_BAND[0], BLUR_BLOCK), BF16
        ),
        in_specs=[pl.BlockSpec(memory_space=pltpu.SMEM)],
        out_specs=pl.BlockSpec(memory_space=pltpu.VMEM),
        compiler_params=pltpu.CompilerParams(vmem_limit_bytes=COL_LIMIT),
        name="col_matrices",
    )(kernels)


def row_body(slots, low_ref, num_ref, x_ref, rows_ref, blur_ref, turned_ref, key_ref, tail_ref,
             out_ref):
    extent, width = x_ref.shape
    owners = out_ref.shape[0]
    blocks = turned_ref.shape[0] // slots
    owner_rows = blocks * ROW_BLOCK // owners
    data_rows = out_ref.shape[1] - TAIL
    for owner in range(owners):
        out_ref[owner, data_rows : data_rows + TAIL, :] = tail_ref[...]

    def times(matrix, start):
        first = pl.multiple_of(jnp.minimum(start, extent - ROW_STEP), 16)
        return halves_sum(dot(matrix, x_ref[pl.ds(first, ROW_STEP), :]))

    def block(at, carry):
        indices = [slot * blocks + at for slot in range(slots)]
        sums = [times(rows_ref[index], low_ref[index]) for index in indices]
        for slot, index in enumerate(indices):

            def more(i, total, index=index):
                start = low_ref[index] + i * ROW_STEP
                matrix = row_matrix(
                    blur_ref, turned_ref[index], key_ref[index], start, extent, True
                )
                return total + times(matrix, start)

            total = lax.fori_loop(1, num_ref[index], more, sums[slot]).astype(BF16)
            for owner in range(ROW_BLOCK // owner_rows):
                for t in range(width // LANES):
                    place = (t * slots + slot) * owner_rows
                    out_ref[
                        at * (ROW_BLOCK // owner_rows) + owner, place : place + owner_rows, :
                    ] = total[
                        owner * owner_rows : (owner + 1) * owner_rows,
                        t * LANES : (t + 1) * LANES,
                    ]
        return carry

    lax.fori_loop(0, blocks, block, 0)


def row_warp(x, low, num, matrices, blur, turned, key, tail, slots, owners):
    width = x.shape[1]
    owner_rows = turned.shape[0] // slots * ROW_BLOCK // owners
    vmem = pl.BlockSpec(memory_space=pltpu.VMEM)
    smem = pl.BlockSpec(memory_space=pltpu.SMEM)
    return pl.pallas_call(
        functools.partial(row_body, slots),
        out_shape=jax.ShapeDtypeStruct(
            (owners, width // LANES * slots * owner_rows + TAIL, LANES), BF16
        ),
        in_specs=[smem, smem] + [vmem] * 6,
        out_specs=vmem,
        compiler_params=pltpu.CompilerParams(vmem_limit_bytes=LIMIT),
        cost_estimate=pl.CostEstimate(
            flops=2_000_000_000, bytes_accessed=8 * 1024 * 1024, transcendentals=0
        ),
        name="row_warp",
    )(low, num, x, matrices, blur, turned, key, tail)


def col_body(cols, slots, pixels, count_ref, list_ref, low_ref, num_ref, from_ref, to_ref, z_hbm,
             blur_hbm, turned_hbm, key_hbm, out_ref, padded, blur, turned_ref, key_ref, tails,
             blurred, held, weight_ref, z_sems, blur_sems, table_sems):
    data_rows = z_hbm.shape[1] - TAIL
    exposures = blur_hbm.shape[0]
    sources = z_hbm.shape[0] // exposures
    tile_rows = data_rows // (cols // sources // LANES)
    rows = tile_rows // slots
    patch = pl.program_id(0)
    begin, end = BLUR_BAND

    @pl.when(patch == 0)
    def _():
        waits = []
        for e in range(exposures):
            copies = [
                pltpu.make_async_copy(
                    z_hbm.at[e * sources + s, pl.ds(0, data_rows)],
                    padded.at[e, pl.ds(tile_rows + s * data_rows, data_rows)],
                    z_sems.at[e, s],
                )
                for s in range(sources)
            ]
            copies.append(
                pltpu.make_async_copy(
                    blur_hbm.at[e], blur.at[e, :, pl.ds(begin, end - begin)], blur_sems.at[e]
                )
            )
            for copy in copies:
                copy.start()
            waits.append(copies)
        tables = [
            pltpu.make_async_copy(turned_hbm, turned_ref, table_sems.at[0]),
            pltpu.make_async_copy(key_hbm, key_ref, table_sems.at[1]),
            pltpu.make_async_copy(
                z_hbm.at[:, pl.ds(data_rows, TAIL)], tails, table_sems.at[2]
            ),
        ]
        for copy in tables:
            copy.start()
        pad = jnp.zeros((tile_rows, LANES), BF16)
        last = padded.shape[1] - tile_rows
        for e in range(exposures):
            padded[e, 0:tile_rows] = pad
            padded[e, last : last + tile_rows] = pad
            for n in range(2):
                blur[e, n, 0:begin] = jnp.zeros((begin, BLUR_BLOCK), BF16)
                blur[e, n, end:BLUR_STEP] = jnp.zeros((BLUR_STEP - end, BLUR_BLOCK), BF16)
            for j in range(slots):
                blurred[e * slots + j, :, cols : cols + COL_STEP] = jnp.zeros(
                    (rows, COL_STEP), BF16
                )
        for e in range(exposures):
            for copy in waits[e]:
                copy.wait()
            windows = jnp.concatenate(
                [
                    jnp.concatenate(
                        [
                            padded[e, t * tile_rows : (t + 1) * tile_rows]
                            for t in range(
                                b * BLUR_BLOCK // LANES, (b * BLUR_BLOCK + BLUR_STEP) // LANES
                            )
                        ],
                        axis=1,
                    )
                    for b in range(cols // BLUR_BLOCK)
                ],
                axis=0,
            )
            matched = (dot(windows, blur[e, 0]) + dot(windows, blur[e, 1])).astype(BF16)
            for b in range(cols // BLUR_BLOCK):
                for j in range(slots):
                    at = (b * slots + j) * rows
                    span = slice(b * BLUR_BLOCK, (b + 1) * BLUR_BLOCK)
                    blurred[e * slots + j, :, span] = matched[at : at + rows]
        for copy in tables:
            copy.wait()
        sums = jnp.sum(tails[...].astype(F32), axis=1)
        cores = 2
        visit_exp = exposures // cores
        lane = lax.broadcasted_iota(jnp.int32, (1, LANES), 1)
        for core in range(cores):
            per_core = sums.shape[0] // cores
            total = jnp.sum(
                sums[core * per_core : (core + 1) * per_core], axis=0, keepdims=True
            )
            for e in range(visit_exp):
                variance = jnp.sum(
                    jnp.where((lane < 3 * visit_exp) & (lane % visit_exp == e), total, 0.0)
                )
                for j in range(slots):
                    weight_ref[(core * visit_exp + e) * slots + j] = 1.0 / (variance / pixels)

    held[...] = jnp.zeros(held.shape, F32)

    blocks = turned_ref.shape[1]

    def part(slot, b, n):
        first = pl.multiple_of(jnp.minimum(low_ref[slot, b] + n * COL_STEP, cols), LANES)
        band = band_of(turned_ref[slot, b], key_ref[slot, b], first, COL_STEP // 8)
        band = jnp.concatenate(band, axis=0).astype(BF16)
        return dot(blurred[slot, :, pl.ds(first, COL_STEP)], band)

    def add_slot(i, carry):
        slot = list_ref[patch, i]
        begin, end = from_ref[slot], to_ref[slot]

        def add_group(c, carry):
            at = begin + c * COL_GROUP
            spots = [jnp.minimum(at + h, blocks - 1) for h in range(COL_GROUP)]
            weights = [jnp.where(at + h < end, weight_ref[slot], 0.0) for h in range(COL_GROUP)]

            def add_parts(n):
                sums = [part(slot, b, n) for b in spots]
                for b, weight, total in zip(spots, weights, sums):
                    span = pl.ds(pl.multiple_of(b * COL_BLOCK, COL_BLOCK), COL_BLOCK)
                    held[:, span] += weight * total

            add_parts(0)
            most = num_ref[slot, spots[0]]
            for b in spots[1:]:
                most = jnp.maximum(most, num_ref[slot, b])

            def more(n, carry):
                add_parts(n)
                return carry

            lax.fori_loop(1, most, more, 0)
            return carry

        steps = (end - begin + COL_GROUP - 1) // COL_GROUP
        return lax.fori_loop(0, steps, add_group, carry)

    lax.fori_loop(0, count_ref[patch], add_slot, 0)
    own_cols = out_ref.shape[3]
    for owner in range(out_ref.shape[1]):
        out_ref[0, owner] = held[:, owner * own_cols : (owner + 1) * own_cols].astype(BF16)


def col_warp(z, count, listed, low, num, begin, end, blur, turned, key, cols, slots, patches,
             owners, pixels):
    slot_total, blocks = turned.shape[:2]
    exposures = blur.shape[0]
    sources = z.shape[0] // exposures
    tile_rows = (z.shape[1] - TAIL) // (cols // sources // LANES)
    rows = tile_rows // slots
    own_cols = blocks * COL_BLOCK // owners
    smem = pl.BlockSpec(memory_space=pltpu.SMEM)
    return pl.pallas_call(
        functools.partial(col_body, cols, slots, pixels),
        out_shape=jax.ShapeDtypeStruct((patches, owners, rows, own_cols), BF16),
        grid=(patches,),
        in_specs=[smem] * 6 + [pl.BlockSpec(memory_space=pl.ANY)] * 4,
        out_specs=pl.BlockSpec((1, owners, rows, own_cols), lambda k: (k, 0, 0, 0)),
        scratch_shapes=[
            pltpu.VMEM((exposures, (cols // LANES + 2) * tile_rows, LANES), BF16),
            pltpu.VMEM((exposures, 2, BLUR_STEP, BLUR_BLOCK), BF16),
            pltpu.VMEM(turned.shape, F32),
            pltpu.VMEM(key.shape, jnp.int32),
            pltpu.VMEM((z.shape[0], TAIL, LANES), BF16),
            pltpu.VMEM((slot_total, rows, cols + COL_STEP), BF16),
            pltpu.VMEM((rows, owners * own_cols), F32),
            pltpu.SMEM((slot_total,), F32),
            pltpu.SemaphoreType.DMA((exposures, sources)),
            pltpu.SemaphoreType.DMA((exposures,)),
            pltpu.SemaphoreType.DMA((3,)),
        ],
        compiler_params=pltpu.CompilerParams(
            dimension_semantics=("arbitrary",), vmem_limit_bytes=COL_LIMIT
        ),
        cost_estimate=pl.CostEstimate(
            flops=8_000_000_000, bytes_accessed=16 * 1024 * 1024, transcendentals=0
        ),
        name="col_warp",
    )(count, listed, low, num, begin, end, z, blur, turned, key)


def split_body(parts, image_ref, out_ref, held, in_sems, out_sems):
    total, _, width = out_ref.shape
    reads = [
        pltpu.make_async_copy(
            image_ref.at[at // parts, :, pl.ds(at % parts * width, width)],
            held.at[at],
            in_sems.at[at],
        )
        for at in range(total)
    ]
    writes = [
        pltpu.make_async_copy(held.at[at], out_ref.at[at], out_sems.at[at])
        for at in range(total)
    ]
    for read in reads:
        read.start()
    for read, write in zip(reads, writes):
        read.wait()
        write.start()
    for write in writes:
        write.wait()


def split_columns(image, parts):
    exposures, height, width = image.shape
    total = exposures * parts
    shape = (total, height, width // parts)
    return pl.pallas_call(
        functools.partial(split_body, parts),
        out_shape=jax.ShapeDtypeStruct(shape, image.dtype),
        in_specs=[pl.BlockSpec(memory_space=pl.ANY)],
        out_specs=pl.BlockSpec(memory_space=pl.ANY),
        scratch_shapes=[
            pltpu.VMEM(shape, image.dtype),
            pltpu.SemaphoreType.DMA((total,)),
            pltpu.SemaphoreType.DMA((total,)),
        ],
        compiler_params=pltpu.CompilerParams(vmem_limit_bytes=COL_LIMIT),
        name="split_columns",
    )(image)


def ring_sum(x, axis):
    size = lax.axis_size(axis)
    return x + sum(
        lax.ppermute(x, axis, [(i, (i + step) % size) for i in range(size)])
        for step in range(1, size)
    )


def local(image, variance, psf_coef, correlations, row_start, row_frac, col_start, col_frac):
    exp_dev, height, width = image.shape
    exposures, slots = correlations.shape
    patch_rows = row_start.shape[2]
    patch_cols = col_start.shape[2]
    cores = lax.axis_size("core")
    visits = lax.axis_size("y") * cores
    regions = lax.axis_size("region")
    extent = height * regions
    parts = regions // exp_dev
    part_cols = width // parts
    own_cols = patch_cols // regions
    pair_at = lax.axis_index("y")
    core_at = lax.axis_index("core")
    visit_at = pair_at * cores + core_at
    region_at = lax.axis_index("region")

    def exchange(x, axis):
        return lax.all_to_all(x, axis, split_axis=0, concat_axis=0, tiled=True)

    sent = split_columns(image, parts)
    (sent, variance, psf_coef, row_start, row_frac, col_start, col_frac) = lax.optimization_barrier(
        (sent, variance, psf_coef, row_start, row_frac, col_start, col_frac)
    )
    columns = exchange(sent, "region").reshape(extent, part_cols)

    kernels = psf_kernel(psf_coef)

    own_exp = region_at // parts
    at_exp = visit_at * exp_dev + own_exp
    blocks = slots * patch_rows // ROW_BLOCK
    starts = lax.dynamic_index_in_dim(row_start, at_exp, 0, keepdims=False)
    fracs = lax.dynamic_index_in_dim(row_frac, at_exp, 0, keepdims=False)
    starts = starts.reshape(blocks, ROW_BLOCK)
    row_turned, row_key = band_tables(starts, lanczos_taps(fracs.reshape(blocks, ROW_BLOCK)))
    row_low = jnp.clip(starts[:, 0] - RADIUS, 0, extent - ROW_STEP) // 16 * 16
    row_end = jnp.minimum(starts[:, -1] + TAPS + RADIUS, extent)
    row_num = jnp.maximum(row_end - row_low + ROW_STEP - 1, 0) // ROW_STEP
    row_matrices, row_blur = make_row_matrices(
        lax.dynamic_slice_in_dim(kernels, own_exp, 1, 0), row_low, row_turned, row_key, extent
    )

    rest = jnp.sum(variance.astype(F32), axis=(1, 2))
    sum_parts = []
    for _ in range(3):
        sum_parts.append(lax.reduce_precision(rest, 8, 7))
        rest = rest - sum_parts[-1]
    tail = jnp.zeros((TAIL, LANES), F32).at[0, : 3 * exp_dev].set(jnp.concatenate(sum_parts))
    tail = tail.astype(BF16)
    pair_exp = cores * exp_dev
    first_exp = pair_at * pair_exp

    slot_total = pair_exp * slots
    col_blocks = patch_cols // COL_BLOCK
    own_starts = lax.dynamic_slice_in_dim(col_start, first_exp, pair_exp, 0)
    own_fracs = lax.dynamic_slice_in_dim(col_frac, first_exp, pair_exp, 0)
    own_starts = own_starts.reshape(slot_total, col_blocks, COL_BLOCK)
    own_fracs = own_fracs.reshape(slot_total, col_blocks, COL_BLOCK)
    col_turned, col_key = band_tables(own_starts, lanczos_taps(own_fracs))
    col_low = jnp.clip(own_starts[:, :, 0], 0, width) // LANES * LANES
    col_end = jnp.minimum(own_starts[:, :, -1] + TAPS, width)
    col_num = jnp.maximum(col_end - col_low + COL_STEP - 1, 0) // COL_STEP
    block_at = jnp.arange(col_blocks, dtype=jnp.int32)
    col_from = jnp.min(jnp.where(col_num > 0, block_at, col_blocks), axis=1)
    col_to = jnp.max(jnp.where(col_num > 0, block_at + 1, 0), axis=1)
    col_from = jnp.minimum(col_from, col_to)
    owners = lax.dynamic_slice_in_dim(correlations, first_exp, pair_exp, 0).reshape(slot_total)
    named = owners == jnp.arange(visits, dtype=jnp.int32)[:, None]
    named = named.astype(jnp.int32)
    count = jnp.sum(named, axis=1)
    slot_ids = jnp.arange(slot_total, dtype=jnp.int32)
    rank = jnp.sum(jnp.where(slot_ids[:, None] < slot_ids, named[:, :, None], 0), axis=1)
    listed = jnp.sum(
        jnp.where((named[:, None, :] > 0) & (rank[:, None, :] == slot_ids[:, None]), slot_ids, 0),
        axis=2,
    )

    warped = row_warp(
        columns, row_low, row_num, row_matrices, row_blur, row_turned, row_key, tail, slots,
        cores * regions,
    )
    psf_tile = jnp.zeros((8, LANES), F32).at[:exp_dev, : 2 * RADIUS + 1].set(kernels)
    psf_tile, warped = lax.optimization_barrier((psf_tile, warped))
    rows = exchange(warped, ("core", "region"))
    other = lax.ppermute(psf_tile, "core", [(i, i ^ 1) for i in range(cores)])
    other = other[:exp_dev, : 2 * RADIUS + 1]
    col_blur = make_col_matrices(
        jnp.concatenate(
            [jnp.where(core_at == 0, kernels, other), jnp.where(core_at == 0, other, kernels)]
        )
    )
    partial = col_warp(
        rows, count, listed, col_low, col_num, col_from, col_to, col_blur, col_turned, col_key,
        width, slots, visits, regions, extent * width,
    )
    tile = rows[:, -TAIL, : 3 * exp_dev].astype(F32).reshape(cores, regions, 3, exp_dev)
    tile = jnp.sum(jnp.sum(tile, axis=2), axis=1)
    own = lax.broadcasted_iota(jnp.int32, (8, LANES), 0) // cores == pair_at
    placed = jnp.zeros((8, LANES), F32).at[:, :exp_dev].set(jnp.tile(tile, (8 // cores, 1)))
    tile = ring_sum(jnp.where(own, placed, 0.0), "y")
    weight = 1.0 / (tile[:visits, :exp_dev].reshape(exposures) / (extent * width))
    mean_weight = jnp.mean(weight)
    pieces = exchange(
        partial.reshape((visits * regions,) + partial.shape[2:]), ("y", "core", "region")
    )
    summed = jnp.sum(
        pieces.reshape(visits // cores, patch_rows, own_cols).astype(F32), axis=0, keepdims=True
    )

    total_slots = exposures * slots
    row_cover = coverage(
        row_start.reshape(total_slots, patch_rows),
        lanczos_taps(row_frac.reshape(total_slots, patch_rows)),
        extent,
    )
    at = region_at * own_cols
    col_cover = coverage(
        lax.dynamic_slice_in_dim(col_start, at, own_cols, 2).reshape(total_slots, own_cols),
        lanczos_taps(
            lax.dynamic_slice_in_dim(col_frac, at, own_cols, 2).reshape(total_slots, own_cols)
        ),
        width,
    )
    scale = jnp.where(
        correlations.reshape(total_slots) == visit_at, jnp.repeat(weight, slots), 0.0
    )
    weight_map = lax.dot_general(
        row_cover,
        col_cover * scale[:, None],
        (((0,), (0,)), ((), ())),
        precision=lax.Precision.HIGHEST,
        preferred_element_type=F32,
    ).reshape(1, patch_rows, own_cols)
    coadd = summed / jnp.maximum(weight_map, FLOOR_SHARE * mean_weight)
    return coadd, weight_map


def solution(mesh):
    visits, regions = mesh.devices.shape
    split = jax.sharding.Mesh(
        mesh.devices.reshape(visits // 2, 2, regions), ("y", "core", "region")
    )
    visit = ("y", "core")
    placed = (
        P(visit, "region", None),
        P(visit, "region", None),
        P(visit, None),
        P(),
        P(),
        P(),
        P(),
        P(),
    )
    return jax.shard_map(
        local,
        mesh=split,
        in_specs=placed,
        out_specs=(P(visit, None, "region"), P(visit, None, "region")),
        check_vma=False,
    )
```
